32 devices in a mesh: dp: 8 (over z, y), mp: 4 (over x, core).
Axes of the slice: x: 2, y: 2, z: 4, core: 2. Of those that a mesh axis runs over, the one named last changes fastest.
Arguments:
- chars: int32 [4096, 50], P('dp'), may hold values from 0 to 261
- char_mask: int32 [4096, 50], P('dp'), may hold values from 0 to 1, as said below
- word_order: int32 [4096], replicated, may hold values from 0 to 4095, as said below
- segment_ids: int32 [8, 512], P('dp'), may hold values from 0 to 7, never falling along the last dimension, each value on 1 to 128 neighbouring positions
- char_table: float32 [262, 16], replicated, may hold values from -6 to 6
- conv_weight: bfloat16 [112, 2048], P(None, 'mp'), may hold values from -0.75 to 0.75
- conv_bias: float32 [2048], P('mp'), may hold values from -3 to 3
- highway_weight: bfloat16 [2, 2048, 2, 2048], P(None, None, None, 'mp'), may hold values from -0.125 to 0.125
- highway_bias: float32 [2, 2, 2048], P(None, None, 'mp'), may hold values from -3 to 3
- project_weight: bfloat16 [2048, 768], P('mp'), may hold values from -0.125 to 0.125
- project_bias: float32 [768], replicated, may hold values from -3 to 3
- position_table: float32 [512, 768], replicated, may hold values from -5 to 5
- norm_gain: float32 [3, 768], replicated, may hold values from 0.5 to 1.5
- norm_bias: float32 [3, 768], replicated, may hold values from -2 to 2
- qkv_weight: bfloat16 [768, 3, 768], P(None, None, 'mp'), may hold values from -0.21875 to 0.21875
- qv_bias: float32 [2, 768], P(None, 'mp'), may hold values from -2 to 2
- out_weight: bfloat16 [768, 768], P('mp'), may hold values from -0.875 to 0.875
- out_bias: float32 [768], replicated, may hold values from -2 to 2
- up_weight: bfloat16 [768, 3072], P(None, 'mp'), may hold values from -0.21875 to 0.21875
- up_bias: float32 [3072], P('mp'), may hold values from -2 to 2
- down_weight: bfloat16 [3072, 768], P('mp'), may hold values from -0.109375 to 0.109375
- down_bias: float32 [768], replicated, may hold values from -2 to 2
- out_grad: float32 [4096, 768], P('dp'), may hold values from -6 to 6
Outputs:
- encoded: float32 [4096, 768], P('dp')
- char_table_grad: float32 [262, 16], replicated
- conv_weight_grad: float32 [112, 2048], P(None, 'mp')
- conv_bias_grad: float32 [2048], P('mp')
- highway_weight_grad: float32 [2, 2048, 2, 2048], P(None, 'dp', None, 'mp')
- highway_bias_grad: float32 [2, 2, 2048], P(None, None, 'mp')
- project_weight_grad: float32 [2048, 768], P('mp', 'dp')
- project_bias_grad: float32 [768], replicated
- position_table_grad: float32 [512, 768], replicated
- norm_gain_grad: float32 [3, 768], replicated
- norm_bias_grad: float32 [3, 768], replicated
- qkv_weight_grad: float32 [768, 3, 768], P('dp', None, 'mp')
- qv_bias_grad: float32 [2, 768], P(None, 'mp')
- out_weight_grad: float32 [768, 768], P('mp', 'dp')
- out_bias_grad: float32 [768], replicated
- up_weight_grad: float32 [768, 3072], P('dp', 'mp')
- up_bias_grad: float32 [3072], P('mp')
- down_weight_grad: float32 [3072, 768], P('mp', 'dp')
- down_bias_grad: float32 [768], replicated
The draws below stay inside these ranges and needn't reach their ends.
Inputs may be any that keep to these rules, and one draw needn't show every extreme that they name: `char_mask`: each slot's mask is 1 on its first l characters and 0 after, 1 <= l <= 50; some slot has l = 50. `word_order`: a permutation of the tokens; cut the slots that one index s of dp holds into 8 equal runs in order, numbered d from 0; run d holds exactly the tokens of a share of the rows that index d of dp holds, every token of those rows in some run d of some index s; over the runs d of all indices s, taken in the order of s, words have at least as many characters in later runs.
All inputs are finite; a program needn't handle non-finite values.
Results may differ from the reference program's by a relative error of at most 0.023.
Values may be sent and summed in bfloat16 or wider, within the bound.
No kernel may reach another device: no remote copies, remote signals or barrier semaphores. Data moves between devices by JAX's collectives and lax.ppermute only.
A program may use at most 192 MiB of HBM per device.

```python
import math
import jax
import jax.numpy as jnp
import numpy as np
from jax import lax

D = 768
HEADS = 12
HEAD = 64
FF = 3072
CHANNELS = 2048
CHAR_DIM = 16
VOCAB = 262
CHARS = 50
TAPS = 7
LAYERS = 2
ROW = 512
TOK_DEV = 512
TOKENS = 4096
SEQS = 8


def draw_char_mask(key, part):
    key = jax.random.fold_in(key, 11)
    groups = TOKENS // TOK_DEV
    per_peer = TOK_DEV // groups
    lengths = jax.random.randint(key, (groups, TOK_DEV), 1, CHARS + 1)
    lengths = jnp.sort(lengths, axis=1)
    lengths = lengths.at[:, TOK_DEV - 1].set(CHARS)
    lengths = lengths.reshape(groups, groups, per_peer).transpose(1, 0, 2).reshape(TOKENS)
    return (jnp.arange(CHARS)[None, :] < lengths[:, None]).astype(jnp.int32)


def draw_word_order(key, part):
    key = jax.random.fold_in(key, 23)
    groups = TOKENS // TOK_DEV
    per_peer = TOK_DEV // groups
    keys_all = jax.random.split(key, groups)
    local_order = jax.vmap(lambda one_key: jax.random.permutation(one_key, TOK_DEV))(keys_all)
    tokens_all = local_order + (jnp.arange(groups) * TOK_DEV)[:, None]
    return tokens_all.reshape(groups, groups, per_peer).transpose(1, 0, 2).reshape(TOKENS).astype(jnp.int32)


def set_ends(drawn, own_key, smallest, top_value):
    longest = drawn.shape.index(max(drawn.shape))
    spots = []
    for shift in (0, 1):
        where = [jax.random.randint(jax.random.fold_in(own_key, axis), (), 0, length) for axis, length in enumerate(drawn.shape)]
        where[longest] = (where[longest] + shift) % drawn.shape[longest]
        spots.append(tuple(where))
    return drawn.at[spots[0]].set(smallest).at[spots[1]].set(top_value)


def levels(stream_key, shape, pieces, smallest, largest):
    level, own = 1.0, jax.random.fold_in(stream_key, 6)
    for position, parts in pieces:
        heights = jnp.exp(jax.random.uniform(jax.random.fold_in(own, position), (parts,), jnp.float32, smallest / len(pieces), largest / len(pieces)))
        level = level * jnp.repeat(heights, shape[position] // parts).reshape([-1 if axis == position else 1 for axis in range(len(shape))])
    return level


def length_profile(number_of, total, limit, skew):
    weights = [(1 << 20) // math.isqrt(grade ** skew) + 1 for grade in range(2, number_of + 1)]
    rest, counts = total - limit - (number_of - 1), [1] * (number_of - 1)
    while rest > 0:
        candidates = [i for i in range(number_of - 1) if counts[i] < limit]
        whole, left = sum([weights[i] for i in candidates]), rest
        for i in candidates:
            more = min(limit - counts[i], max(1, left * weights[i] // whole), rest)
            counts[i] = counts[i] + more
            rest = rest - more
    return np.array([limit] + counts)


def uneven(key, count, total, most, lean):
    if count == 2:
        one = jax.random.randint(key, (), max(1, total - most), min(most, total - 1) + 1)
        return jnp.stack([one, total - one])
    tallies = jnp.asarray(length_profile(count, total, most, lean), jnp.int32)
    couples = (count - 1) // 2
    giver, receiver = tallies[1:1 + 2 * couples:2], tallies[2:2 + 2 * couples:2]
    margin = jnp.minimum(giver - 1, most - receiver)
    shifted = jax.random.randint(jax.random.fold_in(key, 1), (couples,), 0, 1 << 20) % (margin + 1)
    tallies = tallies.at[1:1 + 2 * couples:2].set(giver - shifted).at[2:2 + 2 * couples:2].set(receiver + shifted)
    return tallies[jax.random.permutation(jax.random.fold_in(key, 2), count)]


def scatter_about(key, extent, scale, bound, cuts=(), kind=jnp.bfloat16):
    level = levels(key, extent, cuts, -0.22, 0.18) if cuts else 1.0
    array = jax.random.normal(key, extent, jnp.float32) * scale * level
    return jnp.minimum(jnp.maximum(array, -bound), bound).astype(kind)


def setup_inputs(seed: int = 0) -> dict:
    arg_keys = jax.random.split(jax.random.key(seed), 24)
    chars = set_ends(jax.random.randint(arg_keys[0], (TOKENS, CHARS), 0, VOCAB), jax.random.fold_in(arg_keys[0], 1), 0, VOCAB - 1).astype(jnp.int32)
    char_mask = draw_char_mask(jax.random.fold_in(arg_keys[23], 71), 0)
    word_order = draw_word_order(jax.random.fold_in(arg_keys[23], 71), 0)
    segment_ids = jax.vmap(lambda own: jnp.searchsorted(jnp.cumsum(uneven(own, 8, ROW, ROW // 4, 0)), jnp.arange(ROW), side="right"))(jax.random.split(arg_keys[3], SEQS)).reshape((SEQS, ROW)).astype(jnp.int32)
    char_table = scatter_about(arg_keys[4], (VOCAB, CHAR_DIM), 1.0, 6.0, (), jnp.float32)
    conv_weight = scatter_about(arg_keys[5], (TAPS * CHAR_DIM, CHANNELS), (TAPS * CHAR_DIM // 2) ** -0.5, 0.75, ((1, 4),))
    conv_bias = scatter_about(arg_keys[6], (CHANNELS,), 0.5, 3.0, ((0, 4),), jnp.float32)
    highway_weight = scatter_about(arg_keys[7], (LAYERS, CHANNELS, 2, CHANNELS), CHANNELS ** -0.5, 0.125, ((3, 4),))
    highway_bias = scatter_about(arg_keys[8], (LAYERS, 2, CHANNELS), 0.5, 3.0, ((2, 4),), jnp.float32)
    project_weight = scatter_about(arg_keys[9], (CHANNELS, D), CHANNELS ** -0.5, 0.125, ((0, 4),))
    project_bias = scatter_about(arg_keys[10], (D,), 0.5, 3.0, (), jnp.float32)
    position_table = scatter_about(arg_keys[11], (ROW, D), 1.0, 5.0, (), jnp.float32)
    norm_gain = jnp.clip(1.0 + 0.1 * jax.random.normal(arg_keys[12], (3, D), jnp.float32), 0.5, 1.5)
    norm_bias = scatter_about(arg_keys[13], (3, D), 0.3, 2.0, (), jnp.float32)
    qkv_weight = scatter_about(arg_keys[14], (D, 3, HEADS * HEAD), D ** -0.5, 0.21875, ((2, 4),))
    qv_bias = scatter_about(arg_keys[15], (2, HEADS * HEAD), 0.3, 2.0, ((1, 4),), jnp.float32)
    out_weight = scatter_about(arg_keys[16], (HEADS * HEAD, D), (HEADS * HEAD // 16) ** -0.5, 0.875, ((0, 4),))
    out_bias = scatter_about(arg_keys[17], (D,), 0.3, 2.0, (), jnp.float32)
    up_weight = scatter_about(arg_keys[18], (D, FF), D ** -0.5, 0.21875, ((1, 4),))
    up_bias = scatter_about(arg_keys[19], (FF,), 0.3, 2.0, ((0, 4),), jnp.float32)
    down_weight = scatter_about(arg_keys[20], (FF, D), FF ** -0.5, 0.109375, ((0, 4),))
    down_bias = scatter_about(arg_keys[21], (D,), 0.3, 2.0, (), jnp.float32)
    out_grad = scatter_about(arg_keys[22], (TOKENS, D), 1.0, 6.0, ((0, 8),), jnp.float32)
    return dict(chars=chars, char_mask=char_mask, word_order=word_order, segment_ids=segment_ids, char_table=char_table, conv_weight=conv_weight, conv_bias=conv_bias, highway_weight=highway_weight, highway_bias=highway_bias, project_weight=project_weight, project_bias=project_bias, position_table=position_table, norm_gain=norm_gain, norm_bias=norm_bias, qkv_weight=qkv_weight, qv_bias=qv_bias, out_weight=out_weight, out_bias=out_bias, up_weight=up_weight, up_bias=up_bias, down_weight=down_weight, down_bias=down_bias, out_grad=out_grad)


HIGH = lax.Precision.HIGHEST
EPSILON = 1e-05
NEGATIVE = -1e+30

@jax.custom_vjp
def low(v):
    return lax.optimization_barrier(v.astype(jnp.bfloat16)).astype(jnp.float32)

@jax.custom_vjp
def low_back(v):
    return v

def low_keep(v):
    return (low(v), None)

def low_pass(kept, grad):
    return (grad,)

def back_keep(v):
    return (v, None)

def back_low(kept, grad):
    return (low(grad),)
low.defvjp(low_keep, low_pass)
low_back.defvjp(back_keep, back_low)

def filter_mask():
    channel = jnp.arange(CHANNELS, dtype=jnp.int32)
    tap_count = 1 + sum(((channel >= CHANNELS // divisor).astype(jnp.int32) for divisor in (64, 32, 16, 8, 4, 2)))
    tap_index = jnp.arange(TAPS * CHAR_DIM, dtype=jnp.int32) // CHAR_DIM
    return (tap_index[:, None] < tap_count[None, :]).astype(jnp.float32)

def char_windows(embedded):
    padded = jnp.pad(embedded, ((0, 0), (0, TAPS - 1), (0, 0)))
    return jnp.concatenate([padded[:, offset:offset + CHARS, :] for offset in range(TAPS)], axis=2)

def layer_norm(values, gain_row, bias_row):
    center = values - lax.optimization_barrier(jnp.mean(values, axis=-1, keepdims=True))
    spread = lax.optimization_barrier(jnp.mean(center * center, axis=-1, keepdims=True))
    return center * lax.rsqrt(spread + EPSILON) * gain_row + bias_row

def embed_words(ids_block, mask_block, char_table, conv_w, conv_b, hw_w, hw_b, proj_w, proj_b):
    embedded = char_table[ids_block] * mask_block[..., None].astype(jnp.float32)
    windows = char_windows(low(embedded))
    filters = conv_w * filter_mask()
    conv_out = low_back(jnp.einsum('npk,kc->npc', windows, filters, precision=HIGH) + conv_b)
    pooled = lax.optimization_barrier(jnp.mean(jax.nn.silu(conv_out), axis=1))
    carried = low(low_back(pooled))
    for depth_index in range(LAYERS):
        inputs = carried if depth_index == 0 else low(carried)
        both_parts = low_back(jnp.einsum('nk,kjc->njc', inputs, hw_w[depth_index], precision=HIGH) + hw_b[depth_index])
        opened = jax.nn.sigmoid(both_parts[:, 1])
        carried = opened * jax.nn.silu(both_parts[:, 0]) + (1.0 - opened) * carried
    return low_back(jnp.dot(low(carried), proj_w, precision=HIGH) + proj_b)

def encode_rows(hidden_in, segment_row, qkv_w, qv_b, out_w, out_b, up_w, up_b, down_w, down_b, gains, shifts):
    x_low = low(hidden_in)
    qkv_out = jnp.einsum('nd,djh->njh', x_low, qkv_w, precision=HIGH)
    query = low(low_back(qkv_out[:, 0] + qv_b[0])).reshape(ROW, HEADS, HEAD)
    keys_all = low(low_back(qkv_out[:, 1])).reshape(ROW, HEADS, HEAD)
    values_all = low(low_back(qkv_out[:, 2] + qv_b[1])).reshape(ROW, HEADS, HEAD)
    scores = low_back(jnp.einsum('qhe,khe->hqk', query, keys_all, precision=HIGH) * HEAD ** (-0.5))
    same_doc = segment_row[:, None] == segment_row[None, :]
    scores = jnp.where(same_doc[None], scores, NEGATIVE)
    probs = jax.nn.softmax(scores, axis=-1)
    mixed = jnp.einsum('hqk,khe->qhe', low(probs), values_all, precision=HIGH).reshape(ROW, HEADS * HEAD)
    mixed = low(low_back(mixed))
    attended = low_back(jnp.dot(mixed, out_w, precision=HIGH) + out_b)
    hidden_mid = layer_norm(hidden_in + attended, gains[1], shifts[1])
    upward = low_back(jnp.dot(low(hidden_mid), up_w, precision=HIGH) + up_b)
    downward = low_back(jnp.dot(low(jax.nn.gelu(upward)), down_w, precision=HIGH) + down_b)
    return layer_norm(hidden_mid + downward, gains[2], shifts[2])

def reference(chars, char_mask, word_order, segment_ids, char_table, conv_weight, conv_bias, highway_weight, highway_bias, project_weight, project_bias, position_table, norm_gain, norm_bias, qkv_weight, qv_bias, out_weight, out_bias, up_weight, up_bias, down_weight, down_bias, out_grad):
    floats = tuple((item.astype(jnp.float32) for item in (char_table, conv_weight, conv_bias, highway_weight, highway_bias, project_weight, project_bias, position_table, norm_gain, norm_bias, qkv_weight, qv_bias, out_weight, out_bias, up_weight, up_bias, down_weight, down_bias)))
    words_block = 512 if TOKENS % 512 == 0 else TOKENS
    inverse = jnp.zeros((TOKENS,), jnp.int32).at[word_order].set(jnp.arange(TOKENS, dtype=jnp.int32))

    def forward(table_w, conv_w, conv_b, hw_w, hw_b, proj_w, proj_b, pos_table, gains, shifts, qkv_w, qv_b, out_w, out_b, up_w, up_b, down_w, down_b):

        def embed_one(block_pair):
            return embed_words(block_pair[0], block_pair[1], table_w, conv_w, conv_b, hw_w, hw_b, proj_w, proj_b)
        slots = lax.map(jax.checkpoint(embed_one), (chars.reshape(-1, words_block, CHARS), char_mask.reshape(-1, words_block, CHARS)))
        token_rows = slots.reshape(TOKENS, D)[inverse].reshape(SEQS, ROW, D)

        def encode_one(block_pair):
            hidden_in = layer_norm(block_pair[0] + pos_table, gains[0], shifts[0])
            return encode_rows(hidden_in, block_pair[1], qkv_w, qv_b, out_w, out_b, up_w, up_b, down_w, down_b, gains, shifts)
        return lax.map(jax.checkpoint(encode_one), (token_rows, segment_ids)).reshape(TOKENS, D)
    encoded, undo = jax.vjp(forward, *floats)
    grads = undo(out_grad.astype(jnp.float32))
    return (encoded, grads[0], grads[1], grads[2], grads[3], grads[4], grads[5], grads[6], grads[7], grads[8], grads[9], grads[10], grads[11], grads[12], grads[13], grads[14], grads[15], grads[16], grads[17])
```

```python
import jax
import jax.numpy as jnp
from jax import lax
from jax.sharding import PartitionSpec as P

HEAD = 64
CHANNELS = 2048
CHAR_DIM = 16
CHARS = 50
TAPS = 7
LAYERS = 2

HIGH = lax.Precision.HIGHEST
EPSILON = 1e-05
NEGATIVE = -1e30
F32 = jnp.float32
BF16 = jnp.bfloat16


def filter_mask(local_count, first):
    channel = first + jnp.arange(local_count, dtype=jnp.int32)
    tap_count = 1 + sum(
        ((channel >= CHANNELS // divisor).astype(jnp.int32) for divisor in (64, 32, 16, 8, 4, 2))
    )
    tap_index = jnp.arange(TAPS * CHAR_DIM, dtype=jnp.int32) // CHAR_DIM
    return tap_index[:, None] < tap_count[None, :]


def char_windows(embedded):
    padded = jnp.pad(embedded, ((0, 0), (0, TAPS - 1), (0, 0)))
    return jnp.concatenate(
        [padded[:, offset : offset + CHARS, :] for offset in range(TAPS)], axis=2
    )


def layer_norm(values, gain_row, bias_row):
    center = values - jnp.mean(values, axis=-1, keepdims=True)
    spread = jnp.mean(center * center, axis=-1, keepdims=True)
    return center * lax.rsqrt(spread + EPSILON) * gain_row + bias_row


def embed_rows(ids_block, char_table, filters, conv_bias):
    embedded = (
        jnp.take(char_table, jnp.maximum(ids_block, 0), axis=0)
        * (ids_block >= 0)[..., None].astype(F32)
    ).astype(BF16)
    windows = char_windows(embedded)
    conv_out = jnp.einsum("npk,kc->npc", windows, filters, preferred_element_type=F32) + conv_bias
    return (windows, conv_out)


def pool_conv(conv_out):
    return jnp.mean(jax.nn.silu(conv_out), axis=1)


def cnn_forward(ids_all, char_table, filters, conv_bias):
    def one_block(ids_block):
        return pool_conv(embed_rows(ids_block, char_table, filters, conv_bias)[1])

    pooled = lax.map(one_block, ids_all.reshape(-1, 128, CHARS))
    return pooled.reshape(ids_all.shape[0], -1)


def cnn_backward(ids_all, pooled_grad, char_table, filters, conv_bias):
    block_words = 128
    vocab_ids = jnp.arange(char_table.shape[0], dtype=jnp.int32)

    def one_block(totals, pieces):
        ids_block, grad_block = pieces
        windows, conv_out = embed_rows(ids_block, char_table, filters, conv_bias)
        _, undo = jax.vjp(pool_conv, conv_out)
        conv_grad = undo(grad_block)[0].astype(BF16)
        weight_sum = totals[0] + jnp.einsum(
            "npk,npc->kc", windows, conv_grad, preferred_element_type=F32
        )
        bias_sum = totals[1] + jnp.sum(conv_grad.astype(F32), axis=(0, 1))
        window_grad = jnp.einsum("npc,kc->npk", conv_grad, filters, preferred_element_type=F32)
        window_grad = window_grad.reshape(block_words, CHARS, TAPS, CHAR_DIM)
        padded = jnp.pad(window_grad, ((0, 0), (TAPS - 1, 0), (0, 0), (0, 0)))
        embed_grad = sum(
            (
                padded[:, TAPS - 1 - offset : TAPS - 1 - offset + CHARS, offset, :]
                for offset in range(TAPS)
            )
        )
        onehot = (ids_block.reshape(-1)[:, None] == vocab_ids[None, :]).astype(F32)
        table_sum = totals[2] + jnp.einsum(
            "mv,me->ve", onehot, embed_grad.reshape(-1, CHAR_DIM), precision=HIGH
        )
        return ((weight_sum, bias_sum, table_sum), None)

    local_count = filters.shape[1]
    start_totals = (
        jnp.zeros(filters.shape, F32),
        jnp.zeros((local_count,), F32),
        jnp.zeros(char_table.shape, F32),
    )
    pieces = (
        ids_all.reshape(-1, block_words, CHARS),
        pooled_grad.reshape(-1, block_words, local_count),
    )
    totals, _ = lax.scan(one_block, start_totals, pieces)
    return totals


def highway_mix(both_parts, carried):
    opened = jax.nn.sigmoid(both_parts[:, 1])
    return opened * jax.nn.silu(both_parts[:, 0]) + (1.0 - opened) * carried


def column_sum(values):
    return jnp.sum(values.astype(F32), axis=0)


def swap(values, axis, bit):
    count = lax.axis_size(axis)
    return lax.ppermute(values, axis, [(i, i ^ bit) for i in range(count)])


def bit_reversed(count):
    bits = count.bit_length() - 1
    return [sum(((i >> b) & 1) << (bits - 1 - b) for b in range(bits)) for i in range(count)]


def blocks_by_peer(values, axis, order, count):
    size = values.shape[axis] // count
    me = lax.axis_index("dp")
    return [lax.dynamic_slice_in_dim(values, (me ^ r) * size, size, axis) for r in order]


def halve(blocks, bits, final=F32):
    for bit in bits:
        half = blocks.shape[0] // 2
        got = swap(blocks[half:], "dp", bit)
        blocks = blocks[:half].astype(F32) + got.astype(F32)
        if half > 1:
            blocks = blocks.astype(BF16)
    return blocks[0]


def on_device(
    chars,
    char_mask,
    word_order,
    segment_ids,
    char_table,
    conv_weight,
    conv_bias,
    highway_weight,
    highway_bias,
    project_weight,
    project_bias,
    position_table,
    norm_gain,
    norm_bias,
    qkv_weight,
    qv_bias,
    out_weight,
    out_bias,
    up_weight,
    up_bias,
    down_weight,
    down_bias,
    out_grad,
):
    dp_count = lax.axis_size("dp")
    dp_index = lax.axis_index("dp")
    mp_index = lax.axis_index("mp")
    low = mp_index & 1
    word_count = chars.shape[0]
    per_peer = word_count // dp_count
    half_count = word_count // 2
    local_channels = conv_weight.shape[1]
    dp_bits = [1 << b for b in range(dp_count.bit_length() - 1)]
    order = bit_reversed(dp_count)

    local_rows = (
        lax.dynamic_slice(
            word_order.reshape(dp_count, dp_count, per_peer),
            (0, dp_index, 0),
            (dp_count, 1, per_peer),
        ).reshape(word_count)
        - dp_index * word_count
    )
    places = local_rows ^ (low * half_count)
    perm = (jnp.arange(word_count, dtype=jnp.int32)[:, None] == places[None, :]).astype(BF16)

    def own_half(values):
        return lax.dynamic_slice_in_dim(values, low * half_count, half_count, 0)

    ids = jnp.where(char_mask > 0, chars, -1).reshape(dp_count, per_peer * CHARS)
    ids = lax.all_to_all(ids, "dp", split_axis=0, concat_axis=0, tiled=True)
    ids = ids.reshape(word_count, CHARS)

    used_taps = filter_mask(local_channels, mp_index * local_channels)
    filters = jnp.where(used_taps, conv_weight, jnp.zeros_like(conv_weight))
    pooled = cnn_forward(ids, char_table, filters, conv_bias).astype(BF16)

    def weight_part(depth, r):
        rows = lax.dynamic_slice_in_dim(
            highway_weight[depth], (mp_index ^ r) * local_channels, local_channels, 0
        )
        return rows.reshape(local_channels, -1)

    carried = pooled.astype(F32)
    inputs = pooled
    kept = []
    for depth in range(LAYERS):
        a = inputs
        b = swap(a, "mp", 1)
        c = swap(a, "mp", 2)
        d = swap(c, "mp", 1)
        both = sum(
            jnp.dot(piece, weight_part(depth, r), preferred_element_type=F32)
            for r, piece in enumerate((a, b, c, d))
        )
        both = both.reshape(word_count, 2, local_channels) + highway_bias[depth]
        whole = jnp.zeros((word_count, CHANNELS), BF16)
        for r, piece in enumerate((a, b, c, d)):
            whole = lax.dynamic_update_slice(
                whole, piece, (0, (mp_index ^ r) * local_channels)
            )
        blocks = blocks_by_peer(whole, 1, order, dp_count)
        ours = jnp.concatenate(blocks[: dp_count // 2], axis=1)
        theirs = swap(jnp.concatenate(blocks[dp_count // 2 :], axis=1), "dp", 1)
        kept.append((carried, both, ours, theirs))
        carried = highway_mix(both, carried)
        inputs = carried.astype(BF16)

    def sum_halves(rows, matrix, transposed=False):
        def product(part):
            if transposed:
                return jnp.einsum("nf,df->nd", part, matrix, preferred_element_type=F32)
            return jnp.dot(part, matrix, preferred_element_type=F32)

        got = swap(product(rows[half_count:]), "mp", 1)
        pair = (product(rows[:half_count]) + got).astype(BF16)
        return pair.astype(F32) + swap(pair, "mp", 2).astype(F32)

    def both_halves(values):
        return jnp.concatenate([values, swap(values, "mp", 1)], axis=0)

    state = jnp.dot(perm, inputs, preferred_element_type=F32).astype(BF16)
    embed_total = sum_halves(state, project_weight) + project_bias + own_half(position_table)
    hidden_in = layer_norm(embed_total, norm_gain[0], norm_bias[0])
    x_low = both_halves(hidden_in.astype(BF16))
    qkv_out = jnp.einsum("nd,djh->njh", x_low, qkv_weight, preferred_element_type=F32)
    heads = qkv_weight.shape[2] // HEAD
    head_shape = (word_count, heads, HEAD)
    query = (qkv_out[:, 0] + qv_bias[0]).astype(BF16).reshape(head_shape)
    keys = qkv_out[:, 1].astype(BF16).reshape(head_shape)
    values = (qkv_out[:, 2] + qv_bias[1]).astype(BF16).reshape(head_shape)
    segments = segment_ids[0]
    segments = jnp.where(low > 0, jnp.roll(segments, half_count), segments)
    same_doc = segments[:, None] == segments[None, :]
    scale = HEAD ** (-0.5)
    scores = jnp.einsum("qhe,khe->hqk", query, keys, preferred_element_type=F32) * scale
    scores = jnp.where(same_doc[None], scores, NEGATIVE)
    exps = jnp.exp(scores - jnp.max(scores, axis=-1, keepdims=True))
    probs = exps / jnp.sum(exps, axis=-1, keepdims=True)
    probs_low = probs.astype(BF16)
    mixed = jnp.einsum("hqk,khe->qhe", probs_low, values, preferred_element_type=F32)
    mixed = mixed.astype(BF16).reshape(word_count, -1)
    resid_one = hidden_in + sum_halves(mixed, out_weight) + out_bias
    hidden_mid = layer_norm(resid_one, norm_gain[1], norm_bias[1])
    mid_low = both_halves(hidden_mid.astype(BF16))
    upward = jnp.dot(mid_low, up_weight, preferred_element_type=F32) + up_bias
    activated = jax.nn.gelu(upward).astype(BF16)
    resid_two = hidden_mid + sum_halves(activated, down_weight) + down_bias
    encoded = layer_norm(resid_two, norm_gain[2], norm_bias[2])

    _, undo = jax.vjp(layer_norm, resid_two, norm_gain[2], norm_bias[2])
    resid_two_grad, gain_two, shift_two = undo(own_half(out_grad))
    down_low = resid_two_grad.astype(BF16)
    down_bias_grad = column_sum(down_low)
    down_grad = both_halves(down_low)
    act_grad = jnp.einsum("nd,fd->nf", down_grad, down_weight, preferred_element_type=F32)
    _, undo = jax.vjp(jax.nn.gelu, upward)
    up_grad = undo(act_grad)[0].astype(BF16)
    mid_grad = resid_two_grad + sum_halves(up_grad, up_weight, True)
    up_bias_grad = column_sum(up_grad)
    down_weight_grad = jnp.einsum("nd,nf->df", down_grad, activated, preferred_element_type=F32)
    up_weight_grad = jnp.einsum("nd,nf->df", mid_low, up_grad, preferred_element_type=F32)
    _, undo = jax.vjp(layer_norm, resid_one, norm_gain[1], norm_bias[1])
    resid_one_grad, gain_one, shift_one = undo(mid_grad)
    attn_low = resid_one_grad.astype(BF16)
    out_bias_grad = column_sum(attn_low)
    attn_grad = both_halves(attn_low)
    mixed_grad = jnp.einsum("nd,hd->nh", attn_grad, out_weight, preferred_element_type=F32)
    mixed_grad = mixed_grad.astype(BF16).reshape(head_shape)
    out_weight_grad = jnp.einsum("nd,nh->dh", attn_grad, mixed, preferred_element_type=F32)
    prob_grad = jnp.einsum("qhe,khe->hqk", mixed_grad, values, preferred_element_type=F32)
    score_grad = (
        probs * (prob_grad - jnp.sum(probs * prob_grad, axis=-1, keepdims=True))
    ).astype(BF16)
    query_grad = jnp.einsum("hqk,khe->qhe", score_grad, keys, preferred_element_type=F32) * scale
    key_grad = jnp.einsum("hqk,qhe->khe", score_grad, query, preferred_element_type=F32) * scale
    value_grad = jnp.einsum("hqk,qhe->khe", probs_low, mixed_grad, preferred_element_type=F32)
    qkv_grad = jnp.concatenate(
        [g.astype(BF16).reshape(word_count, -1) for g in (query_grad, key_grad, value_grad)],
        axis=1,
    )
    qkv_flat = qkv_weight.reshape(qkv_weight.shape[0], -1)
    hidden_grad = resid_one_grad + sum_halves(qkv_grad, qkv_flat, True)
    local_heads = qkv_weight.shape[2]
    qkv_sums = column_sum(qkv_grad)
    qv_bias_grad = jnp.stack([qkv_sums[:local_heads], qkv_sums[2 * local_heads :]], axis=0)
    qkv_weight_grad = jnp.einsum("nd,nh->dh", x_low, qkv_grad, preferred_element_type=F32)
    _, undo = jax.vjp(layer_norm, embed_total, norm_gain[0], norm_bias[0])
    embed_grad, gain_zero, shift_zero = undo(hidden_grad)
    proj_low = embed_grad.astype(BF16)
    project_bias_grad = column_sum(proj_low)
    proj_grad = both_halves(proj_low)
    proj_words = jnp.einsum("tw,td->wd", perm, proj_grad, preferred_element_type=F32).astype(BF16)
    state_grad = jnp.einsum("nd,cd->nc", proj_words, project_weight, preferred_element_type=F32)
    project_weight_grad = jnp.einsum(
        "nd,nc->dc", proj_words, inputs, preferred_element_type=F32
    )
    encoder_grads = jnp.concatenate(
        [qkv_weight_grad, out_weight_grad, up_weight_grad, down_weight_grad, project_weight_grad],
        axis=1,
    )
    encoder_blocks = jnp.stack(blocks_by_peer(encoder_grads, 0, order, dp_count), axis=0)
    encoder_sum = halve(encoder_blocks.astype(BF16), dp_bits)

    level_sums = [None] * LAYERS
    level_bias_grads = [None] * LAYERS
    for depth in reversed(range(LAYERS)):
        carried_now, both_now, ours, theirs = kept[depth]
        _, undo = jax.vjp(highway_mix, both_now, carried_now)
        both_grad, carried_grad = undo(state_grad)
        both_low = both_grad.astype(BF16).reshape(word_count, -1)
        level_bias_grads[depth] = column_sum(both_low).reshape(2, local_channels)
        parts = [
            jnp.einsum(
                "nf,kf->nk", both_low, weight_part(depth, r), preferred_element_type=F32
            )
            for r in (3, 2, 1, 0)
        ]
        far = (parts[1] + swap(parts[0].astype(BF16), "mp", 1).astype(F32)).astype(BF16)
        near = parts[3] + swap(parts[2].astype(BF16), "mp", 1).astype(F32)
        state_grad = near + swap(far, "mp", 2).astype(F32) + carried_grad
        peer_grad = swap(both_low, "dp", 1)
        weight_grad = jnp.einsum("nk,nf->kf", ours, both_low, preferred_element_type=F32)
        weight_grad += jnp.einsum("nk,nf->kf", theirs, peer_grad, preferred_element_type=F32)
        weight_grad = weight_grad.astype(BF16).reshape(
            dp_count // 2, CHANNELS // dp_count, 2 * local_channels
        )
        level_sums[depth] = halve(weight_grad, dp_bits[1:]).reshape(-1, 2, local_channels)
    highway_weight_grad = jnp.stack(level_sums, axis=0)
    highway_bias_grad = jnp.stack(level_bias_grads, axis=0)
    pooled_grad = state_grad.astype(BF16).astype(F32)

    conv_sum, conv_bias_sum, table_sum = cnn_backward(
        ids, pooled_grad, char_table, filters, conv_bias
    )
    conv_weight_sum = jnp.where(used_taps, conv_sum, jnp.zeros_like(conv_sum))

    def over_dp(values):
        for bit in dp_bits:
            values = values + swap(values, "dp", bit)
        return values

    def pack(items):
        return jnp.concatenate([item.reshape(-1) for item in items]).reshape(-1, 128)

    def unpack(packed, items):
        flat = packed.reshape(-1)
        result, first = [], 0
        for item in items:
            result.append(flat[first : first + item.size].reshape(item.shape))
            first += item.size
        return result

    row_items = [
        project_bias_grad,
        jnp.stack([gain_zero, gain_one, gain_two], axis=0),
        jnp.stack([shift_zero, shift_one, shift_two], axis=0),
        out_bias_grad,
        down_bias_grad,
    ]
    row_pack = pack(row_items)
    row_pack = row_pack + swap(row_pack, "mp", 1)
    shard_items = [highway_bias_grad, qv_bias_grad, up_bias_grad]
    small = over_dp(jnp.concatenate([row_pack, pack(shard_items)], axis=0))
    row_sums = unpack(small[: row_pack.shape[0]], row_items)
    shard_sums = unpack(small[row_pack.shape[0] :], shard_items)

    position_half = over_dp(embed_grad)
    position_grad = both_halves(position_half)

    conv_items = [conv_weight_sum, conv_bias_sum]
    conv_pack = pack(conv_items)
    conv_sums = unpack(over_dp(conv_pack), conv_items)
    table_total = table_sum
    table_total = table_total + swap(table_total, "mp", 1)
    table_total = table_total + swap(table_total, "mp", 2)
    table_total = over_dp(table_total)

    def in_order(values):
        first, second = values[:half_count], values[half_count:]
        return jnp.concatenate(
            [jnp.where(low > 0, second, first), jnp.where(low > 0, first, second)], axis=0
        )

    bounds, first = [], 0
    for width in (3 * local_heads, local_heads, up_weight.shape[1], down_weight.shape[0], local_channels):
        bounds.append(encoder_sum[:, first : first + width])
        first += width
    return (
        in_order(both_halves(encoded)),
        table_total,
        conv_sums[0],
        conv_sums[1],
        highway_weight_grad,
        shard_sums[0],
        bounds[4].T,
        row_sums[0],
        in_order(position_grad),
        row_sums[1],
        row_sums[2],
        bounds[0].reshape(-1, 3, local_heads),
        shard_sums[1],
        bounds[1].T,
        row_sums[3],
        bounds[2],
        shard_sums[2],
        bounds[3].T,
        row_sums[4],
    )


def solution(mesh):
    return jax.shard_map(
        on_device,
        mesh=mesh,
        in_specs=(
            P("dp", None),
            P("dp", None),
            P(),
            P("dp", None),
            P(),
            P(None, "mp"),
            P("mp"),
            P(None, None, None, "mp"),
            P(None, None, "mp"),
            P("mp", None),
            P(),
            P(),
            P(),
            P(),
            P(None, None, "mp"),
            P(None, "mp"),
            P("mp", None),
            P(),
            P(None, "mp"),
            P("mp"),
            P("mp", None),
            P(),
            P("dp", None),
        ),
        out_specs=(
            P("dp", None),
            P(),
            P(None, "mp"),
            P("mp"),
            P(None, "dp", None, "mp"),
            P(None, None, "mp"),
            P("mp", "dp"),
            P(),
            P(),
            P(),
            P(),
            P("dp", None, "mp"),
            P(None, "mp"),
            P("mp", "dp"),
            P(),
            P("dp", "mp"),
            P("mp"),
            P("mp", "dp"),
            P(),
        ),
        check_vma=False,
    )
```

```python
import functools

import jax
import jax.numpy as jnp
from jax import lax
from jax.experimental import pallas as pl
from jax.experimental.pallas import tpu as pltpu
from jax.sharding import PartitionSpec as P

HEAD = 64
CHANNELS = 2048
CHAR_DIM = 16
CHARS = 50
TAPS = 7
LAYERS = 2
BLOCK = 128

EPSILON = 1e-05
NEGATIVE = -1e30
F32 = jnp.float32
BF16 = jnp.bfloat16


def filter_mask(local_count, first):
    channel = first + jnp.arange(local_count, dtype=jnp.int32)
    tap_count = 1 + sum(
        ((channel >= CHANNELS // divisor).astype(jnp.int32) for divisor in (64, 32, 16, 8, 4, 2))
    )
    tap_index = jnp.arange(TAPS * CHAR_DIM, dtype=jnp.int32) // CHAR_DIM
    return tap_index[:, None] < tap_count[None, :]


def layer_norm(values, gain_row, bias_row):
    center = values - jnp.mean(values, axis=-1, keepdims=True)
    spread = jnp.mean(center * center, axis=-1, keepdims=True)
    return center * lax.rsqrt(spread + EPSILON) * gain_row + bias_row


STEPS = 8
ROWS = 7
SPAN = STEPS * CHAR_DIM
VMEM_LIMIT = 60 << 20

def spread_table(char_table):
    low = char_table.astype(BF16)
    eye = jnp.eye(STEPS, dtype=BF16)
    first = low[:256]
    rest = jnp.pad(low[256:], ((0, CHAR_DIM - (low.shape[0] - 256)), (0, 0)))
    parts = [(eye[:, None, :, None] * part[None, :, None, :]).reshape(-1, SPAN) for part in (first, rest)]
    return jnp.concatenate(parts, axis=0)

def place_filters(filters_ref, shifted):
    shifted[...] = jnp.zeros_like(shifted)
    taps = filters_ref.shape[0]
    width = filters_ref.shape[1]
    halved = (filters_ref[...].astype(F32) * 0.5).astype(BF16)
    for r in range(STEPS):
        shifted[CHAR_DIM * r : CHAR_DIM * r + taps, r * width : (r + 1) * width] = halved

def forward_kernel(block, counts, ids_ref, table_ref, filters_ref, bias_ref, pooled_ref, embed_ref, shifted, hot, total):
    words, width = pooled_ref.shape
    place_filters(filters_ref, shifted)
    lanes = lax.broadcasted_iota(jnp.int32, (words, 256), 1)
    lane = lax.broadcasted_iota(jnp.int32, (words, 128), 1)
    embed_ref[ROWS] = jnp.zeros_like(embed_ref[ROWS])
    total[...] = jnp.zeros_like(total)
    for q in range(ROWS):
        left = jnp.zeros((words, 128), F32)
        for r in range(STEPS):
            j = q * STEPS + r
            if j < CHARS:
                ids = ids_ref[:, j : j + 1]
                hot[:, r * 256 : (r + 1) * 256] = jnp.where(ids == lanes, 1.0, 0.0).astype(BF16)
                mark = jnp.where(lane // CHAR_DIM == r, lane % CHAR_DIM + 256, -7)
                left = jnp.where(ids == mark, 1.0, left)
            else:
                hot[:, r * 256 : (r + 1) * 256] = jnp.zeros((words, 256), BF16)
        hot[:, STEPS * 256 :] = left.astype(BF16)
        embed_ref[q] = jnp.dot(hot[...], table_ref[...], preferred_element_type=F32).astype(BF16)
    half = bias_ref[...] * 0.5
    blocks = words // block
    for q in range(ROWS):
        def one(i, carry):
            rows = pl.ds(pl.multiple_of(i * block, block), block)
            x = jnp.concatenate([embed_ref[q, rows, :], embed_ref[q + 1, rows, :]], axis=1)
            for r in range(STEPS):
                u = jnp.dot(x, shifted[:, r * width : (r + 1) * width], preferred_element_type=F32) + half
                total[rows, :] += u + u * jnp.tanh(u)
            return carry
        lax.fori_loop(counts[blocks + q], blocks, one, 0)
    rest = half + half * jnp.tanh(half)
    for i in range(blocks):
        rows = slice(i * block, (i + 1) * block)
        seen = STEPS * counts[i]
        pooled_ref[rows, :] = ((total[rows, :] + (CHARS - seen).astype(F32) * rest) * (1.0 / CHARS)).astype(BF16)

def block_counts(ids, block):
    most = jnp.max(jnp.sum((ids >= 0).astype(jnp.int32), axis=1).reshape(-1, block), axis=1)
    need = lax.cummax((most + STEPS - 1) // STEPS)
    first = jnp.sum((need[None, :] <= jnp.arange(ROWS, dtype=jnp.int32)[:, None]).astype(jnp.int32), axis=1)
    return jnp.concatenate([need, first])

def cnn_forward(ids, counts, table, filters, bias, block):
    words = ids.shape[0]
    width = filters.shape[1]
    vm = pl.BlockSpec(memory_space=pltpu.VMEM)
    return pl.pallas_call(
        functools.partial(forward_kernel, block),
        in_specs=[pl.BlockSpec(memory_space=pltpu.SMEM), vm, vm, vm, vm],
        out_specs=[vm, vm],
        out_shape=[jax.ShapeDtypeStruct((words, width), BF16), jax.ShapeDtypeStruct((ROWS + 1, words, SPAN), BF16)],
        scratch_shapes=[pltpu.VMEM((2 * SPAN, STEPS * width), BF16), pltpu.VMEM((words, STEPS * 256 + 128), BF16), pltpu.VMEM((words, width), F32)],
        compiler_params=pltpu.CompilerParams(vmem_limit_bytes=VMEM_LIMIT),
    )(counts, ids, table, filters, bias.reshape(1, -1))


def backward_kernel(block, vocab, counts, ids_ref, embed_ref, filters_ref, bias_ref, grad_ref,
                    filter_out, bias_out, table_out, shifted, slopes, sums, embed_grad, hot):
    words, width = grad_ref.shape
    blocks = words // block
    place_filters(filters_ref, shifted)
    half = bias_ref[...] * 0.5
    still = jnp.tanh(half)
    rest = (1.0 + still) + half * (1.0 - still * still)
    bias_out[...] = jnp.zeros_like(bias_out)
    sums[...] = jnp.zeros_like(sums)
    embed_grad[...] = jnp.zeros_like(embed_grad)
    scale = 0.5 / CHARS
    for i in range(blocks):
        grads = grad_ref[i * block : (i + 1) * block, :].astype(F32) * scale
        left = (CHARS - STEPS * counts[i]).astype(F32)
        bias_out[...] += jnp.sum(grads, axis=0, keepdims=True) * (rest * left)
    for q in range(ROWS):
        first = counts[blocks + q]
        if q:
            def clear(i, carry):
                rows = pl.ds(pl.multiple_of(i * block, block), block)
                slopes[rows, :] = jnp.zeros((block, STEPS * width), BF16)
                return carry
            lax.fori_loop(counts[blocks + q - 1], first, clear, 0)

        def one(i, carry):
            rows = pl.ds(pl.multiple_of(i * block, block), block)
            x = jnp.concatenate([embed_ref[q, rows, :], embed_ref[q + 1, rows, :]], axis=1)
            grads = grad_ref[rows, :].astype(F32) * scale
            column = jnp.zeros((1, width), F32)
            for r in range(STEPS):
                u = jnp.dot(x, shifted[:, r * width : (r + 1) * width], preferred_element_type=F32) + half
                t = jnp.tanh(u)
                slope = grads * ((1.0 + t) + u * (1.0 - t * t))
                column += jnp.sum(slope, axis=0, keepdims=True)
                slopes[rows, r * width : (r + 1) * width] = slope.astype(BF16)
            bias_out[...] += column
            return carry
        lax.fori_loop(first, blocks, one, 0)

        def spread(start):
            rows = slice(start, words)
            x = jnp.concatenate([embed_ref[q, rows, :], embed_ref[q + 1, rows, :]], axis=1)
            back = lax.dot_general(slopes[rows, :], shifted[...], (((1,), (1,)), ((), ())), preferred_element_type=F32)
            embed_grad[q, rows, :] += back[:, :SPAN]
            embed_grad[q + 1, rows, :] += back[:, SPAN:]
            for r in range(STEPS):
                cols = slice(r * width, (r + 1) * width)
                sums[:, cols] += lax.dot_general(x, slopes[rows, cols], (((0,), (0,)), ((), ())), preferred_element_type=F32)

        middle = blocks // 2
        if q < 1:
            spread(0)
        else:
            @pl.when(first < middle)
            def _():
                spread(0)

            @pl.when((first >= middle) & (first < blocks))
            def _():
                spread(middle * block)
    taps = filters_ref.shape[0]
    total = sums[:taps, :width]
    for r in range(1, STEPS):
        total = total + sums[CHAR_DIM * r : CHAR_DIM * r + taps, r * width : (r + 1) * width]
    filter_out[...] = total
    high = embed_grad[:ROWS].reshape(ROWS * words, SPAN) * 2.0
    low = high.astype(BF16)
    pair = jnp.concatenate([low, (high - low.astype(F32)).astype(BF16)], axis=1)
    which = lax.broadcasted_iota(jnp.int32, (vocab, words), 0)
    lane = lax.broadcasted_iota(jnp.int32, (vocab, SPAN), 1) // CHAR_DIM
    table = jnp.zeros((vocab, SPAN), F32)
    for r in range(STEPS):
        for q in range(ROWS):
            j = q * STEPS + r
            cols = slice(q * words, (q + 1) * words)
            if j < CHARS:
                hot[:, cols] = jnp.where(ids_ref[j : j + 1, :] == which, 1.0, 0.0).astype(BF16)
            else:
                hot[:, cols] = jnp.zeros((vocab, words), BF16)
        both = jnp.dot(hot[...], pair, preferred_element_type=F32)
        table = jnp.where(lane == r, both[:, :SPAN] + both[:, SPAN:], table)
    table_out[...] = table

def cnn_backward(ids_columns, counts, embed, filters, bias, grad, block, vocab):
    words = ids_columns.shape[1]
    taps, width = filters.shape
    rows = -(-vocab // 16) * 16
    vm = pl.BlockSpec(memory_space=pltpu.VMEM)
    conv, bias_sum, table = pl.pallas_call(
        functools.partial(backward_kernel, block, rows),
        in_specs=[pl.BlockSpec(memory_space=pltpu.SMEM), vm, vm, vm, vm, vm],
        out_specs=[vm, vm, vm],
        out_shape=[jax.ShapeDtypeStruct((taps, width), F32), jax.ShapeDtypeStruct((1, width), F32), jax.ShapeDtypeStruct((rows, SPAN), F32)],
        scratch_shapes=[pltpu.VMEM((2 * SPAN, STEPS * width), BF16), pltpu.VMEM((words, STEPS * width), BF16),
                        pltpu.VMEM((2 * SPAN, STEPS * width), F32), pltpu.VMEM((ROWS + 1, words, SPAN), F32),
                        pltpu.VMEM((rows, ROWS * words), BF16)],
        compiler_params=pltpu.CompilerParams(vmem_limit_bytes=VMEM_LIMIT),
    )(counts, ids_columns, embed, filters, bias.reshape(1, -1), grad)
    return conv, bias_sum[0], jnp.sum(table[:vocab].reshape(vocab, STEPS, CHAR_DIM), axis=1)


def highway_mix(transform, gate, carried):
    opened = jax.nn.sigmoid(gate)
    return opened * jax.nn.silu(transform) + (1.0 - opened) * carried


def column_sum(values):
    return jnp.sum(values.astype(F32), axis=0)


def swap(values, axis, bit):
    count = lax.axis_size(axis)
    return lax.ppermute(values, axis, [(i, i ^ bit) for i in range(count)])


def bit_reversed(count):
    bits = count.bit_length() - 1
    return [sum(((i >> b) & 1) << (bits - 1 - b) for b in range(bits)) for i in range(count)]


def blocks_by_peer(values, axis, order, count):
    size = values.shape[axis] // count
    me = lax.axis_index("dp")
    return [lax.dynamic_slice_in_dim(values, (me ^ r) * size, size, axis) for r in order]


def halve(blocks, bits, final=F32):
    for bit in bits:
        half = blocks.shape[0] // 2
        got = swap(blocks[half:], "dp", bit)
        blocks = blocks[:half].astype(F32) + got.astype(F32)
        if half > 1:
            blocks = blocks.astype(BF16)
    return blocks[0]


def on_device(
    chars,
    char_mask,
    word_order,
    segment_ids,
    char_table,
    conv_weight,
    conv_bias,
    highway_weight,
    highway_bias,
    project_weight,
    project_bias,
    position_table,
    norm_gain,
    norm_bias,
    qkv_weight,
    qv_bias,
    out_weight,
    out_bias,
    up_weight,
    up_bias,
    down_weight,
    down_bias,
    out_grad,
):
    dp_count = lax.axis_size("dp")
    dp_index = lax.axis_index("dp")
    mp_index = lax.axis_index("mp")
    low = mp_index & 1
    word_count = chars.shape[0]
    per_peer = word_count // dp_count
    half_count = word_count // 2
    local_channels = conv_weight.shape[1]
    dp_bits = [1 << b for b in range(dp_count.bit_length() - 1)]
    order = bit_reversed(dp_count)

    local_rows = (
        lax.dynamic_slice(
            word_order.reshape(dp_count, dp_count, per_peer),
            (0, dp_index, 0),
            (dp_count, 1, per_peer),
        ).reshape(word_count)
        - dp_index * word_count
    )
    places = local_rows ^ (low * half_count)
    perm = (jnp.arange(word_count, dtype=jnp.int32)[:, None] == places[None, :]).astype(BF16)

    def own_half(values):
        return lax.dynamic_slice_in_dim(values, low * half_count, half_count, 0)

    ids = jnp.where(char_mask > 0, chars, -1).reshape(dp_count, per_peer * CHARS)
    ids = lax.all_to_all(ids, "dp", split_axis=0, concat_axis=0, tiled=True)
    ids = ids.reshape(word_count, CHARS)

    used_taps = filter_mask(local_channels, mp_index * local_channels)
    filters = jnp.where(used_taps, conv_weight, jnp.zeros_like(conv_weight))
    counts = block_counts(ids, BLOCK)
    pooled, embedded = cnn_forward(
        ids, counts, spread_table(char_table), filters, conv_bias, BLOCK
    )
    levels = lax.optimization_barrier(jnp.swapaxes(highway_weight, 1, 2))

    def weight_part(depth, r):
        rows = lax.dynamic_slice_in_dim(
            levels[depth], (mp_index ^ r) * local_channels, local_channels, 1
        )
        return rows[0], rows[1]

    carried = pooled.astype(F32)
    inputs = pooled
    kept = []
    for depth in range(LAYERS):
        a = inputs
        b = swap(a, "mp", 1)
        c = swap(a, "mp", 2)
        d = swap(c, "mp", 1)
        both = [
            sum(
                jnp.dot(piece, weight_part(depth, r)[j], preferred_element_type=F32)
                for r, piece in enumerate((a, b, c, d))
            )
            + highway_bias[depth, j]
            for j in range(2)
        ]
        whole = jnp.zeros((word_count, CHANNELS), BF16)
        for r, piece in enumerate((a, b, c, d)):
            whole = lax.dynamic_update_slice(
                whole, piece, (0, (mp_index ^ r) * local_channels)
            )
        blocks = blocks_by_peer(whole, 1, order, dp_count)
        ours = jnp.concatenate(blocks[: dp_count // 2], axis=1)
        theirs = swap(jnp.concatenate(blocks[dp_count // 2 :], axis=1), "dp", 1)
        kept.append((carried, both, ours, theirs))
        carried = highway_mix(*both, carried)
        inputs = carried.astype(BF16)

    def sum_halves(rows, matrix, transposed=False):
        def product(part):
            if transposed:
                return jnp.einsum("nf,df->nd", part, matrix, preferred_element_type=F32)
            return jnp.dot(part, matrix, preferred_element_type=F32)

        got = swap(product(rows[half_count:]), "mp", 1)
        pair = (product(rows[:half_count]) + got).astype(BF16)
        return pair.astype(F32) + swap(pair, "mp", 2).astype(F32)

    def both_halves(values):
        return jnp.concatenate([values, swap(values, "mp", 1)], axis=0)

    state = jnp.dot(perm, inputs, preferred_element_type=F32).astype(BF16)
    embed_total = sum_halves(state, project_weight) + project_bias + own_half(position_table)
    hidden_in = layer_norm(embed_total, norm_gain[0], norm_bias[0])
    x_low = both_halves(hidden_in.astype(BF16))
    qkv_out = jnp.einsum("nd,djh->njh", x_low, qkv_weight, preferred_element_type=F32)
    heads = qkv_weight.shape[2] // HEAD
    head_shape = (word_count, heads, HEAD)
    query = (qkv_out[:, 0] + qv_bias[0]).astype(BF16).reshape(head_shape)
    keys = qkv_out[:, 1].astype(BF16).reshape(head_shape)
    values = (qkv_out[:, 2] + qv_bias[1]).astype(BF16).reshape(head_shape)
    segments = segment_ids[0]
    segments = jnp.where(low > 0, jnp.roll(segments, half_count), segments)
    same_doc = segments[:, None] == segments[None, :]
    scale = HEAD ** (-0.5)
    scores = jnp.einsum("qhe,khe->hqk", query, keys, preferred_element_type=F32) * scale
    scores = jnp.where(same_doc[None], scores, NEGATIVE)
    exps = jnp.exp(scores - jnp.max(scores, axis=-1, keepdims=True))
    probs = exps / jnp.sum(exps, axis=-1, keepdims=True)
    probs_low = probs.astype(BF16)
    mixed = jnp.einsum("hqk,khe->qhe", probs_low, values, preferred_element_type=F32)
    mixed = mixed.astype(BF16).reshape(word_count, -1)
    resid_one = hidden_in + sum_halves(mixed, out_weight) + out_bias
    hidden_mid = layer_norm(resid_one, norm_gain[1], norm_bias[1])
    mid_low = both_halves(hidden_mid.astype(BF16))
    upward = jnp.dot(mid_low, up_weight, preferred_element_type=F32) + up_bias
    activated = jax.nn.gelu(upward).astype(BF16)
    resid_two = hidden_mid + sum_halves(activated, down_weight) + down_bias
    encoded = layer_norm(resid_two, norm_gain[2], norm_bias[2])

    _, undo = jax.vjp(layer_norm, resid_two, norm_gain[2], norm_bias[2])
    resid_two_grad, gain_two, shift_two = undo(own_half(out_grad))
    down_low = resid_two_grad.astype(BF16)
    down_bias_grad = column_sum(down_low)
    down_grad = both_halves(down_low)
    act_grad = jnp.einsum("nd,fd->nf", down_grad, down_weight, preferred_element_type=F32)
    _, undo = jax.vjp(jax.nn.gelu, upward)
    up_grad = undo(act_grad)[0].astype(BF16)
    mid_grad = resid_two_grad + sum_halves(up_grad, up_weight, True)
    up_bias_grad = column_sum(up_grad)
    down_weight_grad = jnp.einsum("nd,nf->df", down_grad, activated, preferred_element_type=F32)
    up_weight_grad = jnp.einsum("nd,nf->df", mid_low, up_grad, preferred_element_type=F32)
    _, undo = jax.vjp(layer_norm, resid_one, norm_gain[1], norm_bias[1])
    resid_one_grad, gain_one, shift_one = undo(mid_grad)
    attn_low = resid_one_grad.astype(BF16)
    out_bias_grad = column_sum(attn_low)
    attn_grad = both_halves(attn_low)
    mixed_grad = jnp.einsum("nd,hd->nh", attn_grad, out_weight, preferred_element_type=F32)
    mixed_grad = mixed_grad.astype(BF16).reshape(head_shape)
    out_weight_grad = jnp.einsum("nd,nh->dh", attn_grad, mixed, preferred_element_type=F32)
    prob_grad = jnp.einsum("qhe,khe->hqk", mixed_grad, values, preferred_element_type=F32)
    score_grad = (
        probs * (prob_grad - jnp.sum(probs * prob_grad, axis=-1, keepdims=True))
    ).astype(BF16)
    query_grad = jnp.einsum("hqk,khe->qhe", score_grad, keys, preferred_element_type=F32) * scale
    key_grad = jnp.einsum("hqk,qhe->khe", score_grad, query, preferred_element_type=F32) * scale
    value_grad = jnp.einsum("hqk,qhe->khe", probs_low, mixed_grad, preferred_element_type=F32)
    qkv_grad = jnp.concatenate(
        [g.astype(BF16).reshape(word_count, -1) for g in (query_grad, key_grad, value_grad)],
        axis=1,
    )
    qkv_flat = qkv_weight.reshape(qkv_weight.shape[0], -1)
    hidden_grad = resid_one_grad + sum_halves(qkv_grad, qkv_flat, True)
    local_heads = qkv_weight.shape[2]
    qkv_sums = column_sum(qkv_grad)
    qv_bias_grad = jnp.stack([qkv_sums[:local_heads], qkv_sums[2 * local_heads :]], axis=0)
    qkv_weight_grad = jnp.einsum("nd,nh->dh", x_low, qkv_grad, preferred_element_type=F32)
    _, undo = jax.vjp(layer_norm, embed_total, norm_gain[0], norm_bias[0])
    embed_grad, gain_zero, shift_zero = undo(hidden_grad)
    proj_low = embed_grad.astype(BF16)
    project_bias_grad = column_sum(proj_low)
    proj_grad = both_halves(proj_low)
    proj_words = jnp.einsum("tw,td->wd", perm, proj_grad, preferred_element_type=F32).astype(BF16)
    state_grad = jnp.einsum("nd,cd->nc", proj_words, project_weight, preferred_element_type=F32)
    project_weight_grad = jnp.einsum(
        "nd,nc->dc", proj_words, inputs, preferred_element_type=F32
    )
    encoder_grads = jnp.concatenate(
        [qkv_weight_grad, out_weight_grad, up_weight_grad, down_weight_grad, project_weight_grad],
        axis=1,
    )
    encoder_blocks = jnp.stack(blocks_by_peer(encoder_grads, 0, order, dp_count), axis=0)
    encoder_sum = halve(encoder_blocks.astype(BF16), dp_bits)

    level_sums = [None] * LAYERS
    level_bias_grads = [None] * LAYERS
    for depth in reversed(range(LAYERS)):
        carried_now, both_now, ours, theirs = kept[depth]
        _, undo = jax.vjp(highway_mix, *both_now, carried_now)
        *both_grad, carried_grad = undo(state_grad)
        both_low = jnp.concatenate([g.astype(BF16) for g in both_grad], axis=1)
        level_bias_grads[depth] = column_sum(both_low).reshape(2, local_channels)
        parts = [
            sum(
                jnp.einsum(
                    "nf,kf->nk",
                    both_low[:, j * local_channels : (j + 1) * local_channels],
                    weight_part(depth, r)[j],
                    preferred_element_type=F32,
                )
                for j in range(2)
            )
            for r in (3, 2, 1, 0)
        ]
        far = (parts[1] + swap(parts[0].astype(BF16), "mp", 1).astype(F32)).astype(BF16)
        near = parts[3] + swap(parts[2].astype(BF16), "mp", 1).astype(F32)
        state_grad = near + swap(far, "mp", 2).astype(F32) + carried_grad
        peer_grad = swap(both_low, "dp", 1)
        weight_grad = jnp.einsum("nk,nf->kf", ours, both_low, preferred_element_type=F32)
        weight_grad += jnp.einsum("nk,nf->kf", theirs, peer_grad, preferred_element_type=F32)
        weight_grad = weight_grad.astype(BF16).reshape(
            dp_count // 2, CHANNELS // dp_count, 2 * local_channels
        )
        level_sums[depth] = halve(weight_grad, dp_bits[1:]).reshape(-1, 2, local_channels)
    highway_weight_grad = jnp.stack(level_sums, axis=0)
    highway_bias_grad = jnp.stack(level_bias_grads, axis=0)
    conv_sum, conv_bias_sum, table_sum = cnn_backward(
        ids.T,
        counts,
        embedded,
        filters,
        conv_bias,
        state_grad.astype(BF16),
        BLOCK,
        char_table.shape[0],
    )
    conv_weight_sum = jnp.where(used_taps, conv_sum, jnp.zeros_like(conv_sum))

    def over_dp(values):
        for bit in dp_bits:
            values = values + swap(values, "dp", bit)
        return values

    def pack(items):
        return jnp.concatenate([item.reshape(-1) for item in items]).reshape(-1, 128)

    def unpack(packed, items):
        flat = packed.reshape(-1)
        result, first = [], 0
        for item in items:
            result.append(flat[first : first + item.size].reshape(item.shape))
            first += item.size
        return result

    row_items = [
        project_bias_grad,
        jnp.stack([gain_zero, gain_one, gain_two], axis=0),
        jnp.stack([shift_zero, shift_one, shift_two], axis=0),
        out_bias_grad,
        down_bias_grad,
    ]
    row_pack = pack(row_items)
    row_pack = row_pack + swap(row_pack, "mp", 1)
    shard_items = [highway_bias_grad, qv_bias_grad, up_bias_grad]
    small = over_dp(jnp.concatenate([row_pack, pack(shard_items)], axis=0))
    row_sums = unpack(small[: row_pack.shape[0]], row_items)
    shard_sums = unpack(small[row_pack.shape[0] :], shard_items)

    position_half = over_dp(embed_grad)
    position_grad = both_halves(position_half)

    conv_items = [conv_weight_sum, conv_bias_sum]
    conv_pack = pack(conv_items)
    conv_sums = unpack(over_dp(conv_pack), conv_items)
    table_total = table_sum
    table_total = table_total + swap(table_total, "mp", 1)
    table_total = table_total + swap(table_total, "mp", 2)
    table_total = over_dp(table_total)

    def in_order(values):
        first, second = values[:half_count], values[half_count:]
        return jnp.concatenate(
            [jnp.where(low > 0, second, first), jnp.where(low > 0, first, second)], axis=0
        )

    bounds, first = [], 0
    for width in (3 * local_heads, local_heads, up_weight.shape[1], down_weight.shape[0], local_channels):
        bounds.append(encoder_sum[:, first : first + width])
        first += width
    return (
        in_order(both_halves(encoded)),
        table_total,
        conv_sums[0],
        conv_sums[1],
        highway_weight_grad,
        shard_sums[0],
        bounds[4].T,
        row_sums[0],
        in_order(position_grad),
        row_sums[1],
        row_sums[2],
        bounds[0].reshape(-1, 3, local_heads),
        shard_sums[1],
        bounds[1].T,
        row_sums[3],
        bounds[2],
        shard_sums[2],
        bounds[3].T,
        row_sums[4],
    )


def solution(mesh):
    return jax.shard_map(
        on_device,
        mesh=mesh,
        in_specs=(
            P("dp", None),
            P("dp", None),
            P(),
            P("dp", None),
            P(),
            P(None, "mp"),
            P("mp"),
            P(None, None, None, "mp"),
            P(None, None, "mp"),
            P("mp", None),
            P(),
            P(),
            P(),
            P(),
            P(None, None, "mp"),
            P(None, "mp"),
            P("mp", None),
            P(),
            P(None, "mp"),
            P("mp"),
            P("mp", None),
            P(),
            P("dp", None),
        ),
        out_specs=(
            P("dp", None),
            P(),
            P(None, "mp"),
            P("mp"),
            P(None, "dp", None, "mp"),
            P(None, None, "mp"),
            P("mp", "dp"),
            P(),
            P(),
            P(),
            P(),
            P("dp", None, "mp"),
            P(None, "mp"),
            P("mp", "dp"),
            P(),
            P("dp", "mp"),
            P("mp"),
            P("mp", "dp"),
            P(),
        ),
        check_vma=False,
    )
```

```python
import functools

import jax
import jax.numpy as jnp
from jax import lax
from jax.experimental import pallas as pl
from jax.experimental.pallas import tpu as pltpu
from jax.sharding import PartitionSpec as P

HEAD = 64
CHANNELS = 2048
CHAR_DIM = 16
CHARS = 50
TAPS = 7
LAYERS = 2
BLOCK = 128
TILES = 4

EPSILON = 1e-05
NEGATIVE = -1e30
F32 = jnp.float32
BF16 = jnp.bfloat16


def filter_mask(local_count, first):
    channel = first + jnp.arange(local_count, dtype=jnp.int32)
    tap_count = 1 + sum(
        ((channel >= CHANNELS // divisor).astype(jnp.int32) for divisor in (64, 32, 16, 8, 4, 2))
    )
    tap_index = jnp.arange(TAPS * CHAR_DIM, dtype=jnp.int32) // CHAR_DIM
    return tap_index[:, None] < tap_count[None, :]


STEPS = 8
ROWS = 7
SPAN = STEPS * CHAR_DIM
VMEM_LIMIT = 24 << 20
FREE = pl.CostEstimate(flops=1, bytes_accessed=1, transcendentals=0)

def spread_table(char_table):
    low = char_table.astype(BF16)
    eye = jnp.eye(STEPS, dtype=BF16)
    first = low[:256]
    rest = jnp.pad(low[256:], ((0, CHAR_DIM - (low.shape[0] - 256)), (0, 0)))
    parts = [(eye[:, None, :, None] * part[None, :, None, :]).reshape(-1, SPAN) for part in (first, rest)]
    return jnp.concatenate(parts, axis=0)

def place_filters(filters_ref, shifted):
    shifted[...] = jnp.zeros_like(shifted)
    taps = filters_ref.shape[0]
    width = filters_ref.shape[1]
    halved = (filters_ref[...].astype(F32) * 0.5).astype(BF16)
    for r in range(STEPS):
        shifted[CHAR_DIM * r : CHAR_DIM * r + taps, r * width : (r + 1) * width] = halved

def forward_kernel(block, counts, ids_ref, table_ref, filters_ref, bias_ref, pooled_ref, embed_ref, shifted, hot, total):
    words, width = pooled_ref.shape
    place_filters(filters_ref, shifted)
    lanes = lax.broadcasted_iota(jnp.int32, (words, 256), 1)
    lane = lax.broadcasted_iota(jnp.int32, (words, 128), 1)
    embed_ref[ROWS] = jnp.zeros_like(embed_ref[ROWS])
    total[...] = jnp.zeros_like(total)
    for q in range(ROWS):
        left = jnp.zeros((words, 128), F32)
        for r in range(STEPS):
            j = q * STEPS + r
            if j < CHARS:
                ids = ids_ref[:, j : j + 1]
                hot[:, r * 256 : (r + 1) * 256] = jnp.where(ids == lanes, 1.0, 0.0).astype(BF16)
                mark = jnp.where(lane // CHAR_DIM == r, lane % CHAR_DIM + 256, -7)
                left = jnp.where(ids == mark, 1.0, left)
            else:
                hot[:, r * 256 : (r + 1) * 256] = jnp.zeros((words, 256), BF16)
        hot[:, STEPS * 256 :] = left.astype(BF16)
        embed_ref[q] = jnp.dot(hot[...], table_ref[...], preferred_element_type=F32).astype(BF16)
    half = bias_ref[...] * 0.5
    blocks = words // block
    for q in range(ROWS):
        def one(i, carry):
            rows = pl.ds(pl.multiple_of(i * block, block), block)
            x = jnp.concatenate([embed_ref[q, rows, :], embed_ref[q + 1, rows, :]], axis=1)
            for r in range(STEPS):
                u = jnp.dot(x, shifted[:, r * width : (r + 1) * width], preferred_element_type=F32) + half
                total[rows, :] += u + u * jnp.tanh(u)
            return carry
        lax.fori_loop(counts[blocks + q], blocks, one, 0)
    rest = half + half * jnp.tanh(half)
    for i in range(blocks):
        rows = slice(i * block, (i + 1) * block)
        seen = STEPS * counts[i]
        pooled_ref[rows, :] = ((total[rows, :] + (CHARS - seen).astype(F32) * rest) * (1.0 / CHARS)).astype(BF16)

def block_counts(ids, block):
    most = jnp.max(jnp.sum((ids >= 0).astype(jnp.int32), axis=1).reshape(-1, block), axis=1)
    need = (most + STEPS - 1) // STEPS
    first = jnp.sum((need[None, :] <= jnp.arange(ROWS, dtype=jnp.int32)[:, None]).astype(jnp.int32), axis=1)
    return jnp.concatenate([need, first])

def cnn_forward(ids, counts, table, filters, bias, block):
    words = ids.shape[0]
    width = filters.shape[1]
    vm = pl.BlockSpec(memory_space=pltpu.VMEM)
    return pl.pallas_call(
        functools.partial(forward_kernel, block),
        in_specs=[pl.BlockSpec(memory_space=pltpu.SMEM), vm, vm, vm, vm],
        out_specs=[vm, vm],
        out_shape=[jax.ShapeDtypeStruct((words, width), BF16), jax.ShapeDtypeStruct((ROWS + 1, words, SPAN), BF16)],
        scratch_shapes=[pltpu.VMEM((2 * SPAN, STEPS * width), BF16), pltpu.VMEM((words, STEPS * 256 + 128), BF16), pltpu.VMEM((words, width), F32)],
        compiler_params=pltpu.CompilerParams(vmem_limit_bytes=VMEM_LIMIT),
        cost_estimate=FREE,
    )(counts, ids, table, filters, bias.reshape(1, -1))


def backward_kernel(
    block,
    counts,
    embed_ref,
    filters_ref,
    bias_ref,
    grad_ref,
    embed_in,
    filter_out,
    bias_out,
    embed_grad,
    shifted,
    slopes,
    sums,
):
    words, width = grad_ref.shape
    blocks = words // block
    place_filters(filters_ref, shifted)
    half = bias_ref[...] * 0.5
    still = jnp.tanh(half)
    rest = (1.0 + still) + half * (1.0 - still * still)
    bias_out[...] = jnp.zeros_like(bias_out)
    sums[...] = jnp.zeros_like(sums)
    if embed_in is None:
        embed_grad[...] = jnp.zeros_like(embed_grad)
    else:
        embed_grad[...] = embed_in[...]
    scale = 0.5 / CHARS
    for i in range(blocks):
        grads = grad_ref[i * block : (i + 1) * block, :].astype(F32) * scale
        left = (CHARS - STEPS * counts[i]).astype(F32)
        bias_out[...] += jnp.sum(grads, axis=0, keepdims=True) * (rest * left)
    for q in range(ROWS):
        first = counts[blocks + q]
        if q:

            def clear(i, carry):
                rows = pl.ds(pl.multiple_of(i * block, block), block)
                slopes[rows, :] = jnp.zeros((block, STEPS * width), BF16)
                return carry

            lax.fori_loop(counts[blocks + q - 1], first, clear, 0)

        def one(i, carry):
            rows = pl.ds(pl.multiple_of(i * block, block), block)
            x = jnp.concatenate([embed_ref[q, rows, :], embed_ref[q + 1, rows, :]], axis=1)
            grads = grad_ref[rows, :].astype(F32) * scale
            column = jnp.zeros((1, width), F32)
            for r in range(STEPS):
                cols = slice(r * width, (r + 1) * width)
                u = jnp.dot(x, shifted[:, cols], preferred_element_type=F32) + half
                t = jnp.tanh(u)
                slope = grads * ((1.0 + t) + u * (1.0 - t * t))
                column += jnp.sum(slope, axis=0, keepdims=True)
                slopes[rows, cols] = slope.astype(BF16)
            bias_out[...] += column
            return carry

        lax.fori_loop(first, blocks, one, 0)

        def spread(start):
            rows = slice(start, words)
            x = jnp.concatenate([embed_ref[q, rows, :], embed_ref[q + 1, rows, :]], axis=1)
            back = lax.dot_general(
                slopes[rows, :], shifted[...], (((1,), (1,)), ((), ())), preferred_element_type=F32
            )
            embed_grad[q, rows, :] += back[:, :SPAN]
            embed_grad[q + 1, rows, :] += back[:, SPAN:]
            for r in range(STEPS):
                cols = slice(r * width, (r + 1) * width)
                sums[:, cols] += lax.dot_general(
                    x, slopes[rows, cols], (((0,), (0,)), ((), ())), preferred_element_type=F32
                )

        middle = blocks // 2
        if q < 1:
            spread(0)
        else:

            @pl.when(first < middle)
            def _():
                spread(0)

            @pl.when((first >= middle) & (first < blocks))
            def _():
                spread(middle * block)

    taps = filters_ref.shape[0]
    total = sums[:taps, :width]
    for r in range(1, STEPS):
        lower = CHAR_DIM * r
        total = total + sums[lower : lower + taps, r * width : (r + 1) * width]
    filter_out[...] = total


def cnn_backward(counts, embed, filters, bias, grad, embed_grad, block):
    words, width = grad.shape
    taps = filters.shape[0]
    vm = pl.BlockSpec(memory_space=pltpu.VMEM)
    operands = [counts, embed, filters, bias.reshape(1, -1), grad]
    kernel = functools.partial(backward_kernel, block)
    if embed_grad is None:
        inner = kernel

        def kernel(counts, embed, filters, bias, grad, *rest):
            inner(counts, embed, filters, bias, grad, None, *rest)
    else:
        operands.append(embed_grad)
    return pl.pallas_call(
        kernel,
        in_specs=[pl.BlockSpec(memory_space=pltpu.SMEM)] + [vm] * (len(operands) - 1),
        out_specs=[vm] * 3,
        out_shape=[
            jax.ShapeDtypeStruct((taps, width), F32),
            jax.ShapeDtypeStruct((1, width), F32),
            jax.ShapeDtypeStruct((ROWS + 1, words, SPAN), F32),
        ],
        scratch_shapes=[
            pltpu.VMEM((2 * SPAN, STEPS * width), BF16),
            pltpu.VMEM((words, STEPS * width), BF16),
            pltpu.VMEM((2 * SPAN, STEPS * width), F32),
        ],
        compiler_params=pltpu.CompilerParams(vmem_limit_bytes=VMEM_LIMIT),
        cost_estimate=FREE,
    )(*operands)


def table_kernel(ids_ref, embed_grad, table_out, hot):
    vocab, words = table_out.shape[0], ids_ref.shape[1]
    high = embed_grad[:ROWS].reshape(ROWS * words, SPAN) * 2.0
    low = high.astype(BF16)
    pair = jnp.concatenate([low, (high - low.astype(F32)).astype(BF16)], axis=1)
    which = lax.broadcasted_iota(jnp.int32, (vocab, words), 0)
    lane = lax.broadcasted_iota(jnp.int32, (vocab, SPAN), 1) // CHAR_DIM
    table = jnp.zeros((vocab, SPAN), F32)
    for r in range(STEPS):
        for q in range(ROWS):
            j = q * STEPS + r
            cols = slice(q * words, (q + 1) * words)
            if j < CHARS:
                hot[:, cols] = jnp.where(ids_ref[j : j + 1, :] == which, 1.0, 0.0).astype(BF16)
            else:
                hot[:, cols] = jnp.zeros((vocab, words), BF16)
        both = jnp.dot(hot[...], pair, preferred_element_type=F32)
        table = jnp.where(lane == r, both[:, :SPAN] + both[:, SPAN:], table)
    table_out[...] = table


def table_gradient(ids_columns, embed_grad, vocab):
    words = ids_columns.shape[1]
    rows = -(-vocab // 16) * 16
    vm = pl.BlockSpec(memory_space=pltpu.VMEM)
    table = pl.pallas_call(
        table_kernel,
        in_specs=[vm, vm],
        out_specs=vm,
        out_shape=jax.ShapeDtypeStruct((rows, SPAN), F32),
        scratch_shapes=[pltpu.VMEM((rows, ROWS * words), BF16)],
        compiler_params=pltpu.CompilerParams(vmem_limit_bytes=VMEM_LIMIT),
        cost_estimate=FREE,
    )(ids_columns, embed_grad)
    return jnp.sum(table[:vocab].reshape(vocab, STEPS, CHAR_DIM), axis=1)


def level_call(kernel, places, level, picks, weights, arrays, shapes, hidden=False):
    width = weights.shape[3]
    rows = arrays[0].shape[0]
    tile = rows // TILES
    weights = pltpu.with_memory_space_constraint(weights, pltpu.HBM)

    def picked(pick):
        return pl.BlockSpec((1, 2, width, width), lambda i, spots: (level, 0, spots[pick], 0))

    def tiled(shape):
        if shape[0] == rows:
            return pl.BlockSpec((tile, shape[1]), lambda i, spots: (i, 0))
        return pl.BlockSpec(shape, lambda i, spots: (0, 0))

    cost = FREE
    if hidden:
        cost = pl.CostEstimate(
            flops=8 * rows * width * width, bytes_accessed=16 * rows * width, transcendentals=0
        )
    return pl.pallas_call(
        kernel,
        grid_spec=pltpu.PrefetchScalarGridSpec(
            num_scalar_prefetch=1,
            grid=(TILES,),
            in_specs=[picked(pick) for pick in picks] + [tiled(item.shape) for item in arrays],
            out_specs=[tiled(item.shape) for item in shapes],
        ),
        out_shape=shapes,
        compiler_params=pltpu.CompilerParams(vmem_limit_bytes=VMEM_LIMIT),
        cost_estimate=cost,
    )(places, *[weights] * len(picks), *arrays)


def level_near_kernel(places, own_w, near_w, own, near, transform_out, gate_out):
    for j, out in enumerate((transform_out, gate_out)):
        out[...] = jnp.dot(own[...], own_w[0, j], preferred_element_type=F32) + jnp.dot(
            near[...], near_w[0, j], preferred_element_type=F32
        )


def level_far_kernel(
    places, mid_w, far_w, mid, far, transform_in, gate_in, carried, bias,
    transform_out, gate_out, carried_out, low_out,
):
    parts = []
    for j, part in enumerate((transform_in, gate_in)):
        total = part[...] + jnp.dot(mid[...], mid_w[0, j], preferred_element_type=F32)
        total = total + jnp.dot(far[...], far_w[0, j], preferred_element_type=F32)
        parts.append(total + bias[j : j + 1, :])
    transform, gate = parts
    transform_out[...] = transform
    gate_out[...] = gate
    opened = 1.0 / (1.0 + jnp.exp(-gate))
    swished = transform / (1.0 + jnp.exp(-transform))
    mixed = opened * swished + (1.0 - opened) * carried[...].astype(F32)
    carried_out[...] = mixed
    low_out[...] = mixed.astype(BF16)


def level_back_kernel(places, far_w, mid_w, transform, gate, carried, grad, both_out, carry_out, bias_out, far_out, mid_out):
    width = transform.shape[1]
    value = grad[...]
    opened = 1.0 / (1.0 + jnp.exp(-gate[...]))
    squashed = 1.0 / (1.0 + jnp.exp(-transform[...]))
    swished = transform[...] * squashed
    slope = value * opened
    first = slope * (squashed * (1.0 + transform[...] * (1.0 - squashed)))
    second = (slope * (1.0 - opened)) * (swished - carried[...].astype(F32))
    carry_out[...] = value - slope
    both_out[:, :width] = first.astype(BF16)
    both_out[:, width:] = second.astype(BF16)

    @pl.when(pl.program_id(0) == 0)
    def _():
        bias_out[...] = jnp.zeros_like(bias_out)

    bias_out[:, :width] += jnp.sum(first.astype(BF16).astype(F32), axis=0, keepdims=True)
    bias_out[:, width:] += jnp.sum(second.astype(BF16).astype(F32), axis=0, keepdims=True)
    far_out[...] = back_product(both_out, far_w).astype(BF16)
    mid_out[...] = back_product(both_out, mid_w)


def back_product(both, weights):
    width = weights.shape[3]
    dims = (((1,), (1,)), ((), ()))
    first = lax.dot_general(both[:, :width], weights[0, 0], dims, preferred_element_type=F32)
    return first + lax.dot_general(both[:, width:], weights[0, 1], dims, preferred_element_type=F32)


def level_rest_kernel(places, near_w, own_w, both, carry, near_out, own_out):
    near_out[...] = back_product(both, near_w).astype(BF16)
    own_out[...] = back_product(both, own_w) + carry[...]


NT = (((1,), (1,)), ((), ()))
TN = (((0,), (0,)), ((), ()))


def dot(left, right, dims=(((1,), (0,)), ((), ()))):
    return lax.dot_general(left, right, dims, preferred_element_type=F32)


def local_call(kernel, arrays, shapes, scalars=None, cost=FREE):
    vm = pl.BlockSpec(memory_space=pltpu.VMEM)
    specs = [vm] * len(arrays)
    if scalars is not None:
        arrays = (scalars, *arrays)
        specs = [pl.BlockSpec(memory_space=pltpu.SMEM)] + specs
    return pl.pallas_call(
        kernel,
        in_specs=specs,
        out_specs=[vm] * len(shapes),
        out_shape=[jax.ShapeDtypeStruct(shape, kind) for shape, kind in shapes],
        compiler_params=pltpu.CompilerParams(vmem_limit_bytes=VMEM_LIMIT),
        cost_estimate=cost,
    )(*arrays)


def center_scale(total):
    center = total - jnp.mean(total, axis=-1, keepdims=True)
    return center, lax.rsqrt(jnp.mean(center * center, axis=-1, keepdims=True) + EPSILON)


def norm_kernel(pair, got, bias, base, gain, shift, total_out, hidden_out, low_out):
    total = pair[...].astype(F32) + got[...].astype(F32) + bias[...] + base[...]
    center, spread = center_scale(total)
    hidden = center * spread * gain[...] + shift[...]
    total_out[...] = total
    hidden_out[...] = hidden
    low_out[...] = hidden.astype(BF16)


def norm_back(total, gain, grad, grad_out, low_out, sums_out):
    center, spread = center_scale(total)
    normed = center * spread
    inner = grad * gain
    mean_inner = jnp.mean(inner, axis=-1, keepdims=True)
    mean_both = jnp.mean(inner * normed, axis=-1, keepdims=True)
    result = spread * (inner - mean_inner - normed * mean_both)
    low = result.astype(BF16)
    grad_out[...] = result
    low_out[...] = low
    sums_out[0:1, :] = jnp.sum(grad * normed, axis=0, keepdims=True)
    sums_out[1:2, :] = jnp.sum(grad, axis=0, keepdims=True)
    sums_out[2:3, :] = jnp.sum(low.astype(F32), axis=0, keepdims=True)


def last_norm_kernel(
    pair, got, bias, base, gain, shift, out_grad, encoded_out, grad_out, low_out, sums_out
):
    total = pair[...].astype(F32) + got[...].astype(F32) + bias[...] + base[...]
    center, spread = center_scale(total)
    encoded_out[...] = center * spread * gain[...] + shift[...]
    norm_back(total, gain[...], out_grad[...], grad_out, low_out, sums_out)


def norm_back_kernel(pair, got, base, total, gain, grad_out, low_out, sums_out):
    grad = pair[...].astype(F32) + got[...].astype(F32) + base[...]
    norm_back(total[...], gain[...], grad, grad_out, low_out, sums_out)


def project_kernel(perm, inputs, weight, own_out, send_out):
    half = own_out.shape[0]
    state = dot(perm[...], inputs[...]).astype(BF16)
    own_out[...] = state[:half]
    send_out[...] = dot(state[half:], weight[...]).astype(BF16)


def project_back_kernel(own, other, perm, weight, words_out, grad_out):
    half = own.shape[0]
    words = dot(perm[:half], own[...], TN) + dot(perm[half:], other[...], TN)
    words = words.astype(BF16)
    words_out[...] = words
    grad_out[...] = dot(words, weight[...], NT)


def head_probs(qkv, head, width, same):
    query = qkv[:, head * HEAD : (head + 1) * HEAD]
    keys = qkv[:, width + head * HEAD : width + (head + 1) * HEAD]
    scores = jnp.where(same, dot(query, keys, NT) * HEAD ** (-0.5), NEGATIVE)
    exps = jnp.exp(scores - jnp.max(scores, axis=-1, keepdims=True))
    return query, keys, exps * (1.0 / jnp.sum(exps, axis=-1, keepdims=True))


def attend_kernel(own, other, weight, biases, column, row, out_w, qkv_out, mixed_out, send_out):
    half, width = own.shape[0], out_w.shape[0]
    for rows, part in ((slice(0, half), own), (slice(half, 2 * half), other)):
        product = dot(part[...], weight[...], NT)
        qkv_out[rows, :width] = (product[:, :width] + biases[0:1, :]).astype(BF16)
        qkv_out[rows, width : 2 * width] = product[:, width : 2 * width].astype(BF16)
        qkv_out[rows, 2 * width :] = (product[:, 2 * width :] + biases[1:2, :]).astype(BF16)
    qkv = qkv_out[...]
    same = column[...] == row[...]
    for head in range(width // HEAD):
        _, _, probs = head_probs(qkv, head, width, same)
        values = qkv[:, 2 * width + head * HEAD : 2 * width + (head + 1) * HEAD]
        mixed_out[:, head * HEAD : (head + 1) * HEAD] = dot(probs.astype(BF16), values).astype(BF16)
    send_out[...] = dot(mixed_out[half:, :], out_w[...]).astype(BF16)


def attend_back_kernel(own, other, out_w, qkv_ref, column, row, weight, grad_out, sums_out, send_out):
    half, width = own.shape[0], out_w.shape[0]
    qkv = qkv_ref[...]
    same = column[...] == row[...]
    mixed = jnp.concatenate(
        [dot(part[...], out_w[...], NT).astype(BF16) for part in (own, other)], axis=0
    )
    scale = HEAD ** (-0.5)
    for head in range(width // HEAD):
        query, keys, probs = head_probs(qkv, head, width, same)
        values = qkv[:, 2 * width + head * HEAD : 2 * width + (head + 1) * HEAD]
        grads = mixed[:, head * HEAD : (head + 1) * HEAD]
        inner = dot(grads, values, NT)
        slope = probs * (inner - jnp.sum(probs * inner, axis=-1, keepdims=True))
        slope = slope.astype(BF16)
        parts = (
            dot(slope, keys) * scale,
            dot(slope, query, TN) * scale,
            dot(probs.astype(BF16), grads, TN),
        )
        for j, part in enumerate(parts):
            first = j * width + head * HEAD
            grad_out[:, first : first + HEAD] = part.astype(BF16)
    sums_out[...] = jnp.sum(grad_out[...].astype(F32), axis=0, keepdims=True)
    send_out[...] = dot(grad_out[half:, :], weight[...]).astype(BF16)


def gelu_parts(value):
    scale = 0.7978845608028654
    square = value * value
    t = jnp.tanh(scale * value * (1.0 + 0.044715 * square))
    return t, scale * (1.0 + 3 * 0.044715 * square)


def feed_kernel(own, other, up_w, up_b, down_w, upward_out, active_out, send_out):
    half = own.shape[0]
    for rows, part in ((slice(0, half), own), (slice(half, 2 * half), other)):
        upward = dot(part[...], up_w[...]) + up_b[...]
        t, _ = gelu_parts(upward)
        upward_out[rows, :] = upward
        active_out[rows, :] = (0.5 * upward * (1.0 + t)).astype(BF16)
    send_out[...] = dot(active_out[half:, :], down_w[...]).astype(BF16)


def feed_back_kernel(own, other, down_w, upward_ref, up_w, grad_out, sums_out, send_out):
    half = own.shape[0]
    total = jnp.zeros(sums_out.shape, F32)
    for rows, part in ((slice(0, half), own), (slice(half, 2 * half), other)):
        grad = dot(part[...], down_w[...], NT)
        upward = upward_ref[rows, :]
        t, inner = gelu_parts(upward)
        slope = 0.5 * (1.0 + t) + 0.5 * upward * (1.0 - t * t) * inner
        low = (grad * slope).astype(BF16)
        grad_out[rows, :] = low
        total = total + jnp.sum(low.astype(F32), axis=0, keepdims=True)
    sums_out[...] = total
    send_out[...] = dot(grad_out[half:, :], up_w[...], NT).astype(BF16)


def weight_blocks_kernel(counts, spots, *refs):
    *operands, keep, send = refs
    half, rows, _ = keep.shape
    first, position = 0, 0
    for count in counts:
        lefts, right = operands[position : position + count], operands[position + count]
        position += count + 1
        width, step = right.shape[1], right.shape[0] // count
        product = sum(
            dot(left[...], right[i * step : (i + 1) * step, :], TN) for i, left in enumerate(lefts)
        )
        cols = slice(first, first + width)
        first += width
        for d in range(2 * half):
            block = product[d * rows : (d + 1) * rows].astype(BF16)

            @pl.when(spots[d] < half)
            def _():
                keep[spots[d], :, cols] = block

            @pl.when(spots[d] >= half)
            def _():
                send[spots[d] - half, :, cols] = block


def weight_blocks(groups, spots):
    peers = spots.shape[0]
    total = sum(right.shape[1] for _, right in groups)
    rows = groups[0][0][0].shape[1] // peers
    shape = ((peers // 2, rows, total), BF16)
    return local_call(
        functools.partial(weight_blocks_kernel, [len(lefts) for lefts, _ in groups]),
        [item for lefts, right in groups for item in (*lefts, right)],
        [shape, shape],
        spots,
        pl.CostEstimate(flops=4 * 10**9, bytes_accessed=10**7, transcendentals=0),
    )


def fence(*values):
    return lax.optimization_barrier(values)


def swap(values, axis, bit):
    count = lax.axis_size(axis)
    return lax.ppermute(values, axis, [(i, i ^ bit) for i in range(count)])


def bit_reversed(count):
    bits = count.bit_length() - 1
    return [sum(((i >> b) & 1) << (bits - 1 - b) for b in range(bits)) for i in range(count)]


def blocks_by_peer(values, axis, order, count):
    size = values.shape[axis] // count
    me = lax.axis_index("dp")
    return [lax.dynamic_slice_in_dim(values, (me ^ r) * size, size, axis) for r in order]


def on_device(
    chars,
    char_mask,
    word_order,
    segment_ids,
    char_table,
    conv_weight,
    conv_bias,
    highway_weight,
    highway_bias,
    project_weight,
    project_bias,
    position_table,
    norm_gain,
    norm_bias,
    qkv_weight,
    qv_bias,
    out_weight,
    out_bias,
    up_weight,
    up_bias,
    down_weight,
    down_bias,
    out_grad,
):
    dp_count = lax.axis_size("dp")
    dp_index = lax.axis_index("dp")
    mp_index = lax.axis_index("mp")
    low = mp_index & 1
    word_count = chars.shape[0]
    per_peer = word_count // dp_count
    half_count = word_count // 2
    local_channels = conv_weight.shape[1]
    dp_bits = [1 << b for b in range(dp_count.bit_length() - 1)]
    order = bit_reversed(dp_count)

    local_rows = (
        lax.dynamic_slice(
            word_order.reshape(dp_count, dp_count, per_peer),
            (0, dp_index, 0),
            (dp_count, 1, per_peer),
        ).reshape(word_count)
        - dp_index * word_count
    )
    places = local_rows ^ (low * half_count)
    perm = (jnp.arange(word_count, dtype=jnp.int32)[:, None] == places[None, :]).astype(BF16)

    def own_half(values):
        return lax.dynamic_slice_in_dim(values, low * half_count, half_count, 0)

    ids = jnp.where(char_mask > 0, chars, -1).reshape(dp_count, per_peer * CHARS)
    ids = lax.all_to_all(ids, "dp", split_axis=0, concat_axis=0, tiled=True)
    weights = jnp.swapaxes(highway_weight, 1, 2)
    ids, weights = fence(ids, weights)
    ids = ids.reshape(word_count, CHARS)

    used_taps = filter_mask(local_channels, mp_index * local_channels)
    filters = jnp.where(used_taps, conv_weight, jnp.zeros_like(conv_weight))
    counts = block_counts(ids, BLOCK)
    pooled, embedded = cnn_forward(
        ids, counts, spread_table(char_table), filters, conv_bias, BLOCK
    )
    places = mp_index ^ jnp.arange(4, dtype=jnp.int32)
    square = (word_count, local_channels)
    wide_f32 = jax.ShapeDtypeStruct(square, F32)
    wide_bf16 = jax.ShapeDtypeStruct(square, BF16)

    carried = inputs = pooled
    kept = []
    theirs = None
    for depth in range(LAYERS):
        a = inputs
        b = swap(a, "mp", 1)
        c = swap(a, "mp", 2)
        d = swap(c, "mp", 1)
        transform, gate = level_call(
            level_near_kernel, places, depth, (0, 1), weights, (a, b), [wide_f32] * 2, True
        )
        transform, gate, mixed_state, inputs = level_call(
            level_far_kernel,
            places,
            depth,
            (2, 3),
            weights,
            (c, d, transform, gate, carried, highway_bias[depth]),
            [wide_f32, wide_f32, wide_f32, wide_bf16],
        )
        whole = jnp.zeros((word_count, CHANNELS), BF16)
        for r, piece in enumerate((a, b, c, d)):
            whole = lax.dynamic_update_slice(whole, piece, (0, (mp_index ^ r) * local_channels))
        blocks = blocks_by_peer(whole, 1, order, dp_count)
        ours = jnp.concatenate(blocks[: dp_count // 2], axis=1)
        theirs = jnp.concatenate(blocks[dp_count // 2 :], axis=1)
        inputs, ours, theirs = fence(inputs, ours, theirs)
        theirs = swap(theirs, "dp", 1)
        kept.append([carried, transform, gate, ours, theirs])
        carried = mixed_state

    width = project_weight.shape[1]
    half_f32, half_bf16 = ((half_count, width), F32), ((half_count, width), BF16)
    sums_shape = ((3, width), F32)

    def cross(own, matrix, sent, beside=None, dims=(((1,), (0,)), ((), ()))):
        got = swap(sent, "mp", 1)
        pair, beside = fence((dot(own, matrix, dims) + got.astype(F32)).astype(BF16), beside)
        return pair, swap(pair, "mp", 2), beside

    def row(vector):
        return vector.reshape(1, -1)

    def send(parts, bit):
        return parts[0], swap(parts[1], "dp", bit)

    def join(parts):
        half = parts[0].shape[0] // 2
        if half == 0:
            return parts[0][0].astype(F32) + parts[1][0].astype(F32)
        return [
            (parts[0][rows].astype(F32) + parts[1][rows].astype(F32)).astype(BF16)
            for rows in (slice(0, half), slice(half, 2 * half))
        ]

    def finish(parts, bits):
        for bit in bits:
            parts = send(join(parts), bit)
        return join(parts)

    own_state, sent = local_call(
        project_kernel,
        (perm, inputs, project_weight),
        [((half_count, local_channels), BF16), half_bf16],
    )
    pair, got, kept[0][4] = cross(own_state, project_weight, sent, kept[0][4])
    embed_total, hidden_in, x_own = local_call(
        norm_kernel,
        (pair, got, row(project_bias), own_half(position_table), row(norm_gain[0]), row(norm_bias[0])),
        [half_f32, half_f32, half_bf16],
    )
    x_other = swap(x_own, "mp", 1)
    local_heads = qkv_weight.shape[2]
    qkv_flat = jnp.transpose(qkv_weight, (1, 2, 0)).reshape(3 * local_heads, width)
    segments = segment_ids[0]
    segments = jnp.where(low > 0, jnp.roll(segments, half_count), segments)
    column, line = segments.reshape(-1, 1), segments.reshape(1, -1)
    qkv_shape = ((word_count, 3 * local_heads), BF16)
    qkv, mixed, sent = local_call(
        attend_kernel,
        (x_own, x_other, qkv_flat, qv_bias, column, line, out_weight),
        [qkv_shape, ((word_count, local_heads), BF16), half_bf16],
    )
    pair, got, _ = cross(mixed[:half_count], out_weight, sent)
    resid_one, hidden_mid, mid_own = local_call(
        norm_kernel,
        (pair, got, row(out_bias), hidden_in, row(norm_gain[1]), row(norm_bias[1])),
        [half_f32, half_f32, half_bf16],
    )
    mid_other = swap(mid_own, "mp", 1)
    hidden_units = up_weight.shape[1]
    upward, activated, sent = local_call(
        feed_kernel,
        (mid_own, mid_other, up_weight, row(up_bias), down_weight),
        [((word_count, hidden_units), F32), ((word_count, hidden_units), BF16), half_bf16],
    )
    pair, got, kept[1][4] = cross(activated[:half_count], down_weight, sent, kept[1][4])
    encoded, resid_two_grad, down_own, sums_two = local_call(
        last_norm_kernel,
        (
            pair,
            got,
            row(down_bias),
            hidden_mid,
            row(norm_gain[2]),
            row(norm_bias[2]),
            own_half(out_grad),
        ),
        [half_f32, half_f32, half_bf16, sums_shape],
    )
    down_other = swap(down_own, "mp", 1)
    up_grad, up_bias_grad, sent = local_call(
        feed_back_kernel,
        (down_own, down_other, down_weight, upward, up_weight),
        [((word_count, hidden_units), BF16), ((1, hidden_units), F32), half_bf16],
    )
    pair, got, _ = cross(up_grad[:half_count], up_weight, sent, None, NT)
    resid_one_grad, attn_own, sums_one = local_call(
        norm_back_kernel,
        (pair, got, resid_two_grad, resid_one, row(norm_gain[1])),
        [half_f32, half_bf16, sums_shape],
    )
    spots = jnp.sum(
        jnp.where(
            (dp_index ^ jnp.array(order, jnp.int32))[None, :]
            == jnp.arange(dp_count, dtype=jnp.int32)[:, None],
            jnp.arange(dp_count, dtype=jnp.int32)[None, :],
            0,
        ),
        axis=1,
    )
    first_blocks = weight_blocks(
        [((mid_own, mid_other), up_grad), ((down_own, down_other), activated)], spots
    )
    attn_own, first_blocks = fence(attn_own, first_blocks)
    first_parts = send(first_blocks, dp_bits[0])
    attn_other = swap(attn_own, "mp", 1)
    qkv_grad, qkv_sums, sent = local_call(
        attend_back_kernel,
        (attn_own, attn_other, out_weight, qkv, column, line, qkv_flat),
        [qkv_shape, ((1, 3 * local_heads), F32), half_bf16],
    )
    pair, got, _ = cross(qkv_grad[:half_count], qkv_flat, sent)
    embed_grad, proj_own, sums_zero = local_call(
        norm_back_kernel,
        (pair, got, resid_one_grad, embed_total, row(norm_gain[0])),
        [half_f32, half_bf16, sums_shape],
    )
    proj_own, first_parts = fence(proj_own, first_parts)
    first_parts = send(join(first_parts), dp_bits[1])
    proj_other = swap(proj_own, "mp", 1)
    proj_words, state_grad = local_call(
        project_back_kernel,
        (proj_own, proj_other, perm, project_weight),
        [((word_count, width), BF16), ((word_count, local_channels), F32)],
    )
    second_blocks = weight_blocks(
        [((x_own, x_other), qkv_grad), ((attn_own, attn_other), mixed), ((proj_words,), inputs)],
        spots,
    )

    def level_back(depth, grad, beside):
        carried_now, transform_now, gate_now, _, _ = kept[depth]
        both_low, carry, bias_sum, far, mid = level_call(
            level_back_kernel,
            places,
            depth,
            (3, 2),
            weights,
            (transform_now, gate_now, carried_now, grad),
            [
                jax.ShapeDtypeStruct((word_count, 2 * local_channels), BF16),
                wide_f32,
                jax.ShapeDtypeStruct((1, 2 * local_channels), F32),
                wide_bf16,
                wide_f32,
            ],
        )
        got = swap(far, "mp", 1)
        pair, beside = fence((mid + got.astype(F32)).astype(BF16), beside)
        crossing = swap(pair, "mp", 2)
        near, own = level_call(
            level_rest_kernel,
            places,
            depth,
            (1, 0),
            weights,
            (both_low, carry),
            [wide_bf16, wide_f32],
            True,
        )
        below = own + swap(near, "mp", 1).astype(F32) + crossing.astype(F32)
        return below, bias_sum.reshape(2, local_channels), both_low, beside

    def level_weights(depth, half, peer):
        _, _, _, ours, theirs = kept[depth]
        total = jnp.einsum("nk,nf->kf", ours, half, preferred_element_type=F32)
        total += jnp.einsum("nk,nf->kf", theirs, peer, preferred_element_type=F32)
        total = total.astype(BF16).reshape(2, dp_count // 4, CHANNELS // dp_count, -1)
        return [total[0], total[1]]

    state_grad, bias_one, low_one, first_parts = level_back(1, state_grad, first_parts)
    first_parts = send(join(first_parts), dp_bits[2])
    peer_one = swap(low_one, "dp", 1)
    state_grad, second_blocks = fence(state_grad, second_blocks)
    state_grad, bias_zero, low_zero, peer_one = level_back(0, state_grad, peer_one)
    pooled_grad = state_grad.astype(BF16)
    peer_zero = swap(low_zero, "dp", 1)
    one_blocks = level_weights(1, low_one, peer_one)
    pooled_grad, one_blocks, first_parts = fence(pooled_grad, one_blocks, first_parts)
    first_sum = finish(first_parts, dp_bits[3:])

    def pack(items):
        flat = jnp.concatenate([item.reshape(-1) for item in items])
        return jnp.pad(flat, (0, -flat.size % 1024)).reshape(-1, 128)

    def unpack(packed, items):
        flat = packed.reshape(-1)
        result, first = [], 0
        for item in items:
            result.append(flat[first : first + item.size].reshape(item.shape))
            first += item.size
        return result

    def exchange(values, bit):
        sent = fence(values.astype(BF16))[0]
        return sent, swap(sent, "dp", bit)

    def combine(parts):
        return parts[0].astype(F32) + parts[1].astype(F32)

    def complete(parts, bits):
        for bit in bits:
            parts = exchange(combine(parts), bit)
        return combine(parts)

    row_items = [sums_zero, sums_one, sums_two]
    row_pack = pack(row_items)
    row_pack = row_pack + swap(row_pack, "mp", 1)
    quarter = half_count // 2
    high = (mp_index >> 1) & 1
    position_part = lax.dynamic_slice_in_dim(embed_grad, high * quarter, quarter, 0)
    early_items = [row_pack, qkv_sums, up_bias_grad, position_part]
    early = exchange(pack(early_items), dp_bits[0])

    one_parts = send(one_blocks, dp_bits[1])
    middle = local_channels // 2
    lower, upper = slice(0, middle), slice(middle, local_channels)
    cnn_out = cnn_backward(
        counts, embedded, filters[:, lower], conv_bias[lower], pooled_grad[:, lower], None, BLOCK
    )
    (conv_low, bias_low, embed_part), one_parts, peer_zero, early = fence(
        cnn_out, one_parts, peer_zero, early
    )
    one_blocks = join(one_parts)
    zero_blocks = level_weights(0, low_zero, peer_zero)
    embed_part, one_blocks, zero_blocks, early = fence(
        embed_part, one_blocks, zero_blocks, combine(early)
    )
    one_parts = send(one_blocks, dp_bits[2])
    zero_parts = send(zero_blocks, dp_bits[1])
    second_parts = send(second_blocks, dp_bits[0])
    early = exchange(early, dp_bits[1])
    cnn_out = cnn_backward(
        counts, embedded, filters[:, upper], conv_bias[upper], pooled_grad[:, upper], embed_part, BLOCK
    )
    (conv_high, bias_high, embed_part), one_parts, zero_parts, second_parts, early = fence(
        cnn_out, one_parts, zero_parts, second_parts, early
    )
    conv_sum = jnp.concatenate([conv_low, conv_high], axis=1)
    conv_items = [
        jnp.where(used_taps, conv_sum, jnp.zeros_like(conv_sum)),
        jnp.concatenate([bias_low[0], bias_high[0]]),
        jnp.stack([bias_zero, bias_one], axis=0),
    ]
    conv_parts = exchange(pack(conv_items), dp_bits[0])
    zero_parts = send(join(zero_parts), dp_bits[2])
    second_parts = send(join(second_parts), dp_bits[1])
    early = exchange(combine(early), dp_bits[2])
    one_sum = finish(one_parts, dp_bits[3:])
    table_sum = table_gradient(ids.T, embed_part, char_table.shape[0])
    table_sum, conv_parts = fence(table_sum, conv_parts)
    conv_parts = exchange(combine(conv_parts), dp_bits[1])
    table_total = pack([table_sum])
    table_total = table_total + swap(table_total, "mp", 1)
    table_total = table_total + swap(table_total, "mp", 2)
    table_total, conv_parts, second_parts = fence(table_total, conv_parts, second_parts)
    conv_parts = exchange(combine(conv_parts), dp_bits[2])
    second_parts = send(join(second_parts), dp_bits[2])
    for bit in dp_bits:
        table_total = table_total + swap(table_total, "dp", bit)
    table_total = unpack(table_total, [table_sum])[0]
    conv_sums = unpack(complete(conv_parts, dp_bits[3:]), conv_items)
    second_sum = finish(second_parts, dp_bits[3:])
    zero_sum = finish(zero_parts, dp_bits[3:])
    highway_weight_grad = jnp.stack([zero_sum, one_sum], axis=0).reshape(
        LAYERS, -1, 2, local_channels
    )
    row_pack, qkv_sums, up_bias_grad, position_part = unpack(
        complete(early, dp_bits[3:]), early_items
    )
    sums_zero, sums_one, sums_two = unpack(row_pack, row_items)
    qv_bias_grad = jnp.stack(
        [qkv_sums[0, :local_heads], qkv_sums[0, 2 * local_heads :]], axis=0
    )
    position_other = swap(position_part, "mp", 2)
    position_half = jnp.concatenate(
        [
            jnp.where(high > 0, position_other, position_part),
            jnp.where(high > 0, position_part, position_other),
        ],
        axis=0,
    )

    def both_halves(values):
        return jnp.concatenate([values, swap(values, "mp", 1)], axis=0)

    position_grad = both_halves(position_half)

    def in_order(values):
        first, second = values[:half_count], values[half_count:]
        return jnp.concatenate(
            [jnp.where(low > 0, second, first), jnp.where(low > 0, first, second)], axis=0
        )

    def split(total, widths):
        parts, first = [], 0
        for width in widths:
            parts.append(total[:, first : first + width])
            first += width
        return parts

    up_sum, down_sum = split(first_sum, (up_weight.shape[1], down_weight.shape[0]))
    qkv_sum, out_sum, project_sum = split(
        second_sum, (3 * local_heads, local_heads, local_channels)
    )
    return (
        in_order(both_halves(encoded)),
        table_total,
        conv_sums[0],
        conv_sums[1],
        highway_weight_grad,
        conv_sums[2],
        project_sum.T,
        sums_zero[2],
        in_order(position_grad),
        jnp.stack([sums_zero[0], sums_one[0], sums_two[0]], axis=0),
        jnp.stack([sums_zero[1], sums_one[1], sums_two[1]], axis=0),
        qkv_sum.reshape(-1, 3, local_heads),
        qv_bias_grad,
        out_sum.T,
        sums_one[2],
        up_sum,
        up_bias_grad[0],
        down_sum.T,
        sums_two[2],
    )


def solution(mesh):
    return jax.shard_map(
        on_device,
        mesh=mesh,
        in_specs=(
            P("dp", None),
            P("dp", None),
            P(),
            P("dp", None),
            P(),
            P(None, "mp"),
            P("mp"),
            P(None, None, None, "mp"),
            P(None, None, "mp"),
            P("mp", None),
            P(),
            P(),
            P(),
            P(),
            P(None, None, "mp"),
            P(None, "mp"),
            P("mp", None),
            P(),
            P(None, "mp"),
            P("mp"),
            P("mp", None),
            P(),
            P("dp", None),
        ),
        out_specs=(
            P("dp", None),
            P(),
            P(None, "mp"),
            P("mp"),
            P(None, "dp", None, "mp"),
            P(None, None, "mp"),
            P("mp", "dp"),
            P(),
            P(),
            P(),
            P(),
            P("dp", None, "mp"),
            P(None, "mp"),
            P("mp", "dp"),
            P(),
            P("dp", "mp"),
            P("mp"),
            P("mp", "dp"),
            P(),
        ),
        check_vma=False,
    )
```

```python
import functools

import jax
import jax.numpy as jnp
from jax import lax
from jax.experimental import pallas as pl
from jax.experimental.pallas import tpu as pltpu
from jax.sharding import PartitionSpec as P

HEAD = 64
CHANNELS = 2048
CHAR_DIM = 16
CHARS = 50
TAPS = 7
LAYERS = 2
BLOCK = 128
TILES = 1

EPSILON = 1e-05
NEGATIVE = -1e30
F32 = jnp.float32
BF16 = jnp.bfloat16


def filter_mask(local_count, first):
    channel = first + jnp.arange(local_count, dtype=jnp.int32)
    tap_count = 1 + sum(
        ((channel >= CHANNELS // divisor).astype(jnp.int32) for divisor in (64, 32, 16, 8, 4, 2))
    )
    tap_index = jnp.arange(TAPS * CHAR_DIM, dtype=jnp.int32) // CHAR_DIM
    return tap_index[:, None] < tap_count[None, :]


STEPS = 8
ROWS = 7
SPAN = STEPS * CHAR_DIM
VMEM_LIMIT = 24 << 20
FREE = pl.CostEstimate(flops=1, bytes_accessed=1, transcendentals=0)

def spread_table(char_table):
    low = char_table.astype(BF16)
    eye = jnp.eye(STEPS, dtype=BF16)
    first = low[:256]
    rest = jnp.pad(low[256:], ((0, CHAR_DIM - (low.shape[0] - 256)), (0, 0)))
    parts = [(eye[:, None, :, None] * part[None, :, None, :]).reshape(-1, SPAN) for part in (first, rest)]
    return jnp.concatenate(parts, axis=0)

def place_filters(filters_ref, shifted):
    shifted[...] = jnp.zeros_like(shifted)
    taps = filters_ref.shape[0]
    width = filters_ref.shape[1]
    halved = (filters_ref[...].astype(F32) * 0.5).astype(BF16)
    for r in range(STEPS):
        shifted[CHAR_DIM * r : CHAR_DIM * r + taps, r * width : (r + 1) * width] = halved

def forward_kernel(block, counts, ids_ref, table_ref, filters_ref, bias_ref, pooled_ref, embed_ref, shifted, hot, total):
    words, width = pooled_ref.shape
    place_filters(filters_ref, shifted)
    lanes = lax.broadcasted_iota(jnp.int32, (words, 256), 1)
    lane = lax.broadcasted_iota(jnp.int32, (words, 128), 1)
    embed_ref[ROWS] = jnp.zeros_like(embed_ref[ROWS])
    total[...] = jnp.zeros_like(total)
    for q in range(ROWS):
        left = jnp.zeros((words, 128), F32)
        for r in range(STEPS):
            j = q * STEPS + r
            if j < CHARS:
                ids = ids_ref[:, j : j + 1]
                hot[:, r * 256 : (r + 1) * 256] = jnp.where(ids == lanes, 1.0, 0.0).astype(BF16)
                mark = jnp.where(lane // CHAR_DIM == r, lane % CHAR_DIM + 256, -7)
                left = jnp.where(ids == mark, 1.0, left)
            else:
                hot[:, r * 256 : (r + 1) * 256] = jnp.zeros((words, 256), BF16)
        hot[:, STEPS * 256 :] = left.astype(BF16)
        embed_ref[q] = jnp.dot(hot[...], table_ref[...], preferred_element_type=F32).astype(BF16)
    half = bias_ref[...] * 0.5
    blocks = words // block
    for q in range(ROWS):
        def one(i, carry):
            rows = pl.ds(pl.multiple_of(i * block, block), block)
            x = jnp.concatenate([embed_ref[q, rows, :], embed_ref[q + 1, rows, :]], axis=1)
            for r in range(STEPS):
                u = jnp.dot(x, shifted[:, r * width : (r + 1) * width], preferred_element_type=F32) + half
                total[rows, :] += u + u * jnp.tanh(u)
            return carry
        lax.fori_loop(counts[blocks + q], blocks, one, 0)
    rest = half + half * jnp.tanh(half)
    for i in range(blocks):
        rows = slice(i * block, (i + 1) * block)
        seen = STEPS * counts[i]
        pooled_ref[rows, :] = ((total[rows, :] + (CHARS - seen).astype(F32) * rest) * (1.0 / CHARS)).astype(BF16)

def block_counts(ids, block):
    most = jnp.max(jnp.sum((ids >= 0).astype(jnp.int32), axis=1).reshape(-1, block), axis=1)
    need = (most + STEPS - 1) // STEPS
    first = jnp.sum((need[None, :] <= jnp.arange(ROWS, dtype=jnp.int32)[:, None]).astype(jnp.int32), axis=1)
    return jnp.concatenate([need, first])

def cnn_forward(ids, counts, table, filters, bias, block):
    words = ids.shape[0]
    width = filters.shape[1]
    vm = pl.BlockSpec(memory_space=pltpu.VMEM)
    return pl.pallas_call(
        functools.partial(forward_kernel, block),
        in_specs=[pl.BlockSpec(memory_space=pltpu.SMEM), vm, vm, vm, vm],
        out_specs=[vm, vm],
        out_shape=[jax.ShapeDtypeStruct((words, width), BF16), jax.ShapeDtypeStruct((ROWS + 1, words, SPAN), BF16)],
        scratch_shapes=[pltpu.VMEM((2 * SPAN, STEPS * width), BF16), pltpu.VMEM((words, STEPS * 256 + 128), BF16), pltpu.VMEM((words, width), F32)],
        compiler_params=pltpu.CompilerParams(vmem_limit_bytes=VMEM_LIMIT),
        cost_estimate=FREE,
    )(counts, ids, table, filters, bias.reshape(1, -1))


def backward_kernel(
    block,
    counts,
    embed_ref,
    filters_ref,
    bias_ref,
    grad_ref,
    embed_in,
    filter_out,
    bias_out,
    embed_grad,
    shifted,
    slopes,
    sums,
):
    words, width = grad_ref.shape
    blocks = words // block
    place_filters(filters_ref, shifted)
    half = bias_ref[...] * 0.5
    still = jnp.tanh(half)
    rest = (1.0 + still) + half * (1.0 - still * still)
    bias_out[...] = jnp.zeros_like(bias_out)
    sums[...] = jnp.zeros_like(sums)
    if embed_in is None:
        embed_grad[...] = jnp.zeros_like(embed_grad)
    else:
        embed_grad[...] = embed_in[...]
    scale = 0.5 / CHARS
    for i in range(blocks):
        grads = grad_ref[i * block : (i + 1) * block, :].astype(F32) * scale
        left = (CHARS - STEPS * counts[i]).astype(F32)
        bias_out[...] += jnp.sum(grads, axis=0, keepdims=True) * (rest * left)
    for q in range(ROWS):
        first = counts[blocks + q]
        if q:

            def clear(i, carry):
                rows = pl.ds(pl.multiple_of(i * block, block), block)
                slopes[rows, :] = jnp.zeros((block, STEPS * width), BF16)
                return carry

            lax.fori_loop(counts[blocks + q - 1], first, clear, 0)

        def one(i, carry):
            rows = pl.ds(pl.multiple_of(i * block, block), block)
            x = jnp.concatenate([embed_ref[q, rows, :], embed_ref[q + 1, rows, :]], axis=1)
            grads = grad_ref[rows, :].astype(F32) * scale
            column = jnp.zeros((1, width), F32)
            for r in range(STEPS):
                cols = slice(r * width, (r + 1) * width)
                u = jnp.dot(x, shifted[:, cols], preferred_element_type=F32) + half
                t = jnp.tanh(u)
                slope = grads * ((1.0 + t) + u * (1.0 - t * t))
                column += jnp.sum(slope, axis=0, keepdims=True)
                slopes[rows, cols] = slope.astype(BF16)
            bias_out[...] += column
            return carry

        lax.fori_loop(first, blocks, one, 0)

        def spread(start):
            rows = slice(start, words)
            x = jnp.concatenate([embed_ref[q, rows, :], embed_ref[q + 1, rows, :]], axis=1)
            back = lax.dot_general(
                slopes[rows, :], shifted[...], (((1,), (1,)), ((), ())), preferred_element_type=F32
            )
            embed_grad[q, rows, :] += back[:, :SPAN]
            embed_grad[q + 1, rows, :] += back[:, SPAN:]
            for r in range(STEPS):
                cols = slice(r * width, (r + 1) * width)
                sums[:, cols] += lax.dot_general(
                    x, slopes[rows, cols], (((0,), (0,)), ((), ())), preferred_element_type=F32
                )

        middle = blocks // 2
        if q < 1:
            spread(0)
        else:

            @pl.when(first < middle)
            def _():
                spread(0)

            @pl.when((first >= middle) & (first < blocks))
            def _():
                spread(middle * block)

    taps = filters_ref.shape[0]
    total = sums[:taps, :width]
    for r in range(1, STEPS):
        lower = CHAR_DIM * r
        total = total + sums[lower : lower + taps, r * width : (r + 1) * width]
    filter_out[...] = total


def cnn_backward(counts, embed, filters, bias, grad, embed_grad, block):
    words, width = grad.shape
    taps = filters.shape[0]
    vm = pl.BlockSpec(memory_space=pltpu.VMEM)
    operands = [counts, embed, filters, bias.reshape(1, -1), grad]
    kernel = functools.partial(backward_kernel, block)
    if embed_grad is None:
        inner = kernel

        def kernel(counts, embed, filters, bias, grad, *rest):
            inner(counts, embed, filters, bias, grad, None, *rest)
    else:
        operands.append(embed_grad)
    return pl.pallas_call(
        kernel,
        in_specs=[pl.BlockSpec(memory_space=pltpu.SMEM)] + [vm] * (len(operands) - 1),
        out_specs=[vm] * 3,
        out_shape=[
            jax.ShapeDtypeStruct((taps, width), F32),
            jax.ShapeDtypeStruct((1, width), F32),
            jax.ShapeDtypeStruct((ROWS + 1, words, SPAN), F32),
        ],
        scratch_shapes=[
            pltpu.VMEM((2 * SPAN, STEPS * width), BF16),
            pltpu.VMEM((words, STEPS * width), BF16),
            pltpu.VMEM((2 * SPAN, STEPS * width), F32),
        ],
        compiler_params=pltpu.CompilerParams(vmem_limit_bytes=VMEM_LIMIT),
        cost_estimate=FREE,
    )(*operands)


def table_kernel(ids_ref, embed_grad, table_out, hot):
    vocab, words = hot.shape[0], ids_ref.shape[1]
    high = embed_grad[:ROWS].reshape(ROWS * words, SPAN) * 2.0
    low = high.astype(BF16)
    pair = jnp.concatenate([low, (high - low.astype(F32)).astype(BF16)], axis=1)
    which = lax.broadcasted_iota(jnp.int32, (vocab, words), 0)
    lane = lax.broadcasted_iota(jnp.int32, (vocab, SPAN), 1) // CHAR_DIM
    table = jnp.zeros((vocab, SPAN), F32)
    for r in range(STEPS):
        for q in range(ROWS):
            j = q * STEPS + r
            cols = slice(q * words, (q + 1) * words)
            if j < CHARS:
                hot[:, cols] = jnp.where(ids_ref[j : j + 1, :] == which, 1.0, 0.0).astype(BF16)
            else:
                hot[:, cols] = jnp.zeros((vocab, words), BF16)
        both = jnp.dot(hot[...], pair, preferred_element_type=F32)
        table = jnp.where(lane == r, both[:, :SPAN] + both[:, SPAN:], table)
    step = table_out.shape[0]
    for shift in (64, 32, 16):
        table = table + pltpu.roll(table, shift, 1)
    table_out[...] = jnp.zeros_like(table_out)
    for g in range(-(-vocab // step)):
        rows = min(step, vocab - g * step)
        cols = slice(g * CHAR_DIM, (g + 1) * CHAR_DIM)
        table_out[:rows, cols] = table[g * step : g * step + rows, cols]


def table_gradient(ids_columns, embed_grad, vocab):
    words = ids_columns.shape[1]
    rows = -(-vocab // 16) * 16
    vm = pl.BlockSpec(memory_space=pltpu.VMEM)
    return pl.pallas_call(
        table_kernel,
        in_specs=[vm, vm],
        out_specs=vm,
        out_shape=jax.ShapeDtypeStruct((-(-vocab // 64) * 8, SPAN), F32),
        scratch_shapes=[pltpu.VMEM((rows, ROWS * words), BF16)],
        compiler_params=pltpu.CompilerParams(vmem_limit_bytes=VMEM_LIMIT),
        cost_estimate=FREE,
    )(ids_columns, embed_grad)


def level_call(kernel, places, level, picks, weights, arrays, shapes, hidden=False):
    width = weights.shape[3]
    rows = arrays[0].shape[0]
    tile = rows // TILES
    weights = pltpu.with_memory_space_constraint(weights, pltpu.HBM)

    def picked(pick):
        return pl.BlockSpec((1, 2, width, width), lambda i, spots: (level, 0, spots[pick], 0))

    def tiled(shape):
        if shape[0] == rows:
            return pl.BlockSpec((tile, shape[1]), lambda i, spots: (i, 0))
        return pl.BlockSpec(shape, lambda i, spots: (0, 0))

    cost = FREE
    if hidden:
        cost = pl.CostEstimate(
            flops=8 * rows * width * width, bytes_accessed=16 * rows * width, transcendentals=0
        )
    return pl.pallas_call(
        kernel,
        grid_spec=pltpu.PrefetchScalarGridSpec(
            num_scalar_prefetch=1,
            grid=(TILES,),
            in_specs=[picked(pick) for pick in picks] + [tiled(item.shape) for item in arrays],
            out_specs=[tiled(item.shape) for item in shapes],
        ),
        out_shape=shapes,
        compiler_params=pltpu.CompilerParams(vmem_limit_bytes=VMEM_LIMIT),
        cost_estimate=cost,
    )(places, *[weights] * len(picks), *arrays)


def level_kernel(
    places, own_w, near_w, mid_w, far_w, own, near, mid, far, carried, bias,
    transform_out, gate_out, carried_out, low_out, *peers_out,
):
    if peers_out:
        ours, theirs = peers_out
        size = own.shape[1] * 4 // (places.shape[0] - 4)
        count = own.shape[1] // size
        for r, piece in enumerate((own, near, mid, far)):
            for h in range(count):
                spot = places[4 + places[r] * count + h]
                half = (places.shape[0] - 4) // 2
                block = piece[:, h * size : (h + 1) * size]

                @pl.when(spot < half)
                def _():
                    ours[:, pl.ds(pl.multiple_of(spot * size, size), size)] = block

                @pl.when(spot >= half)
                def _():
                    theirs[:, pl.ds(pl.multiple_of((spot - half) * size, size), size)] = block

    parts = []
    for j in range(2):
        total = dot(own[...], own_w[0, j]) + dot(near[...], near_w[0, j])
        total = total + dot(mid[...], mid_w[0, j]) + dot(far[...], far_w[0, j])
        parts.append(total + bias[j : j + 1, :])
    transform, gate = parts
    transform_out[...] = transform
    gate_out[...] = gate
    opened = 1.0 / (1.0 + jnp.exp(-gate))
    swished = transform / (1.0 + jnp.exp(-transform))
    mixed = opened * swished + (1.0 - opened) * carried[...].astype(F32)
    carried_out[...] = mixed
    low_out[...] = mixed.astype(BF16)


def level_back_kernel(places, far_w, mid_w, transform, gate, carried, grad, both_out, carry_out, bias_out, far_out, mid_out):
    width = transform.shape[1]
    value = grad[...]
    opened = 1.0 / (1.0 + jnp.exp(-gate[...]))
    squashed = 1.0 / (1.0 + jnp.exp(-transform[...]))
    swished = transform[...] * squashed
    slope = value * opened
    first = slope * (squashed * (1.0 + transform[...] * (1.0 - squashed)))
    second = (slope * (1.0 - opened)) * (swished - carried[...].astype(F32))
    carry_out[...] = value - slope
    both_out[:, :width] = first.astype(BF16)
    both_out[:, width:] = second.astype(BF16)

    @pl.when(pl.program_id(0) == 0)
    def _():
        bias_out[...] = jnp.zeros_like(bias_out)

    bias_out[:, :width] += jnp.sum(first.astype(BF16).astype(F32), axis=0, keepdims=True)
    bias_out[:, width:] += jnp.sum(second.astype(BF16).astype(F32), axis=0, keepdims=True)
    far_out[...] = back_product(both_out, far_w).astype(BF16)
    mid_out[...] = back_product(both_out, mid_w)


def back_product(both, weights):
    width = weights.shape[3]
    dims = (((1,), (1,)), ((), ()))
    first = lax.dot_general(both[:, :width], weights[0, 0], dims, preferred_element_type=F32)
    return first + lax.dot_general(both[:, width:], weights[0, 1], dims, preferred_element_type=F32)


def level_rest_kernel(places, near_w, own_w, both, carry, near_out, own_out):
    near_out[...] = back_product(both, near_w).astype(BF16)
    own_out[...] = back_product(both, own_w) + carry[...]


NT = (((1,), (1,)), ((), ()))
TN = (((0,), (0,)), ((), ()))


def dot(left, right, dims=(((1,), (0,)), ((), ()))):
    return lax.dot_general(left, right, dims, preferred_element_type=F32)


def local_call(kernel, arrays, shapes, scalars=None, cost=FREE):
    vm = pl.BlockSpec(memory_space=pltpu.VMEM)
    specs = [vm] * len(arrays)
    if scalars is not None:
        arrays = (scalars, *arrays)
        specs = [pl.BlockSpec(memory_space=pltpu.SMEM)] + specs
    return pl.pallas_call(
        kernel,
        in_specs=specs,
        out_specs=[vm] * len(shapes),
        out_shape=[jax.ShapeDtypeStruct(shape, kind) for shape, kind in shapes],
        compiler_params=pltpu.CompilerParams(vmem_limit_bytes=VMEM_LIMIT),
        cost_estimate=cost,
    )(*arrays)


def center_scale(total):
    center = total - jnp.mean(total, axis=-1, keepdims=True)
    return center, lax.rsqrt(jnp.mean(center * center, axis=-1, keepdims=True) + EPSILON)


def norm_kernel(pair, got, bias, base, gain, shift, total_out, hidden_out, low_out):
    total = pair[...].astype(F32) + got[...].astype(F32) + bias[...] + base[...]
    center, spread = center_scale(total)
    hidden = center * spread * gain[...] + shift[...]
    total_out[...] = total
    hidden_out[...] = hidden
    low_out[...] = hidden.astype(BF16)


def norm_back(total, gain, grad, grad_out, low_out, sums_out):
    center, spread = center_scale(total)
    normed = center * spread
    inner = grad * gain
    mean_inner = jnp.mean(inner, axis=-1, keepdims=True)
    mean_both = jnp.mean(inner * normed, axis=-1, keepdims=True)
    result = spread * (inner - mean_inner - normed * mean_both)
    low = result.astype(BF16)
    grad_out[...] = result
    low_out[...] = low
    sums_out[0:1, :] = jnp.sum(grad * normed, axis=0, keepdims=True)
    sums_out[1:2, :] = jnp.sum(grad, axis=0, keepdims=True)
    sums_out[2:3, :] = jnp.sum(low.astype(F32), axis=0, keepdims=True)


def last_norm_kernel(
    pair, got, bias, base, gain, shift, out_grad, encoded_out, grad_out, low_out, sums_out
):
    total = pair[...].astype(F32) + got[...].astype(F32) + bias[...] + base[...]
    center, spread = center_scale(total)
    encoded_out[...] = center * spread * gain[...] + shift[...]
    norm_back(total, gain[...], out_grad[...], grad_out, low_out, sums_out)


def norm_back_kernel(pair, got, base, total, gain, grad_out, low_out, sums_out):
    grad = pair[...].astype(F32) + got[...].astype(F32) + base[...]
    norm_back(total[...], gain[...], grad, grad_out, low_out, sums_out)


def project_kernel(perm, inputs, weight, own_out, send_out):
    half = own_out.shape[0]
    state = dot(perm[...], inputs[...]).astype(BF16)
    own_out[...] = state[:half]
    send_out[...] = dot(state[half:], weight[...]).astype(BF16)


def project_back_kernel(own, other, perm, weight, words_out, grad_out):
    half = own.shape[0]
    words = dot(perm[:half], own[...], TN) + dot(perm[half:], other[...], TN)
    words = words.astype(BF16)
    words_out[...] = words
    grad_out[...] = dot(words, weight[...], NT)


def head_probs(qkv, head, width, same):
    query = qkv[:, head * HEAD : (head + 1) * HEAD]
    keys = qkv[:, width + head * HEAD : width + (head + 1) * HEAD]
    scores = jnp.where(same, dot(query, keys, NT) * HEAD ** (-0.5), NEGATIVE)
    exps = jnp.exp(scores - jnp.max(scores, axis=-1, keepdims=True))
    return query, keys, exps * (1.0 / jnp.sum(exps, axis=-1, keepdims=True))


def attend_kernel(own, other, weight, biases, column, row, out_w, qkv_out, mixed_out, send_out):
    half, width = own.shape[0], out_w.shape[0]
    for rows, part in ((slice(0, half), own), (slice(half, 2 * half), other)):
        product = dot(part[...], weight[...], NT)
        qkv_out[rows, :width] = (product[:, :width] + biases[0:1, :]).astype(BF16)
        qkv_out[rows, width : 2 * width] = product[:, width : 2 * width].astype(BF16)
        qkv_out[rows, 2 * width :] = (product[:, 2 * width :] + biases[1:2, :]).astype(BF16)
    qkv = qkv_out[...]
    same = column[...] == row[...]
    for head in range(width // HEAD):
        _, _, probs = head_probs(qkv, head, width, same)
        values = qkv[:, 2 * width + head * HEAD : 2 * width + (head + 1) * HEAD]
        mixed_out[:, head * HEAD : (head + 1) * HEAD] = dot(probs.astype(BF16), values).astype(BF16)
    send_out[...] = dot(mixed_out[half:, :], out_w[...]).astype(BF16)


def attend_back_kernel(own, other, out_w, qkv_ref, column, row, weight, grad_out, sums_out, send_out):
    half, width = own.shape[0], out_w.shape[0]
    qkv = qkv_ref[...]
    same = column[...] == row[...]
    mixed = jnp.concatenate(
        [dot(part[...], out_w[...], NT).astype(BF16) for part in (own, other)], axis=0
    )
    scale = HEAD ** (-0.5)
    for head in range(width // HEAD):
        query, keys, probs = head_probs(qkv, head, width, same)
        values = qkv[:, 2 * width + head * HEAD : 2 * width + (head + 1) * HEAD]
        grads = mixed[:, head * HEAD : (head + 1) * HEAD]
        inner = dot(grads, values, NT)
        slope = probs * (inner - jnp.sum(probs * inner, axis=-1, keepdims=True))
        slope = slope.astype(BF16)
        parts = (
            dot(slope, keys) * scale,
            dot(slope, query, TN) * scale,
            dot(probs.astype(BF16), grads, TN),
        )
        for j, part in enumerate(parts):
            first = j * width + head * HEAD
            grad_out[:, first : first + HEAD] = part.astype(BF16)
    sums_out[...] = jnp.sum(grad_out[...].astype(F32), axis=0, keepdims=True)
    send_out[...] = dot(grad_out[half:, :], weight[...]).astype(BF16)


def gelu_parts(value):
    scale = 0.7978845608028654
    square = value * value
    t = jnp.tanh(scale * value * (1.0 + 0.044715 * square))
    return t, scale * (1.0 + 3 * 0.044715 * square)


def feed_kernel(own, other, up_w, up_b, down_w, upward_out, active_out, send_out):
    half = own.shape[0]
    for rows, part in ((slice(0, half), own), (slice(half, 2 * half), other)):
        upward = dot(part[...], up_w[...]) + up_b[...]
        t, _ = gelu_parts(upward)
        upward_out[rows, :] = upward
        active_out[rows, :] = (0.5 * upward * (1.0 + t)).astype(BF16)
    send_out[...] = dot(active_out[half:, :], down_w[...]).astype(BF16)


def feed_back_kernel(own, other, down_w, upward_ref, up_w, grad_out, sums_out, send_out):
    half = own.shape[0]
    total = jnp.zeros(sums_out.shape, F32)
    for rows, part in ((slice(0, half), own), (slice(half, 2 * half), other)):
        grad = dot(part[...], down_w[...], NT)
        upward = upward_ref[rows, :]
        t, inner = gelu_parts(upward)
        slope = 0.5 * (1.0 + t) + 0.5 * upward * (1.0 - t * t) * inner
        low = (grad * slope).astype(BF16)
        grad_out[rows, :] = low
        total = total + jnp.sum(low.astype(F32), axis=0, keepdims=True)
    sums_out[...] = total
    send_out[...] = dot(grad_out[half:, :], up_w[...], NT).astype(BF16)


def products_kernel(counts, spots, *refs):
    *operands, keep, send = refs
    half, rows, _ = keep.shape
    first, position = 0, 0
    for count in counts:
        lefts, right = operands[position : position + count], operands[position + count]
        position += count + 1
        width, step = right.shape[1], right.shape[0] // count
        product = sum(
            dot(left[...], right[i * step : (i + 1) * step, :], TN) for i, left in enumerate(lefts)
        )
        cols = slice(first, first + width)
        first += width
        for d in range(2 * half):
            block = product[d * rows : (d + 1) * rows].astype(BF16)

            @pl.when(spots[d] < half)
            def _():
                keep[spots[d], :, cols] = block

            @pl.when(spots[d] >= half)
            def _():
                send[spots[d] - half, :, cols] = block


def products(groups, spots):
    peers = spots.shape[0]
    total = sum(right.shape[1] for _, right in groups)
    shape = ((peers // 2, groups[0][0][0].shape[1] // peers, total), BF16)
    return local_call(
        functools.partial(products_kernel, [len(lefts) for lefts, _ in groups]),
        [item for lefts, right in groups for item in (*lefts, right)],
        [shape, shape],
        spots,
        pl.CostEstimate(flops=4 * 10**9, bytes_accessed=10**7, transcendentals=0),
    )


def join_kernel(count, *refs):
    for i in range(count):
        kept, got = refs[2 * i], refs[2 * i + 1]
        first, second = refs[2 * count + 2 * i], refs[2 * count + 2 * i + 1]
        half = first.shape[0]
        for j in range(half):
            first[j] = (kept[j].astype(F32) + got[j].astype(F32)).astype(BF16)
            second[j] = (kept[half + j].astype(F32) + got[half + j].astype(F32)).astype(BF16)


def join_blocks(*parts):
    shapes = []
    for kept, _ in parts:
        shapes += [((kept.shape[0] // 2, *kept.shape[1:]), BF16)] * 2
    joined = local_call(
        functools.partial(join_kernel, len(parts)), [item for pair in parts for item in pair], shapes
    )
    return [joined[2 * i : 2 * i + 2] for i in range(len(parts))]


def level_product_kernel(ours, *refs):
    *theirs, half, peer, keep, send = refs
    product = dot(ours[...], half[...], TN)
    first = 0
    for piece in theirs:
        product = product + dot(piece[...], peer[first : first + piece.shape[0], :], TN)
        first += piece.shape[0]
    middle = keep.shape[0]
    keep[...] = product[:middle].astype(BF16)
    send[...] = product[middle:].astype(BF16)


def level_product(ours, theirs, half, peer):
    shape = ((ours.shape[1] // 2, half.shape[1]), BF16)
    return local_call(
        level_product_kernel,
        (ours, *theirs, half, peer),
        [shape, shape],
        None,
        pl.CostEstimate(flops=4 * 10**9, bytes_accessed=10**7, transcendentals=0),
    )


def fence(*values):
    return lax.optimization_barrier(values)


def swap(values, axis, bit):
    count = lax.axis_size(axis)
    return lax.ppermute(values, axis, [(i, i ^ bit) for i in range(count)])


def peer_order(bits):
    count = 1 << len(bits)
    return [
        sum(bit for i, bit in enumerate(bits) if (p >> (len(bits) - 1 - i)) & 1) for p in range(count)
    ]


def blocks_by_peer(values, axis, order, count):
    size = values.shape[axis] // count
    me = lax.axis_index("dp")
    return [lax.dynamic_slice_in_dim(values, (me ^ r) * size, size, axis) for r in order]


def on_device(
    chars,
    char_mask,
    word_order,
    segment_ids,
    char_table,
    conv_weight,
    conv_bias,
    highway_weight,
    highway_bias,
    project_weight,
    project_bias,
    position_table,
    norm_gain,
    norm_bias,
    qkv_weight,
    qv_bias,
    out_weight,
    out_bias,
    up_weight,
    up_bias,
    down_weight,
    down_bias,
    out_grad,
):
    dp_count = lax.axis_size("dp")
    dp_index = lax.axis_index("dp")
    mp_index = lax.axis_index("mp")
    low = mp_index & 1
    word_count = chars.shape[0]
    per_peer = word_count // dp_count
    half_count = word_count // 2
    local_channels = conv_weight.shape[1]
    dp_bits = [1 << b for b in range(dp_count.bit_length() - 1)]
    order = peer_order(dp_bits)
    far_bits = dp_bits[1:] + dp_bits[:1]

    local_rows = (
        lax.dynamic_slice(
            word_order.reshape(dp_count, dp_count, per_peer),
            (0, dp_index, 0),
            (dp_count, 1, per_peer),
        ).reshape(word_count)
        - dp_index * word_count
    )
    places = local_rows ^ (low * half_count)
    perm = (jnp.arange(word_count, dtype=jnp.int32)[:, None] == places[None, :]).astype(BF16)

    def own_half(values):
        return lax.dynamic_slice_in_dim(values, low * half_count, half_count, 0)

    ids = jnp.where(char_mask > 0, chars, -1).reshape(dp_count, per_peer * CHARS)
    ids = lax.all_to_all(ids, "dp", split_axis=0, concat_axis=0, tiled=True)
    weights = jnp.swapaxes(highway_weight, 1, 2)
    ids, weights = fence(ids, weights)
    ids = ids.reshape(word_count, CHARS)

    used_taps = filter_mask(local_channels, mp_index * local_channels)
    filters = jnp.where(used_taps, conv_weight, jnp.zeros_like(conv_weight))
    counts = block_counts(ids, BLOCK)
    pooled, embedded = cnn_forward(
        ids, counts, spread_table(char_table), filters, conv_bias, BLOCK
    )

    def spots_of(bits):
        peers = dp_index ^ jnp.array(peer_order(bits), jnp.int32)
        index = jnp.arange(dp_count, dtype=jnp.int32)
        return jnp.sum(jnp.where(peers[None, :] == index[:, None], index[None, :], 0), axis=1)

    spots, far_spots = spots_of(dp_bits), spots_of(far_bits)
    places = jnp.concatenate([mp_index ^ jnp.arange(4, dtype=jnp.int32), spots])
    square = (word_count, local_channels)
    wide_f32 = jax.ShapeDtypeStruct(square, F32)
    wide_bf16 = jax.ShapeDtypeStruct(square, BF16)

    carried = inputs = pooled
    kept = []
    theirs = None
    for depth in range(LAYERS):
        a = inputs
        b = swap(a, "mp", 1)
        c = swap(a, "mp", 2)
        if depth:
            c, kept[0][4][0] = fence(c, kept[0][4][0])
        d = swap(c, "mp", 1)
        peer_shape = jax.ShapeDtypeStruct((word_count, CHANNELS // 2), BF16)
        direct = (CHANNELS // dp_count) % 128 == 0
        transform, gate, mixed_state, inputs, *peer_blocks = level_call(
            level_kernel,
            places,
            depth,
            (0, 1, 2, 3),
            weights,
            (a, b, c, d, carried, highway_bias[depth]),
            [wide_f32, wide_f32, wide_f32, wide_bf16] + [peer_shape] * (2 * direct),
        )
        if direct:
            ours, theirs = peer_blocks
        else:
            whole = jnp.zeros((word_count, CHANNELS), BF16)
            for r, piece in enumerate((a, b, c, d)):
                whole = lax.dynamic_update_slice(
                    whole, piece, (0, (mp_index ^ r) * local_channels)
                )
            blocks = blocks_by_peer(whole, 1, order, dp_count)
            ours = jnp.concatenate(blocks[: dp_count // 2], axis=1)
            theirs = jnp.concatenate(blocks[dp_count // 2 :], axis=1)
        step = -(-word_count // 48) * 16
        theirs = [
            swap(theirs[first : first + step], "dp", 1) for first in range(0, word_count, step)
        ]
        kept.append([carried, transform, gate, ours, theirs])
        carried = mixed_state

    width = project_weight.shape[1]
    half_f32, half_bf16 = ((half_count, width), F32), ((half_count, width), BF16)
    sums_shape = ((3, width), F32)

    def cross(own, matrix, sent, beside=None, dims=(((1,), (0,)), ((), ())), after=None):
        got = swap(sent, "mp", 1)
        pair, after = fence((dot(own, matrix, dims) + got.astype(F32)).astype(BF16), after)
        got, beside = fence(swap(pair, "mp", 2), beside)
        return (pair, got, beside) if after is None else (pair, got, beside, after)

    def row(vector):
        return vector.reshape(1, -1)

    def send(parts, bit):
        return parts[0], swap(parts[1], "dp", bit)

    def blocked(parts):
        shape = (dp_count // 4, CHANNELS // dp_count, local_channels)
        return [part.reshape(shape) for part in parts]

    def finish(parts, bits):
        for bit in bits:
            parts = send(join_blocks(parts)[0], bit)
        return parts[0][0].astype(F32) + parts[1][0].astype(F32)

    def blocked(parts):
        shape = (dp_count // 4, CHANNELS // dp_count, local_channels)
        return [part.reshape(shape) for part in parts]

    def finish(parts, bits):
        for bit in bits:
            parts = send(join_blocks(parts)[0], bit)
        return parts[0][0].astype(F32) + parts[1][0].astype(F32)

    spots = jnp.sum(
        jnp.where(
            (dp_index ^ jnp.array(order, jnp.int32))[None, :]
            == jnp.arange(dp_count, dtype=jnp.int32)[:, None],
            jnp.arange(dp_count, dtype=jnp.int32)[None, :],
            0,
        ),
        axis=1,
    )

    own_state, sent = local_call(
        project_kernel,
        (perm, inputs, project_weight),
        [((half_count, local_channels), BF16), half_bf16],
    )
    pair, got, kept[0][4][1] = cross(own_state, project_weight, sent, kept[0][4][1])
    embed_total, hidden_in, x_own = local_call(
        norm_kernel,
        (pair, got, row(project_bias), own_half(position_table), row(norm_gain[0]), row(norm_bias[0])),
        [half_f32, half_f32, half_bf16],
    )
    x_other = swap(x_own, "mp", 1)
    local_heads = qkv_weight.shape[2]
    qkv_flat = jnp.transpose(qkv_weight, (1, 2, 0)).reshape(3 * local_heads, width)
    segments = segment_ids[0]
    segments = jnp.where(low > 0, jnp.roll(segments, half_count), segments)
    column, line = segments.reshape(-1, 1), segments.reshape(1, -1)
    qkv_shape = ((word_count, 3 * local_heads), BF16)
    qkv, mixed, sent = local_call(
        attend_kernel,
        (x_own, x_other, qkv_flat, qv_bias, column, line, out_weight),
        [qkv_shape, ((word_count, local_heads), BF16), half_bf16],
    )
    pair, got, kept[0][4][2] = cross(mixed[:half_count], out_weight, sent, kept[0][4][2])
    resid_one, hidden_mid, mid_own = local_call(
        norm_kernel,
        (pair, got, row(out_bias), hidden_in, row(norm_gain[1]), row(norm_bias[1])),
        [half_f32, half_f32, half_bf16],
    )
    mid_other = swap(mid_own, "mp", 1)
    hidden_units = up_weight.shape[1]
    upward, activated, sent = local_call(
        feed_kernel,
        (mid_own, mid_other, up_weight, row(up_bias), down_weight),
        [((word_count, hidden_units), F32), ((word_count, hidden_units), BF16), half_bf16],
    )
    pair, got, kept[1][4][0] = cross(activated[:half_count], down_weight, sent, kept[1][4][0])
    encoded, resid_two_grad, down_own, sums_two = local_call(
        last_norm_kernel,
        (
            pair,
            got,
            row(down_bias),
            hidden_mid,
            row(norm_gain[2]),
            row(norm_bias[2]),
            own_half(out_grad),
        ),
        [half_f32, half_f32, half_bf16, sums_shape],
    )
    down_other = swap(down_own, "mp", 1)
    up_grad, up_bias_grad, sent = local_call(
        feed_back_kernel,
        (down_own, down_other, down_weight, upward, up_weight),
        [((word_count, hidden_units), BF16), ((1, hidden_units), F32), half_bf16],
    )
    pair, got, kept[1][4][1], up_later = cross(
        up_grad[:half_count], up_weight, sent, kept[1][4][1], NT, up_grad
    )
    resid_one_grad, attn_own, sums_one = local_call(
        norm_back_kernel,
        (pair, got, resid_two_grad, resid_one, row(norm_gain[1])),
        [half_f32, half_bf16, sums_shape],
    )
    first_blocks = products(
        [((mid_own, mid_other), up_later), ((down_own, down_other), activated)], far_spots
    )
    attn_own, first_blocks = fence(attn_own, first_blocks)
    first_parts = send(first_blocks, far_bits[0])
    attn_other = swap(attn_own, "mp", 1)
    qkv_grad, qkv_sums, sent = local_call(
        attend_back_kernel,
        (attn_own, attn_other, out_weight, qkv, column, line, qkv_flat),
        [qkv_shape, ((1, 3 * local_heads), F32), half_bf16],
    )
    pair, got, kept[1][4][2] = cross(qkv_grad[:half_count], qkv_flat, sent, kept[1][4][2])
    embed_grad, proj_own, sums_zero = local_call(
        norm_back_kernel,
        (pair, got, resid_one_grad, embed_total, row(norm_gain[0])),
        [half_f32, half_bf16, sums_shape],
    )
    proj_other = swap(proj_own, "mp", 1)
    proj_words, state_grad = local_call(
        project_back_kernel,
        (proj_own, proj_other, perm, project_weight),
        [((word_count, width), BF16), ((word_count, local_channels), F32)],
    )
    def level_back(depth, grad, before, beside, after):
        carried_now, transform_now, gate_now, _, _ = kept[depth]
        both_low, carry, bias_sum, far, mid = level_call(
            level_back_kernel,
            places,
            depth,
            (3, 2),
            weights,
            (transform_now, gate_now, carried_now, grad),
            [
                jax.ShapeDtypeStruct((word_count, 2 * local_channels), BF16),
                wide_f32,
                jax.ShapeDtypeStruct((1, 2 * local_channels), F32),
                wide_bf16,
                wide_f32,
            ],
        )
        got = swap(far, "mp", 1)
        pair = (mid + got.astype(F32)).astype(BF16)
        pair, later, before, after = fence(pair, both_low, before, after)
        near, own = level_call(
            level_rest_kernel, places, depth, (1, 0), weights, (later, carry), [wide_bf16, wide_f32], True
        )
        halves = [both_low[:, :local_channels], both_low[:, local_channels:]]
        peers = [swap(half, "dp", 1) for half in halves]
        crossing, peers[0], beside = fence(swap(pair, "mp", 2), peers[0], beside)
        below = own + swap(near, "mp", 1).astype(F32) + crossing.astype(F32)
        return below, bias_sum.reshape(2, local_channels), halves, peers, before, beside, after

    def level_part(depth, half, peer):
        return level_product(kept[depth][3], kept[depth][4], half, peer)

    def exchange(values, bit):
        sent = fence(values.astype(BF16))[0]
        return sent, swap(sent, "dp", bit)

    def combine(parts):
        return parts[0].astype(F32) + parts[1].astype(F32)

    def complete(parts, bits):
        for bit in bits:
            parts = exchange(combine(parts), bit)
        return combine(parts)

    def rows_of(values, rows):
        values = values.reshape(-1, values.shape[-1])
        return jnp.pad(values, ((0, rows - values.shape[0]), (0, width - values.shape[1])))

    row_pack = jnp.concatenate([sums_zero, sums_one, sums_two], axis=0)
    row_pack = row_pack + swap(row_pack, "mp", 1)
    quarter = half_count // 2
    high = (mp_index >> 1) & 1
    position_part = lax.dynamic_slice_in_dim(embed_grad, high * quarter, quarter, 0)
    small_rows = -(-(row_pack.shape[0] + 2) // 16) * 16
    small_pack = jnp.concatenate(
        [row_pack, rows_of(up_bias_grad, 1), rows_of(qkv_sums, small_rows - row_pack.shape[0] - 1)],
        axis=0,
    )

    early = jnp.concatenate([position_part, small_pack], axis=0).astype(BF16)
    early = exchange(early, dp_bits[0])
    state_grad, bias_one, halves_one, peers_one, _, beside, words_later = level_back(
        1, state_grad, None, (first_parts, early), proj_words
    )
    first_parts, early = beside
    first_parts = send(join_blocks(first_parts)[0], far_bits[1])
    second_blocks = products(
        [((x_own, x_other), qkv_grad), ((attn_own, attn_other), mixed), ((words_later,), inputs)],
        spots,
    )
    state_grad, second_blocks = fence(state_grad, second_blocks)
    first_one = send(blocked(level_part(1, halves_one[0], peers_one[0])), dp_bits[1])
    state_grad, bias_zero, halves_zero, peers_zero, _, beside, later = level_back(
        0, state_grad, None, (peers_one[1], first_parts), halves_one[1]
    )
    peers_one[1], first_parts = beside
    first_parts = join_blocks(first_parts)[0]
    second_one = level_part(1, later, peers_one[1])
    state_grad, second_one = fence(state_grad, second_one)
    first_zero = level_part(0, halves_zero[0], peers_zero[0])
    pooled_grad, first_zero, first_one, first_parts, second_blocks = fence(
        state_grad.astype(BF16), first_zero, first_one, first_parts, second_blocks
    )
    first_one = send(join_blocks(first_one)[0], dp_bits[2])
    second_parts = send(second_blocks, dp_bits[0])
    second_one = send(blocked(second_one), dp_bits[1])
    first_zero = send(blocked(first_zero), dp_bits[1])

    middle = local_channels // 2
    lower, upper = slice(0, middle), slice(middle, local_channels)
    cnn_out = cnn_backward(
        counts, embedded, filters[:, lower], conv_bias[lower], pooled_grad[:, lower], None, BLOCK
    )
    (conv_low, bias_low, embed_part), first_one, second_one, first_zero, peers_zero[1], second_parts = fence(
        cnn_out, first_one, second_one, first_zero, peers_zero[1], second_parts
    )
    second_zero = level_part(0, halves_zero[1], peers_zero[1])
    second_one, first_zero, second_parts = join_blocks(second_one, first_zero, second_parts)
    embed_part, second_one, first_zero, second_zero, second_parts, early = fence(
        embed_part, second_one, first_zero, second_zero, second_parts, combine(early)
    )
    second_zero = send(blocked(second_zero), dp_bits[1])
    second_one = send(second_one, dp_bits[2])
    first_zero = send(first_zero, dp_bits[2])
    second_parts = send(second_parts, dp_bits[1])
    early = exchange(early, dp_bits[1])
    cnn_out = cnn_backward(
        counts, embedded, filters[:, upper], conv_bias[upper], pooled_grad[:, upper], embed_part, BLOCK
    )
    (conv_high, bias_high, embed_part), second_one, first_zero, second_zero, early, first_parts = fence(
        cnn_out, second_one, first_zero, second_zero, early, first_parts
    )
    second_zero = send(join_blocks(second_zero)[0], dp_bits[2])
    early = exchange(combine(early), dp_bits[2])
    first_sum = finish(send(first_parts, far_bits[2]), far_bits[3:])
    conv_sum = jnp.concatenate([conv_low, conv_high], axis=1)
    conv_pack = jnp.concatenate(
        [
            jnp.where(used_taps, conv_sum, jnp.zeros_like(conv_sum)),
            jnp.concatenate([bias_low, bias_high], axis=1),
            bias_zero,
            bias_one,
        ],
        axis=0,
    )
    conv_rows = conv_sum.shape[0]
    conv_pack = jnp.pad(conv_pack, ((0, -conv_pack.shape[0] % 16), (0, 0)))
    conv_parts = exchange(conv_pack, dp_bits[0])
    table_sum = table_gradient(ids.T, embed_part, char_table.shape[0])
    table_sum, conv_parts, second_parts = fence(table_sum, conv_parts, second_parts)
    second_parts = send(join_blocks(second_parts)[0], dp_bits[2])
    conv_parts = exchange(combine(conv_parts), dp_bits[1])
    table_total = table_sum
    table_total = table_total + swap(table_total, "mp", 1)
    table_total = table_total + swap(table_total, "mp", 2)
    table_total, conv_parts = fence(table_total, conv_parts)
    conv_parts = exchange(combine(conv_parts), dp_bits[2])
    for bit in dp_bits:
        table_total = table_total + swap(table_total, "dp", bit)
    table_total = table_total.reshape(-1, STEPS, CHAR_DIM)
    table_total = jnp.swapaxes(table_total, 0, 1).reshape(-1, CHAR_DIM)[: char_table.shape[0]]
    conv_pack = complete(conv_parts, dp_bits[3:])
    conv_sums = (
        conv_pack[:conv_rows],
        conv_pack[conv_rows],
        conv_pack[conv_rows + 1 : conv_rows + 5].reshape(LAYERS, 2, local_channels),
    )
    second_sum = finish(second_parts, dp_bits[3:])
    level_sums = [
        jnp.stack([finish(parts, dp_bits[3:]) for parts in level], axis=1)
        for level in ((first_zero, second_zero), (first_one, second_one))
    ]
    highway_weight_grad = jnp.stack(level_sums, axis=0)
    early = complete(early, dp_bits[3:])
    position_part, small_pack = early[:quarter], early[quarter:]
    rows = row_pack.shape[0]
    sums_zero, sums_one, sums_two = (small_pack[3 * i : 3 * i + 3] for i in range(3))
    up_bias_grad = small_pack[rows : rows + 1]
    qkv_sums = small_pack[rows + 1 : rows + 2, : 3 * local_heads]
    qv_bias_grad = jnp.stack(
        [qkv_sums[0, :local_heads], qkv_sums[0, 2 * local_heads :]], axis=0
    )
    position_part = fence(position_part.astype(BF16))[0]
    position_other = swap(position_part, "mp", 2)
    position_half = jnp.concatenate(
        [
            jnp.where(high > 0, position_other, position_part),
            jnp.where(high > 0, position_part, position_other),
        ],
        axis=0,
    )

    def both_halves(values):
        return jnp.concatenate([values, swap(values, "mp", 1)], axis=0)

    position_grad = both_halves(position_half).astype(F32)

    def in_order(values):
        first, second = values[:half_count], values[half_count:]
        return jnp.concatenate(
            [jnp.where(low > 0, second, first), jnp.where(low > 0, first, second)], axis=0
        )

    def split(total, widths):
        parts, first = [], 0
        for width in widths:
            parts.append(total[:, first : first + width])
            first += width
        return parts

    up_sum, down_sum = split(first_sum, (up_weight.shape[1], down_weight.shape[0]))
    qkv_sum, out_sum, project_sum = split(
        second_sum, (3 * local_heads, local_heads, local_channels)
    )
    return (
        in_order(both_halves(encoded)),
        table_total,
        conv_sums[0],
        conv_sums[1],
        highway_weight_grad,
        conv_sums[2],
        project_sum.T,
        sums_zero[2],
        in_order(position_grad),
        jnp.stack([sums_zero[0], sums_one[0], sums_two[0]], axis=0),
        jnp.stack([sums_zero[1], sums_one[1], sums_two[1]], axis=0),
        qkv_sum.reshape(-1, 3, local_heads),
        qv_bias_grad,
        out_sum.T,
        sums_one[2],
        up_sum,
        up_bias_grad[0],
        down_sum.T,
        sums_two[2],
    )


def solution(mesh):
    return jax.shard_map(
        on_device,
        mesh=mesh,
        in_specs=(
            P("dp", None),
            P("dp", None),
            P(),
            P("dp", None),
            P(),
            P(None, "mp"),
            P("mp"),
            P(None, None, None, "mp"),
            P(None, None, "mp"),
            P("mp", None),
            P(),
            P(),
            P(),
            P(),
            P(None, None, "mp"),
            P(None, "mp"),
            P("mp", None),
            P(),
            P(None, "mp"),
            P("mp"),
            P("mp", None),
            P(),
            P("dp", None),
        ),
        out_specs=(
            P("dp", None),
            P(),
            P(None, "mp"),
            P("mp"),
            P(None, "dp", None, "mp"),
            P(None, None, "mp"),
            P("mp", "dp"),
            P(),
            P(),
            P(),
            P(),
            P("dp", None, "mp"),
            P(None, "mp"),
            P("mp", "dp"),
            P(),
            P("dp", "mp"),
            P("mp"),
            P("mp", "dp"),
            P(),
        ),
        check_vma=False,
    )
```

```python
import functools

import jax
import jax.numpy as jnp
from jax import lax
from jax.experimental import pallas as pl
from jax.experimental.pallas import tpu as pltpu
from jax.sharding import PartitionSpec as P

HEAD = 64
CHANNELS = 2048
CHAR_DIM = 16
CHARS = 50
TAPS = 7
LAYERS = 2
BLOCK = 128
TILES = 1

EPSILON = 1e-05
NEGATIVE = -1e30
F32 = jnp.float32
BF16 = jnp.bfloat16


def filter_mask(local_count, first):
    channel = first + jnp.arange(local_count, dtype=jnp.int32)
    tap_count = 1 + sum(
        ((channel >= CHANNELS // divisor).astype(jnp.int32) for divisor in (64, 32, 16, 8, 4, 2))
    )
    tap_index = jnp.arange(TAPS * CHAR_DIM, dtype=jnp.int32) // CHAR_DIM
    return tap_index[:, None] < tap_count[None, :]


STEPS = 8
ROWS = 7
SPAN = STEPS * CHAR_DIM
VMEM_LIMIT = 24 << 20
FREE = pl.CostEstimate(flops=1, bytes_accessed=1, transcendentals=0)

def spread_table(char_table):
    low = char_table.astype(BF16)
    eye = jnp.eye(STEPS, dtype=BF16)
    first = low[:256]
    rest = jnp.pad(low[256:], ((0, CHAR_DIM - (low.shape[0] - 256)), (0, 0)))
    parts = [(eye[:, None, :, None] * part[None, :, None, :]).reshape(-1, SPAN) for part in (first, rest)]
    return jnp.concatenate(parts, axis=0)

def place_filters(filters_ref, shifted):
    shifted[...] = jnp.zeros_like(shifted)
    taps = filters_ref.shape[0]
    width = filters_ref.shape[1]
    halved = (filters_ref[...].astype(F32) * 0.5).astype(BF16)
    for r in range(STEPS):
        shifted[CHAR_DIM * r : CHAR_DIM * r + taps, r * width : (r + 1) * width] = halved

def forward_kernel(block, counts, ids_ref, table_ref, filters_ref, bias_ref, pooled_ref, embed_ref, shifted, hot, total):
    words, width = pooled_ref.shape
    place_filters(filters_ref, shifted)
    lanes = lax.broadcasted_iota(jnp.int32, (words, 256), 1)
    lane = lax.broadcasted_iota(jnp.int32, (words, 128), 1)
    embed_ref[ROWS] = jnp.zeros_like(embed_ref[ROWS])
    total[...] = jnp.zeros_like(total)

    def embed(q, carry):
        left = jnp.zeros((words, 128), F32)
        for r in range(STEPS):
            ids = ids_ref[q, :, r : r + 1]
            hot[:, r * 256 : (r + 1) * 256] = jnp.where(ids == lanes, 1.0, 0.0).astype(BF16)
            mark = jnp.where(lane // CHAR_DIM == r, lane % CHAR_DIM + 256, -7)
            left = jnp.where(ids == mark, 1.0, left)
        hot[:, STEPS * 256 :] = left.astype(BF16)
        embed_ref[q] = jnp.dot(hot[...], table_ref[...], preferred_element_type=F32).astype(BF16)
        return carry

    lax.fori_loop(0, ROWS, embed, 0)
    half = bias_ref[...] * 0.5
    blocks = words // block

    def row(q, carry):
        def one(i, inner):
            rows = pl.ds(pl.multiple_of(i * block, block), block)
            x = jnp.concatenate([embed_ref[q, rows, :], embed_ref[q + 1, rows, :]], axis=1)
            for r in range(STEPS):
                u = jnp.dot(x, shifted[:, r * width : (r + 1) * width], preferred_element_type=F32) + half
                total[rows, :] += u + u * jnp.tanh(u)
            return inner

        lax.fori_loop(counts[blocks + q], blocks, one, 0)
        return carry

    lax.fori_loop(0, ROWS, row, 0)
    rest = half + half * jnp.tanh(half)
    for i in range(blocks):
        rows = slice(i * block, (i + 1) * block)
        seen = STEPS * counts[i]
        pooled_ref[rows, :] = (
            (total[rows, :] + (CHARS - seen).astype(F32) * rest) * (1.0 / CHARS)
        ).astype(BF16)


def block_counts(ids, block):
    most = jnp.max(jnp.sum((ids >= 0).astype(jnp.int32), axis=1).reshape(-1, block), axis=1)
    need = (most + STEPS - 1) // STEPS
    first = jnp.sum((need[None, :] <= jnp.arange(ROWS, dtype=jnp.int32)[:, None]).astype(jnp.int32), axis=1)
    return jnp.concatenate([need, first])

def cnn_forward(ids, counts, table, filters, bias, block):
    words = ids.shape[0]
    width = filters.shape[1]
    ids = jnp.pad(ids, ((0, 0), (0, ROWS * STEPS - CHARS)), constant_values=-1)
    ids = jnp.swapaxes(ids.reshape(words, ROWS, STEPS), 0, 1)
    vm = pl.BlockSpec(memory_space=pltpu.VMEM)
    return pl.pallas_call(
        functools.partial(forward_kernel, block),
        in_specs=[pl.BlockSpec(memory_space=pltpu.SMEM), vm, vm, vm, vm],
        out_specs=[vm, vm],
        out_shape=[jax.ShapeDtypeStruct((words, width), BF16), jax.ShapeDtypeStruct((ROWS + 1, words, SPAN), BF16)],
        scratch_shapes=[pltpu.VMEM((2 * SPAN, STEPS * width), BF16), pltpu.VMEM((words, STEPS * 256 + 128), BF16), pltpu.VMEM((words, width), F32)],
        compiler_params=pltpu.CompilerParams(vmem_limit_bytes=VMEM_LIMIT),
        cost_estimate=FREE,
    )(counts, ids, table, filters, bias.reshape(1, -1))


def backward_kernel(
    block,
    counts,
    embed_ref,
    filters_ref,
    bias_ref,
    grad_ref,
    embed_in,
    filter_out,
    bias_out,
    embed_grad,
    shifted,
    slopes,
    sums,
):
    words, width = grad_ref.shape
    blocks = words // block
    place_filters(filters_ref, shifted)
    half = bias_ref[...] * 0.5
    still = jnp.tanh(half)
    rest = (1.0 + still) + half * (1.0 - still * still)
    bias_out[...] = jnp.zeros_like(bias_out)
    sums[...] = jnp.zeros_like(sums)
    if embed_in is None:
        embed_grad[...] = jnp.zeros_like(embed_grad)
    else:
        embed_grad[...] = embed_in[...]
    scale = 0.5 / CHARS
    for i in range(blocks):
        grads = grad_ref[i * block : (i + 1) * block, :].astype(F32) * scale
        left = (CHARS - STEPS * counts[i]).astype(F32)
        bias_out[...] += jnp.sum(grads, axis=0, keepdims=True) * (rest * left)
    def row(q, outer):
        first = counts[blocks + q]

        def clear(i, carry):
            rows = pl.ds(pl.multiple_of(i * block, block), block)
            slopes[rows, :] = jnp.zeros((block, STEPS * width), BF16)
            return carry

        lax.fori_loop(counts[blocks + jnp.maximum(q - 1, 0)], first, clear, 0)

        def one(i, carry):
            rows = pl.ds(pl.multiple_of(i * block, block), block)
            x = jnp.concatenate([embed_ref[q, rows, :], embed_ref[q + 1, rows, :]], axis=1)
            grads = grad_ref[rows, :].astype(F32) * scale
            column = jnp.zeros((1, width), F32)
            for r in range(STEPS):
                cols = slice(r * width, (r + 1) * width)
                u = jnp.dot(x, shifted[:, cols], preferred_element_type=F32) + half
                t = jnp.tanh(u)
                slope = grads * ((1.0 + t) + u * (1.0 - t * t))
                column += jnp.sum(slope, axis=0, keepdims=True)
                slopes[rows, cols] = slope.astype(BF16)
            bias_out[...] += column
            return carry

        lax.fori_loop(first, blocks, one, 0)

        def spread(start):
            rows = slice(start, words)
            x = jnp.concatenate([embed_ref[q, rows, :], embed_ref[q + 1, rows, :]], axis=1)
            back = lax.dot_general(
                slopes[rows, :], shifted[...], (((1,), (1,)), ((), ())), preferred_element_type=F32
            )
            embed_grad[q, rows, :] += back[:, :SPAN]
            embed_grad[q + 1, rows, :] += back[:, SPAN:]
            for r in range(STEPS):
                cols = slice(r * width, (r + 1) * width)
                sums[:, cols] += lax.dot_general(
                    x, slopes[rows, cols], (((0,), (0,)), ((), ())), preferred_element_type=F32
                )

        middle = blocks // 2

        @pl.when(first < middle)
        def _():
            spread(0)

        @pl.when((first >= middle) & (first < blocks))
        def _():
            spread(middle * block)

        return outer

    lax.fori_loop(0, ROWS, row, 0)
    taps = filters_ref.shape[0]
    total = sums[:taps, :width]
    for r in range(1, STEPS):
        lower = CHAR_DIM * r
        total = total + sums[lower : lower + taps, r * width : (r + 1) * width]
    filter_out[...] = total


def cnn_backward(counts, embed, filters, bias, grad, embed_grad, block):
    words, width = grad.shape
    taps = filters.shape[0]
    vm = pl.BlockSpec(memory_space=pltpu.VMEM)
    operands = [counts, embed, filters, bias.reshape(1, -1), grad]
    kernel = functools.partial(backward_kernel, block)
    if embed_grad is None:
        inner = kernel

        def kernel(counts, embed, filters, bias, grad, *rest):
            inner(counts, embed, filters, bias, grad, None, *rest)
    else:
        operands.append(embed_grad)
    return pl.pallas_call(
        kernel,
        in_specs=[pl.BlockSpec(memory_space=pltpu.SMEM)] + [vm] * (len(operands) - 1),
        out_specs=[vm] * 3,
        out_shape=[
            jax.ShapeDtypeStruct((taps, width), F32),
            jax.ShapeDtypeStruct((1, width), F32),
            jax.ShapeDtypeStruct((ROWS + 1, words, SPAN), F32),
        ],
        scratch_shapes=[
            pltpu.VMEM((2 * SPAN, STEPS * width), BF16),
            pltpu.VMEM((words, STEPS * width), BF16),
            pltpu.VMEM((2 * SPAN, STEPS * width), F32),
        ],
        compiler_params=pltpu.CompilerParams(vmem_limit_bytes=VMEM_LIMIT),
        cost_estimate=FREE,
    )(*operands)


def table_kernel(ids_ref, embed_grad, table_out, hot):
    vocab, words = hot.shape[0], ids_ref.shape[1]
    high = embed_grad[:ROWS].reshape(ROWS * words, SPAN) * 2.0
    low = high.astype(BF16)
    pair = jnp.concatenate([low, (high - low.astype(F32)).astype(BF16)], axis=1)
    which = lax.broadcasted_iota(jnp.int32, (vocab, words), 0)
    lane = lax.broadcasted_iota(jnp.int32, (vocab, SPAN), 1) // CHAR_DIM
    table = jnp.zeros((vocab, SPAN), F32)
    for r in range(STEPS):
        for q in range(ROWS):
            j = q * STEPS + r
            cols = slice(q * words, (q + 1) * words)
            if j < CHARS:
                hot[:, cols] = jnp.where(ids_ref[j : j + 1, :] == which, 1.0, 0.0).astype(BF16)
            else:
                hot[:, cols] = jnp.zeros((vocab, words), BF16)
        both = jnp.dot(hot[...], pair, preferred_element_type=F32)
        table = jnp.where(lane == r, both[:, :SPAN] + both[:, SPAN:], table)
    step = table_out.shape[0]
    for shift in (64, 32, 16):
        table = table + pltpu.roll(table, shift, 1)
    table_out[...] = jnp.zeros_like(table_out)
    for g in range(-(-vocab // step)):
        rows = min(step, vocab - g * step)
        cols = slice(g * CHAR_DIM, (g + 1) * CHAR_DIM)
        table_out[:rows, cols] = table[g * step : g * step + rows, cols]


def table_gradient(ids_columns, embed_grad, vocab):
    words = ids_columns.shape[1]
    rows = -(-vocab // 16) * 16
    vm = pl.BlockSpec(memory_space=pltpu.VMEM)
    return pl.pallas_call(
        table_kernel,
        in_specs=[vm, vm],
        out_specs=vm,
        out_shape=jax.ShapeDtypeStruct((-(-vocab // 64) * 8, SPAN), F32),
        scratch_shapes=[pltpu.VMEM((rows, ROWS * words), BF16)],
        compiler_params=pltpu.CompilerParams(vmem_limit_bytes=VMEM_LIMIT),
        cost_estimate=FREE,
    )(ids_columns, embed_grad)


def level_call(kernel, places, level, picks, weights, arrays, shapes, hidden=False):
    width = weights.shape[3]
    rows = arrays[0].shape[0]
    tile = rows // TILES
    weights = pltpu.with_memory_space_constraint(weights, pltpu.HBM)

    def picked(pick):
        return pl.BlockSpec((1, 2, width, width), lambda i, spots: (level, 0, spots[pick], 0))

    def tiled(shape):
        if shape[0] == rows:
            return pl.BlockSpec((tile, shape[1]), lambda i, spots: (i, 0))
        return pl.BlockSpec(shape, lambda i, spots: (0, 0))

    cost = FREE
    if hidden:
        cost = pl.CostEstimate(
            flops=8 * rows * width * width, bytes_accessed=16 * rows * width, transcendentals=0
        )
    return pl.pallas_call(
        kernel,
        grid_spec=pltpu.PrefetchScalarGridSpec(
            num_scalar_prefetch=1,
            grid=(TILES,),
            in_specs=[picked(pick) for pick in picks] + [tiled(item.shape) for item in arrays],
            out_specs=[tiled(item.shape) for item in shapes],
        ),
        out_shape=shapes,
        compiler_params=pltpu.CompilerParams(vmem_limit_bytes=VMEM_LIMIT),
        cost_estimate=cost,
    )(places, *[weights] * len(picks), *arrays)


def level_kernel(
    places, own_w, near_w, mid_w, far_w, own, near, mid, far, carried, bias,
    transform_out, gate_out, carried_out, low_out, *peers_out,
):
    if peers_out:
        ours, theirs = peers_out
        size = own.shape[1] * 4 // (places.shape[0] - 4)
        count = own.shape[1] // size
        for r, piece in enumerate((own, near, mid, far)):
            for h in range(count):
                spot = places[4 + places[r] * count + h]
                half = (places.shape[0] - 4) // 2
                block = piece[:, h * size : (h + 1) * size]

                @pl.when(spot < half)
                def _():
                    ours[:, pl.ds(pl.multiple_of(spot * size, size), size)] = block

                @pl.when(spot >= half)
                def _():
                    theirs[:, pl.ds(pl.multiple_of((spot - half) * size, size), size)] = block

    parts = []
    for j in range(2):
        total = dot(own[...], own_w[0, j]) + dot(near[...], near_w[0, j])
        total = total + dot(mid[...], mid_w[0, j]) + dot(far[...], far_w[0, j])
        parts.append(total + bias[j : j + 1, :])
    transform, gate = parts
    transform_out[...] = transform
    gate_out[...] = gate
    opened = 1.0 / (1.0 + jnp.exp(-gate))
    swished = transform / (1.0 + jnp.exp(-transform))
    mixed = opened * swished + (1.0 - opened) * carried[...].astype(F32)
    carried_out[...] = mixed
    low_out[...] = mixed.astype(BF16)


def level_back_kernel(places, far_w, mid_w, transform, gate, carried, grad, both_out, carry_out, bias_out, far_out, mid_out):
    width = transform.shape[1]
    value = grad[...]
    opened = 1.0 / (1.0 + jnp.exp(-gate[...]))
    squashed = 1.0 / (1.0 + jnp.exp(-transform[...]))
    swished = transform[...] * squashed
    slope = value * opened
    first = slope * (squashed * (1.0 + transform[...] * (1.0 - squashed)))
    second = (slope * (1.0 - opened)) * (swished - carried[...].astype(F32))
    carry_out[...] = value - slope
    both_out[:, :width] = first.astype(BF16)
    both_out[:, width:] = second.astype(BF16)

    @pl.when(pl.program_id(0) == 0)
    def _():
        bias_out[...] = jnp.zeros_like(bias_out)

    bias_out[:, :width] += jnp.sum(first.astype(BF16).astype(F32), axis=0, keepdims=True)
    bias_out[:, width:] += jnp.sum(second.astype(BF16).astype(F32), axis=0, keepdims=True)
    far_out[...] = back_product(both_out, far_w).astype(BF16)
    mid_out[...] = back_product(both_out, mid_w)


def back_product(both, weights):
    width = weights.shape[3]
    dims = (((1,), (1,)), ((), ()))
    first = lax.dot_general(both[:, :width], weights[0, 0], dims, preferred_element_type=F32)
    return first + lax.dot_general(both[:, width:], weights[0, 1], dims, preferred_element_type=F32)


def level_rest_kernel(places, near_w, own_w, both, carry, near_out, own_out):
    near_out[...] = back_product(both, near_w).astype(BF16)
    own_out[...] = back_product(both, own_w) + carry[...]


NT = (((1,), (1,)), ((), ()))
TN = (((0,), (0,)), ((), ()))


def dot(left, right, dims=(((1,), (0,)), ((), ()))):
    return lax.dot_general(left, right, dims, preferred_element_type=F32)


def local_call(kernel, arrays, shapes, scalars=None, cost=FREE):
    vm = pl.BlockSpec(memory_space=pltpu.VMEM)
    specs = [vm] * len(arrays)
    if scalars is not None:
        arrays = (scalars, *arrays)
        specs = [pl.BlockSpec(memory_space=pltpu.SMEM)] + specs
    return pl.pallas_call(
        kernel,
        in_specs=specs,
        out_specs=[vm] * len(shapes),
        out_shape=[jax.ShapeDtypeStruct(shape, kind) for shape, kind in shapes],
        compiler_params=pltpu.CompilerParams(vmem_limit_bytes=VMEM_LIMIT),
        cost_estimate=cost,
    )(*arrays)


def center_scale(total):
    center = total - jnp.mean(total, axis=-1, keepdims=True)
    return center, lax.rsqrt(jnp.mean(center * center, axis=-1, keepdims=True) + EPSILON)


def norm_kernel(pair, got, bias, base, gain, shift, total_out, hidden_out, low_out):
    total = pair[...].astype(F32) + got[...].astype(F32) + bias[...] + base[...]
    center, spread = center_scale(total)
    hidden = center * spread * gain[...] + shift[...]
    total_out[...] = total
    hidden_out[...] = hidden
    low_out[...] = hidden.astype(BF16)


def norm_back(total, gain, grad, grad_out, low_out, sums_out):
    center, spread = center_scale(total)
    normed = center * spread
    inner = grad * gain
    mean_inner = jnp.mean(inner, axis=-1, keepdims=True)
    mean_both = jnp.mean(inner * normed, axis=-1, keepdims=True)
    result = spread * (inner - mean_inner - normed * mean_both)
    low = result.astype(BF16)
    grad_out[...] = result
    low_out[...] = low
    sums_out[0:1, :] = jnp.sum(grad * normed, axis=0, keepdims=True)
    sums_out[1:2, :] = jnp.sum(grad, axis=0, keepdims=True)
    sums_out[2:3, :] = jnp.sum(low.astype(F32), axis=0, keepdims=True)


def last_norm_kernel(
    pair, got, bias, base, gain, shift, out_grad, encoded_out, grad_out, low_out, sums_out
):
    total = pair[...].astype(F32) + got[...].astype(F32) + bias[...] + base[...]
    center, spread = center_scale(total)
    encoded_out[...] = center * spread * gain[...] + shift[...]
    norm_back(total, gain[...], out_grad[...], grad_out, low_out, sums_out)


def norm_back_kernel(pair, got, base, total, gain, grad_out, low_out, sums_out):
    grad = pair[...].astype(F32) + got[...].astype(F32) + base[...]
    norm_back(total[...], gain[...], grad, grad_out, low_out, sums_out)


def project_kernel(perm, inputs, weight, own_out, send_out):
    half = own_out.shape[0]
    state = dot(perm[...], inputs[...]).astype(BF16)
    own_out[...] = state[:half]
    send_out[...] = dot(state[half:], weight[...]).astype(BF16)


def project_back_kernel(own, other, perm, weight, words_out, grad_out):
    half = own.shape[0]
    words = dot(perm[:half], own[...], TN) + dot(perm[half:], other[...], TN)
    words = words.astype(BF16)
    words_out[...] = words
    grad_out[...] = dot(words, weight[...], NT)


def head_probs(qkv, head, width, same):
    query = qkv[:, head * HEAD : (head + 1) * HEAD]
    keys = qkv[:, width + head * HEAD : width + (head + 1) * HEAD]
    scores = jnp.where(same, dot(query, keys, NT) * HEAD ** (-0.5), NEGATIVE)
    exps = jnp.exp(scores - jnp.max(scores, axis=-1, keepdims=True))
    return query, keys, exps * (1.0 / jnp.sum(exps, axis=-1, keepdims=True))


def attend_kernel(own, other, weight, biases, column, row, out_w, qkv_out, mixed_out, send_out):
    half, width = own.shape[0], out_w.shape[0]
    for rows, part in ((slice(0, half), own), (slice(half, 2 * half), other)):
        product = dot(part[...], weight[...], NT)
        qkv_out[rows, :width] = (product[:, :width] + biases[0:1, :]).astype(BF16)
        qkv_out[rows, width : 2 * width] = product[:, width : 2 * width].astype(BF16)
        qkv_out[rows, 2 * width :] = (product[:, 2 * width :] + biases[1:2, :]).astype(BF16)
    qkv = qkv_out[...]
    same = column[...] == row[...]
    for head in range(width // HEAD):
        _, _, probs = head_probs(qkv, head, width, same)
        values = qkv[:, 2 * width + head * HEAD : 2 * width + (head + 1) * HEAD]
        mixed_out[:, head * HEAD : (head + 1) * HEAD] = dot(probs.astype(BF16), values).astype(BF16)
    send_out[...] = dot(mixed_out[half:, :], out_w[...]).astype(BF16)


def attend_back_kernel(own, other, out_w, qkv_ref, column, row, weight, grad_out, sums_out, send_out):
    half, width = own.shape[0], out_w.shape[0]
    qkv = qkv_ref[...]
    same = column[...] == row[...]
    mixed = jnp.concatenate(
        [dot(part[...], out_w[...], NT).astype(BF16) for part in (own, other)], axis=0
    )
    scale = HEAD ** (-0.5)
    for head in range(width // HEAD):
        query, keys, probs = head_probs(qkv, head, width, same)
        values = qkv[:, 2 * width + head * HEAD : 2 * width + (head + 1) * HEAD]
        grads = mixed[:, head * HEAD : (head + 1) * HEAD]
        inner = dot(grads, values, NT)
        slope = probs * (inner - jnp.sum(probs * inner, axis=-1, keepdims=True))
        slope = slope.astype(BF16)
        parts = (
            dot(slope, keys) * scale,
            dot(slope, query, TN) * scale,
            dot(probs.astype(BF16), grads, TN),
        )
        for j, part in enumerate(parts):
            first = j * width + head * HEAD
            grad_out[:, first : first + HEAD] = part.astype(BF16)
    sums_out[...] = jnp.sum(grad_out[...].astype(F32), axis=0, keepdims=True)
    send_out[...] = dot(grad_out[half:, :], weight[...]).astype(BF16)


def gelu_parts(value):
    scale = 0.7978845608028654
    square = value * value
    t = jnp.tanh(scale * value * (1.0 + 0.044715 * square))
    return t, scale * (1.0 + 3 * 0.044715 * square)


def feed_kernel(own, other, up_w, up_b, down_w, upward_out, active_out, send_out):
    half = own.shape[0]
    for rows, part in ((slice(0, half), own), (slice(half, 2 * half), other)):
        upward = dot(part[...], up_w[...]) + up_b[...]
        t, _ = gelu_parts(upward)
        upward_out[rows, :] = upward
        active_out[rows, :] = (0.5 * upward * (1.0 + t)).astype(BF16)
    send_out[...] = dot(active_out[half:, :], down_w[...]).astype(BF16)


def feed_back_kernel(own, other, down_w, upward_ref, up_w, grad_out, sums_out, send_out):
    half = own.shape[0]
    total = jnp.zeros(sums_out.shape, F32)
    for rows, part in ((slice(0, half), own), (slice(half, 2 * half), other)):
        grad = dot(part[...], down_w[...], NT)
        upward = upward_ref[rows, :]
        t, inner = gelu_parts(upward)
        slope = 0.5 * (1.0 + t) + 0.5 * upward * (1.0 - t * t) * inner
        low = (grad * slope).astype(BF16)
        grad_out[rows, :] = low
        total = total + jnp.sum(low.astype(F32), axis=0, keepdims=True)
    sums_out[...] = total
    send_out[...] = dot(grad_out[half:, :], up_w[...], NT).astype(BF16)


def products_kernel(counts, spots, *refs):
    *operands, keep, send = refs
    half, rows, _ = keep.shape
    first, position = 0, 0
    for count in counts:
        lefts, right = operands[position : position + count], operands[position + count]
        position += count + 1
        width, step = right.shape[1], right.shape[0] // count
        product = sum(
            dot(left[...], right[i * step : (i + 1) * step, :], TN) for i, left in enumerate(lefts)
        )
        cols = slice(first, first + width)
        first += width
        for d in range(2 * half):
            block = product[d * rows : (d + 1) * rows].astype(BF16)

            @pl.when(spots[d] < half)
            def _():
                keep[spots[d], :, cols] = block

            @pl.when(spots[d] >= half)
            def _():
                send[spots[d] - half, :, cols] = block


def products(groups, spots):
    peers = spots.shape[0]
    total = sum(right.shape[1] for _, right in groups)
    shape = ((peers // 2, groups[0][0][0].shape[1] // peers, total), BF16)
    return local_call(
        functools.partial(products_kernel, [len(lefts) for lefts, _ in groups]),
        [item for lefts, right in groups for item in (*lefts, right)],
        [shape, shape],
        spots,
        pl.CostEstimate(flops=4 * 10**9, bytes_accessed=10**7, transcendentals=0),
    )


def join_kernel(count, *refs):
    for i in range(count):
        kept, got = refs[2 * i], refs[2 * i + 1]
        first, second = refs[2 * count + 2 * i], refs[2 * count + 2 * i + 1]
        half = first.shape[0]
        for j in range(half):
            first[j] = (kept[j].astype(F32) + got[j].astype(F32)).astype(BF16)
            second[j] = (kept[half + j].astype(F32) + got[half + j].astype(F32)).astype(BF16)


def join_blocks(*parts):
    shapes = []
    for kept, _ in parts:
        shapes += [((kept.shape[0] // 2, *kept.shape[1:]), BF16)] * 2
    joined = local_call(
        functools.partial(join_kernel, len(parts)), [item for pair in parts for item in pair], shapes
    )
    return [joined[2 * i : 2 * i + 2] for i in range(len(parts))]


def level_product_kernel(lower, ours, *refs):
    *theirs, half, peer, keep, send = refs
    middle, width = keep.shape
    cols = slice(lower, lower + width)
    product = dot(ours[...], half[:, cols], TN)
    first = 0
    for piece in theirs:
        product = product + dot(piece[...], peer[first : first + piece.shape[0], cols], TN)
        first += piece.shape[0]
    keep[...] = product[:middle].astype(BF16)
    send[...] = product[middle:].astype(BF16)


def level_product(ours, theirs, half, peer, lower, width):
    shape = ((ours.shape[1] // 2, width), BF16)
    return local_call(
        functools.partial(level_product_kernel, lower),
        (ours, *theirs, half, peer),
        [shape, shape],
        None,
        pl.CostEstimate(flops=4 * 10**9, bytes_accessed=10**7, transcendentals=0),
    )


def fence(*values):
    return lax.optimization_barrier(values)


def swap(values, axis, bit):
    count = lax.axis_size(axis)
    return lax.ppermute(values, axis, [(i, i ^ bit) for i in range(count)])


def peer_order(bits):
    count = 1 << len(bits)
    return [
        sum(bit for i, bit in enumerate(bits) if (p >> (len(bits) - 1 - i)) & 1) for p in range(count)
    ]


def blocks_by_peer(values, axis, order, count):
    size = values.shape[axis] // count
    me = lax.axis_index("dp")
    return [lax.dynamic_slice_in_dim(values, (me ^ r) * size, size, axis) for r in order]


def on_device(
    chars,
    char_mask,
    word_order,
    segment_ids,
    char_table,
    conv_weight,
    conv_bias,
    highway_weight,
    highway_bias,
    project_weight,
    project_bias,
    position_table,
    norm_gain,
    norm_bias,
    qkv_weight,
    qv_bias,
    out_weight,
    out_bias,
    up_weight,
    up_bias,
    down_weight,
    down_bias,
    out_grad,
):
    dp_count = lax.axis_size("dp")
    dp_index = lax.axis_index("dp")
    mp_index = lax.axis_index("mp")
    low = mp_index & 1
    word_count = chars.shape[0]
    per_peer = word_count // dp_count
    half_count = word_count // 2
    local_channels = conv_weight.shape[1]
    dp_bits = [1 << b for b in range(dp_count.bit_length() - 1)]
    order = peer_order(dp_bits)
    far_bits = dp_bits[1:] + dp_bits[:1]

    local_rows = (
        lax.dynamic_slice(
            word_order.reshape(dp_count, dp_count, per_peer),
            (0, dp_index, 0),
            (dp_count, 1, per_peer),
        ).reshape(word_count)
        - dp_index * word_count
    )
    places = local_rows ^ (low * half_count)
    perm = (jnp.arange(word_count, dtype=jnp.int32)[:, None] == places[None, :]).astype(BF16)

    def own_half(values):
        return lax.dynamic_slice_in_dim(values, low * half_count, half_count, 0)

    ids = jnp.where(char_mask > 0, chars, -1).reshape(dp_count, per_peer * CHARS)
    ids = lax.all_to_all(ids, "dp", split_axis=0, concat_axis=0, tiled=True)
    weights = jnp.swapaxes(highway_weight, 1, 2)
    ids, weights = fence(ids, weights)
    ids = ids.reshape(word_count, CHARS)

    used_taps = filter_mask(local_channels, mp_index * local_channels)
    filters = jnp.where(used_taps, conv_weight, jnp.zeros_like(conv_weight))
    counts = block_counts(ids, BLOCK)
    pooled, embedded = cnn_forward(
        ids, counts, spread_table(char_table), filters, conv_bias, BLOCK
    )

    def spots_of(bits):
        peers = dp_index ^ jnp.array(peer_order(bits), jnp.int32)
        index = jnp.arange(dp_count, dtype=jnp.int32)
        return jnp.sum(jnp.where(peers[None, :] == index[:, None], index[None, :], 0), axis=1)

    spots, far_spots = spots_of(dp_bits), spots_of(far_bits)
    places = jnp.concatenate([mp_index ^ jnp.arange(4, dtype=jnp.int32), spots])
    square = (word_count, local_channels)
    wide_f32 = jax.ShapeDtypeStruct(square, F32)
    wide_bf16 = jax.ShapeDtypeStruct(square, BF16)

    carried = inputs = pooled
    kept = []
    theirs = None
    for depth in range(LAYERS):
        a = inputs
        b = swap(a, "mp", 1)
        c = swap(a, "mp", 2)
        if depth:
            c, kept[0][4][0] = fence(c, kept[0][4][0])
        d = swap(c, "mp", 1)
        peer_shape = jax.ShapeDtypeStruct((word_count, CHANNELS // 2), BF16)
        direct = (CHANNELS // dp_count) % 128 == 0
        transform, gate, mixed_state, inputs, *peer_blocks = level_call(
            level_kernel,
            places,
            depth,
            (0, 1, 2, 3),
            weights,
            (a, b, c, d, carried, highway_bias[depth]),
            [wide_f32, wide_f32, wide_f32, wide_bf16] + [peer_shape] * (2 * direct),
        )
        if direct:
            ours, theirs = peer_blocks
        else:
            whole = jnp.zeros((word_count, CHANNELS), BF16)
            for r, piece in enumerate((a, b, c, d)):
                whole = lax.dynamic_update_slice(
                    whole, piece, (0, (mp_index ^ r) * local_channels)
                )
            blocks = blocks_by_peer(whole, 1, order, dp_count)
            ours = jnp.concatenate(blocks[: dp_count // 2], axis=1)
            theirs = jnp.concatenate(blocks[dp_count // 2 :], axis=1)
        step = -(-word_count // 48) * 16
        theirs = [
            swap(theirs[first : first + step], "dp", 1) for first in range(0, word_count, step)
        ]
        kept.append([carried, transform, gate, ours, theirs])
        carried = mixed_state

    width = project_weight.shape[1]
    half_f32, half_bf16 = ((half_count, width), F32), ((half_count, width), BF16)
    sums_shape = ((3, width), F32)

    def cross(own, matrix, sent, beside=None, dims=(((1,), (0,)), ((), ())), after=None):
        got = swap(sent, "mp", 1)
        pair, after = fence((dot(own, matrix, dims) + got.astype(F32)).astype(BF16), after)
        got, beside = fence(swap(pair, "mp", 2), beside)
        return (pair, got, beside) if after is None else (pair, got, beside, after)

    def row(vector):
        return vector.reshape(1, -1)

    def send(parts, bit):
        return parts[0], swap(parts[1], "dp", bit)

    def blocked(parts):
        shape = (dp_count // 4, CHANNELS // dp_count, local_channels)
        return [part.reshape(shape) for part in parts]

    def finish(parts, bits):
        for bit in bits:
            parts = send(join_blocks(parts)[0], bit)
        return parts[0][0].astype(F32) + parts[1][0].astype(F32)

    def blocked(parts):
        shape = (dp_count // 4, CHANNELS // dp_count, local_channels)
        return [part.reshape(shape) for part in parts]

    def finish(parts, bits):
        for bit in bits:
            parts = send(join_blocks(parts)[0], bit)
        return parts[0][0].astype(F32) + parts[1][0].astype(F32)

    spots = jnp.sum(
        jnp.where(
            (dp_index ^ jnp.array(order, jnp.int32))[None, :]
            == jnp.arange(dp_count, dtype=jnp.int32)[:, None],
            jnp.arange(dp_count, dtype=jnp.int32)[None, :],
            0,
        ),
        axis=1,
    )

    own_state, sent = local_call(
        project_kernel,
        (perm, inputs, project_weight),
        [((half_count, local_channels), BF16), half_bf16],
    )
    pair, got, kept[0][4][1] = cross(own_state, project_weight, sent, kept[0][4][1])
    embed_total, hidden_in, x_own = local_call(
        norm_kernel,
        (pair, got, row(project_bias), own_half(position_table), row(norm_gain[0]), row(norm_bias[0])),
        [half_f32, half_f32, half_bf16],
    )
    x_other = swap(x_own, "mp", 1)
    local_heads = qkv_weight.shape[2]
    qkv_flat = jnp.transpose(qkv_weight, (1, 2, 0)).reshape(3 * local_heads, width)
    segments = segment_ids[0]
    segments = jnp.where(low > 0, jnp.roll(segments, half_count), segments)
    column, line = segments.reshape(-1, 1), segments.reshape(1, -1)
    qkv_shape = ((word_count, 3 * local_heads), BF16)
    qkv, mixed, sent = local_call(
        attend_kernel,
        (x_own, x_other, qkv_flat, qv_bias, column, line, out_weight),
        [qkv_shape, ((word_count, local_heads), BF16), half_bf16],
    )
    pair, got, kept[0][4][2] = cross(mixed[:half_count], out_weight, sent, kept[0][4][2])
    resid_one, hidden_mid, mid_own = local_call(
        norm_kernel,
        (pair, got, row(out_bias), hidden_in, row(norm_gain[1]), row(norm_bias[1])),
        [half_f32, half_f32, half_bf16],
    )
    mid_other = swap(mid_own, "mp", 1)
    hidden_units = up_weight.shape[1]
    upward, activated, sent = local_call(
        feed_kernel,
        (mid_own, mid_other, up_weight, row(up_bias), down_weight),
        [((word_count, hidden_units), F32), ((word_count, hidden_units), BF16), half_bf16],
    )
    pair, got, kept[1][4][0] = cross(activated[:half_count], down_weight, sent, kept[1][4][0])
    encoded, resid_two_grad, down_own, sums_two = local_call(
        last_norm_kernel,
        (
            pair,
            got,
            row(down_bias),
            hidden_mid,
            row(norm_gain[2]),
            row(norm_bias[2]),
            own_half(out_grad),
        ),
        [half_f32, half_f32, half_bf16, sums_shape],
    )
    down_other = swap(down_own, "mp", 1)
    up_grad, up_bias_grad, sent = local_call(
        feed_back_kernel,
        (down_own, down_other, down_weight, upward, up_weight),
        [((word_count, hidden_units), BF16), ((1, hidden_units), F32), half_bf16],
    )
    pair, got, kept[1][4][1], up_later = cross(
        up_grad[:half_count], up_weight, sent, kept[1][4][1], NT, up_grad
    )
    resid_one_grad, attn_own, sums_one = local_call(
        norm_back_kernel,
        (pair, got, resid_two_grad, resid_one, row(norm_gain[1])),
        [half_f32, half_bf16, sums_shape],
    )
    first_blocks = products(
        [((mid_own, mid_other), up_later), ((down_own, down_other), activated)], far_spots
    )
    attn_own, first_blocks = fence(attn_own, first_blocks)
    first_parts = send(first_blocks, far_bits[0])
    attn_other = swap(attn_own, "mp", 1)
    qkv_grad, qkv_sums, sent = local_call(
        attend_back_kernel,
        (attn_own, attn_other, out_weight, qkv, column, line, qkv_flat),
        [qkv_shape, ((1, 3 * local_heads), F32), half_bf16],
    )
    pair, got, kept[1][4][2] = cross(qkv_grad[:half_count], qkv_flat, sent, kept[1][4][2])
    embed_grad, proj_own, sums_zero = local_call(
        norm_back_kernel,
        (pair, got, resid_one_grad, embed_total, row(norm_gain[0])),
        [half_f32, half_bf16, sums_shape],
    )
    proj_other = swap(proj_own, "mp", 1)
    proj_words, state_grad = local_call(
        project_back_kernel,
        (proj_own, proj_other, perm, project_weight),
        [((word_count, width), BF16), ((word_count, local_channels), F32)],
    )
    def level_back(depth, grad, before, beside, after):
        carried_now, transform_now, gate_now, _, _ = kept[depth]
        both_low, carry, bias_sum, far, mid = level_call(
            level_back_kernel,
            places,
            depth,
            (3, 2),
            weights,
            (transform_now, gate_now, carried_now, grad),
            [
                jax.ShapeDtypeStruct((word_count, 2 * local_channels), BF16),
                wide_f32,
                jax.ShapeDtypeStruct((1, 2 * local_channels), F32),
                wide_bf16,
                wide_f32,
            ],
        )
        got = swap(far, "mp", 1)
        pair = (mid + got.astype(F32)).astype(BF16)
        pair, later, before, after = fence(pair, both_low, before, after)
        near, own = level_call(
            level_rest_kernel, places, depth, (1, 0), weights, (later, carry), [wide_bf16, wide_f32]
        )
        halves = [both_low]
        if not depth:
            halves = [both_low[:, :local_channels], both_low[:, local_channels:]]
        peers = [swap(half, "dp", 1) for half in halves]
        crossing, peers[0], beside = fence(swap(pair, "mp", 2), peers[0], beside)
        below = own + swap(near, "mp", 1).astype(F32) + crossing.astype(F32)
        return below, bias_sum.reshape(2, local_channels), halves, peers, before, beside, after

    def level_part(depth, half, peer, column=0):
        return level_product(
            kept[depth][3], kept[depth][4], half, peer, column * local_channels, local_channels
        )

    def exchange(values, bit):
        sent = fence(values.astype(BF16))[0]
        return sent, swap(sent, "dp", bit)

    def combine(parts):
        return parts[0].astype(F32) + parts[1].astype(F32)

    def complete(parts, bits):
        for bit in bits:
            parts = exchange(combine(parts), bit)
        return combine(parts)

    def rows_of(values, rows):
        values = values.reshape(-1, values.shape[-1])
        return jnp.pad(values, ((0, rows - values.shape[0]), (0, width - values.shape[1])))

    row_pack = jnp.concatenate([sums_zero, sums_one, sums_two], axis=0)
    row_pack = row_pack + swap(row_pack, "mp", 1)
    quarter = half_count // 2
    high = (mp_index >> 1) & 1
    position_part = lax.dynamic_slice_in_dim(embed_grad, high * quarter, quarter, 0)
    small_rows = -(-(row_pack.shape[0] + 2) // 16) * 16
    small_pack = jnp.concatenate(
        [row_pack, rows_of(up_bias_grad, 1), rows_of(qkv_sums, small_rows - row_pack.shape[0] - 1)],
        axis=0,
    )

    state_grad, bias_one, halves_one, peers_one, _, first_parts, words_later = level_back(
        1, state_grad, None, first_parts, proj_words
    )
    first_parts = send(join_blocks(first_parts)[0], far_bits[1])
    second_blocks = products(
        [((x_own, x_other), qkv_grad), ((attn_own, attn_other), mixed), ((words_later,), inputs)],
        spots,
    )
    early = jnp.concatenate([position_part, small_pack], axis=0).astype(BF16)
    state_grad, second_blocks, early = fence(state_grad, second_blocks, early)
    early = exchange(early, dp_bits[0])
    first_one = level_part(1, halves_one[0], peers_one[0], 0)
    state_grad, bias_zero, halves_zero, peers_zero, first_one, beside, later = level_back(
        0, state_grad, first_one, (first_parts, early), (halves_one[0], peers_one[0])
    )
    first_parts, early = beside
    first_one = send(blocked(first_one), dp_bits[1])
    second_one = level_part(1, *later, 1)
    state_grad, second_one = fence(state_grad, second_one)
    first_zero = level_part(0, halves_zero[0], peers_zero[0])
    pooled_grad, first_zero, first_one, second_blocks = fence(
        state_grad.astype(BF16), first_zero, first_one, second_blocks
    )
    first_parts = join_blocks(first_parts)[0]
    first_one = send(join_blocks(first_one)[0], dp_bits[2])
    second_parts = send(second_blocks, dp_bits[0])
    second_one = send(blocked(second_one), dp_bits[1])
    first_zero = send(blocked(first_zero), dp_bits[1])

    middle = local_channels // 2
    lower, upper = slice(0, middle), slice(middle, local_channels)
    cnn_out = cnn_backward(
        counts, embedded, filters[:, lower], conv_bias[lower], pooled_grad[:, lower], None, BLOCK
    )
    (conv_low, bias_low, embed_part), first_one, second_one, first_zero, peers_zero[1] = fence(
        cnn_out, first_one, second_one, first_zero, peers_zero[1]
    )
    second_zero = level_part(0, halves_zero[1], peers_zero[1])
    second_one, first_zero = join_blocks(second_one, first_zero)
    second_parts = join_blocks(second_parts)[0]
    embed_part, second_one, first_zero, second_zero, second_parts, early = fence(
        embed_part, second_one, first_zero, second_zero, second_parts, combine(early)
    )
    second_zero = send(blocked(second_zero), dp_bits[1])
    second_one = send(second_one, dp_bits[2])
    first_zero = send(first_zero, dp_bits[2])
    second_parts = send(second_parts, dp_bits[1])
    early = exchange(early, dp_bits[1])
    cnn_out = cnn_backward(
        counts, embedded, filters[:, upper], conv_bias[upper], pooled_grad[:, upper], embed_part, BLOCK
    )
    (conv_high, bias_high, embed_part), second_one, first_zero, second_zero, early, first_parts = fence(
        cnn_out, second_one, first_zero, second_zero, early, first_parts
    )
    second_zero = send(join_blocks(second_zero)[0], dp_bits[2])
    early = exchange(combine(early), dp_bits[2])
    first_sum = finish(send(first_parts, far_bits[2]), far_bits[3:])
    conv_sum = jnp.concatenate([conv_low, conv_high], axis=1)
    conv_pack = jnp.concatenate(
        [
            jnp.where(used_taps, conv_sum, jnp.zeros_like(conv_sum)),
            jnp.concatenate([bias_low, bias_high], axis=1),
            bias_zero,
            bias_one,
        ],
        axis=0,
    )
    conv_rows = conv_sum.shape[0]
    conv_pack = jnp.pad(conv_pack, ((0, -conv_pack.shape[0] % 16), (0, 0)))
    conv_parts = exchange(conv_pack, dp_bits[0])
    table_sum = table_gradient(ids.T, embed_part, char_table.shape[0])
    table_sum, conv_parts, second_parts = fence(table_sum, conv_parts, second_parts)
    second_parts = send(join_blocks(second_parts)[0], dp_bits[2])
    conv_parts = exchange(combine(conv_parts), dp_bits[1])
    table_total = table_sum
    table_total = table_total + swap(table_total, "mp", 1)
    table_total = table_total + swap(table_total, "mp", 2)
    table_total, conv_parts = fence(table_total, conv_parts)
    conv_parts = exchange(combine(conv_parts), dp_bits[2])
    for bit in dp_bits:
        table_total = table_total + swap(table_total, "dp", bit)
    table_total = table_total.reshape(-1, STEPS, CHAR_DIM)
    table_total = jnp.swapaxes(table_total, 0, 1).reshape(-1, CHAR_DIM)[: char_table.shape[0]]
    conv_pack = complete(conv_parts, dp_bits[3:])
    conv_sums = (
        conv_pack[:conv_rows],
        conv_pack[conv_rows],
        conv_pack[conv_rows + 1 : conv_rows + 5].reshape(LAYERS, 2, local_channels),
    )
    second_sum = finish(second_parts, dp_bits[3:])
    level_sums = [
        jnp.stack([finish(parts, dp_bits[3:]) for parts in level], axis=1)
        for level in ((first_zero, second_zero), (first_one, second_one))
    ]
    highway_weight_grad = jnp.stack(level_sums, axis=0)
    early = complete(early, dp_bits[3:])
    position_part, small_pack = early[:quarter], early[quarter:]
    rows = row_pack.shape[0]
    sums_zero, sums_one, sums_two = (small_pack[3 * i : 3 * i + 3] for i in range(3))
    up_bias_grad = small_pack[rows : rows + 1]
    qkv_sums = small_pack[rows + 1 : rows + 2, : 3 * local_heads]
    qv_bias_grad = jnp.stack(
        [qkv_sums[0, :local_heads], qkv_sums[0, 2 * local_heads :]], axis=0
    )
    position_part = fence(position_part.astype(BF16))[0]
    position_other = swap(position_part, "mp", 2)
    position_half = jnp.concatenate(
        [
            jnp.where(high > 0, position_other, position_part),
            jnp.where(high > 0, position_part, position_other),
        ],
        axis=0,
    )

    def both_halves(values):
        return jnp.concatenate([values, swap(values, "mp", 1)], axis=0)

    position_grad = both_halves(position_half).astype(F32)

    def in_order(values):
        first, second = values[:half_count], values[half_count:]
        return jnp.concatenate(
            [jnp.where(low > 0, second, first), jnp.where(low > 0, first, second)], axis=0
        )

    def split(total, widths):
        parts, first = [], 0
        for width in widths:
            parts.append(total[:, first : first + width])
            first += width
        return parts

    up_sum, down_sum = split(first_sum, (up_weight.shape[1], down_weight.shape[0]))
    qkv_sum, out_sum, project_sum = split(
        second_sum, (3 * local_heads, local_heads, local_channels)
    )
    return (
        in_order(both_halves(encoded)),
        table_total,
        conv_sums[0],
        conv_sums[1],
        highway_weight_grad,
        conv_sums[2],
        project_sum.T,
        sums_zero[2],
        in_order(position_grad),
        jnp.stack([sums_zero[0], sums_one[0], sums_two[0]], axis=0),
        jnp.stack([sums_zero[1], sums_one[1], sums_two[1]], axis=0),
        qkv_sum.reshape(-1, 3, local_heads),
        qv_bias_grad,
        out_sum.T,
        sums_one[2],
        up_sum,
        up_bias_grad[0],
        down_sum.T,
        sums_two[2],
    )


def solution(mesh):
    return jax.shard_map(
        on_device,
        mesh=mesh,
        in_specs=(
            P("dp", None),
            P("dp", None),
            P(),
            P("dp", None),
            P(),
            P(None, "mp"),
            P("mp"),
            P(None, None, None, "mp"),
            P(None, None, "mp"),
            P("mp", None),
            P(),
            P(),
            P(),
            P(),
            P(None, None, "mp"),
            P(None, "mp"),
            P("mp", None),
            P(),
            P(None, "mp"),
            P("mp"),
            P("mp", None),
            P(),
            P("dp", None),
        ),
        out_specs=(
            P("dp", None),
            P(),
            P(None, "mp"),
            P("mp"),
            P(None, "dp", None, "mp"),
            P(None, None, "mp"),
            P("mp", "dp"),
            P(),
            P(),
            P(),
            P(),
            P("dp", None, "mp"),
            P(None, "mp"),
            P("mp", "dp"),
            P(),
            P("dp", "mp"),
            P("mp"),
            P("mp", "dp"),
            P(),
        ),
        check_vma=False,
    )
```

```python
import functools

import jax
import jax.numpy as jnp
from jax import lax
from jax.experimental import pallas as pl
from jax.experimental.pallas import tpu as pltpu
from jax.sharding import PartitionSpec as P

HEAD = 64
CHANNELS = 2048
CHAR_DIM = 16
CHARS = 50
TAPS = 7
LAYERS = 2
BLOCK = 128
TILES = 1

EPSILON = 1e-05
NEGATIVE = -1e30
F32 = jnp.float32
BF16 = jnp.bfloat16


def filter_mask(local_count, first):
    channel = first + jnp.arange(local_count, dtype=jnp.int32)
    tap_count = 1 + sum(
        ((channel >= CHANNELS // divisor).astype(jnp.int32) for divisor in (64, 32, 16, 8, 4, 2))
    )
    tap_index = jnp.arange(TAPS * CHAR_DIM, dtype=jnp.int32) // CHAR_DIM
    return tap_index[:, None] < tap_count[None, :]


STEPS = 8
ROWS = 7
SPAN = STEPS * CHAR_DIM
VMEM_LIMIT = 24 << 20
FREE = pl.CostEstimate(flops=1, bytes_accessed=1, transcendentals=0)

def spread_table(char_table):
    low = char_table.astype(BF16)
    eye = jnp.eye(STEPS, dtype=BF16)
    first = low[:256]
    rest = jnp.pad(low[256:], ((0, CHAR_DIM - (low.shape[0] - 256)), (0, 0)))
    parts = [(eye[:, None, :, None] * part[None, :, None, :]).reshape(-1, SPAN) for part in (first, rest)]
    return jnp.concatenate(parts, axis=0)

def place_filters(filters_ref, shifted):
    shifted[...] = jnp.zeros_like(shifted)
    taps = filters_ref.shape[0]
    width = filters_ref.shape[1]
    halved = (filters_ref[...].astype(F32) * 0.5).astype(BF16)
    for r in range(STEPS):
        shifted[CHAR_DIM * r : CHAR_DIM * r + taps, r * width : (r + 1) * width] = halved

def forward_kernel(block, counts, ids_ref, table_ref, filters_ref, bias_ref, pooled_ref, embed_ref, shifted, hot, total):
    words, width = pooled_ref.shape
    place_filters(filters_ref, shifted)
    lanes = lax.broadcasted_iota(jnp.int32, (words, 256), 1)
    lane = lax.broadcasted_iota(jnp.int32, (words, 128), 1)
    embed_ref[ROWS] = jnp.zeros_like(embed_ref[ROWS])
    total[...] = jnp.zeros_like(total)

    def embed(q, carry):
        left = jnp.zeros((words, 128), F32)
        for r in range(STEPS):
            ids = ids_ref[q, :, r : r + 1]
            hot[:, r * 256 : (r + 1) * 256] = jnp.where(ids == lanes, 1.0, 0.0).astype(BF16)
            mark = jnp.where(lane // CHAR_DIM == r, lane % CHAR_DIM + 256, -7)
            left = jnp.where(ids == mark, 1.0, left)
        hot[:, STEPS * 256 :] = left.astype(BF16)
        embed_ref[q] = jnp.dot(hot[...], table_ref[...], preferred_element_type=F32).astype(BF16)
        return carry

    lax.fori_loop(0, ROWS, embed, 0)
    half = bias_ref[...] * 0.5
    blocks = words // block

    def row(q, carry):
        def one(i, inner):
            rows = pl.ds(pl.multiple_of(i * block, block), block)
            x = jnp.concatenate([embed_ref[q, rows, :], embed_ref[q + 1, rows, :]], axis=1)
            for r in range(STEPS):
                u = jnp.dot(x, shifted[:, r * width : (r + 1) * width], preferred_element_type=F32) + half
                total[rows, :] += u + u * jnp.tanh(u)
            return inner

        lax.fori_loop(counts[blocks + q], blocks, one, 0)
        return carry

    lax.fori_loop(0, ROWS, row, 0)
    rest = half + half * jnp.tanh(half)
    for i in range(blocks):
        rows = slice(i * block, (i + 1) * block)
        seen = STEPS * counts[i]
        pooled_ref[rows, :] = (
            (total[rows, :] + (CHARS - seen).astype(F32) * rest) * (1.0 / CHARS)
        ).astype(BF16)


def block_counts(ids, block):
    most = jnp.max(jnp.sum((ids >= 0).astype(jnp.int32), axis=1).reshape(-1, block), axis=1)
    need = (most + STEPS - 1) // STEPS
    first = jnp.sum((need[None, :] <= jnp.arange(ROWS, dtype=jnp.int32)[:, None]).astype(jnp.int32), axis=1)
    return jnp.concatenate([need, first])

def cnn_forward(ids, counts, table, filters, bias, block):
    words = ids.shape[0]
    width = filters.shape[1]
    ids = jnp.pad(ids, ((0, 0), (0, ROWS * STEPS - CHARS)), constant_values=-1)
    ids = jnp.swapaxes(ids.reshape(words, ROWS, STEPS), 0, 1)
    vm = pl.BlockSpec(memory_space=pltpu.VMEM)
    return pl.pallas_call(
        functools.partial(forward_kernel, block),
        in_specs=[pl.BlockSpec(memory_space=pltpu.SMEM), vm, vm, vm, vm],
        out_specs=[vm, vm],
        out_shape=[jax.ShapeDtypeStruct((words, width), BF16), jax.ShapeDtypeStruct((ROWS + 1, words, SPAN), BF16)],
        scratch_shapes=[pltpu.VMEM((2 * SPAN, STEPS * width), BF16), pltpu.VMEM((words, STEPS * 256 + 128), BF16), pltpu.VMEM((words, width), F32)],
        compiler_params=pltpu.CompilerParams(vmem_limit_bytes=VMEM_LIMIT),
        cost_estimate=FREE,
    )(counts, ids, table, filters, bias.reshape(1, -1))


def backward_kernel(
    block,
    counts,
    embed_ref,
    filters_ref,
    bias_ref,
    grad_ref,
    embed_in,
    filter_out,
    bias_out,
    embed_grad,
    shifted,
    slopes,
    sums,
):
    words, width = grad_ref.shape
    blocks = words // block
    place_filters(filters_ref, shifted)
    half = bias_ref[...] * 0.5
    still = jnp.tanh(half)
    rest = (1.0 + still) + half * (1.0 - still * still)
    bias_out[...] = jnp.zeros_like(bias_out)
    sums[...] = jnp.zeros_like(sums)
    if embed_in is None:
        embed_grad[...] = jnp.zeros_like(embed_grad)
    else:
        embed_grad[...] = embed_in[...]
    scale = 0.5 / CHARS
    for i in range(blocks):
        grads = grad_ref[i * block : (i + 1) * block, :].astype(F32) * scale
        left = (CHARS - STEPS * counts[i]).astype(F32)
        bias_out[...] += jnp.sum(grads, axis=0, keepdims=True) * (rest * left)
    def row(q, outer):
        first = counts[blocks + q]

        def clear(i, carry):
            rows = pl.ds(pl.multiple_of(i * block, block), block)
            slopes[rows, :] = jnp.zeros((block, STEPS * width), BF16)
            return carry

        lax.fori_loop(counts[blocks + jnp.maximum(q - 1, 0)], first, clear, 0)

        def one(i, carry):
            rows = pl.ds(pl.multiple_of(i * block, block), block)
            x = jnp.concatenate([embed_ref[q, rows, :], embed_ref[q + 1, rows, :]], axis=1)
            grads = grad_ref[rows, :].astype(F32) * scale
            column = jnp.zeros((1, width), F32)
            for r in range(STEPS):
                cols = slice(r * width, (r + 1) * width)
                u = jnp.dot(x, shifted[:, cols], preferred_element_type=F32) + half
                t = jnp.tanh(u)
                slope = grads * ((1.0 + t) + u * (1.0 - t * t))
                column += jnp.sum(slope, axis=0, keepdims=True)
                slopes[rows, cols] = slope.astype(BF16)
            bias_out[...] += column
            return carry

        lax.fori_loop(first, blocks, one, 0)

        def spread(start):
            rows = slice(start, words)
            x = jnp.concatenate([embed_ref[q, rows, :], embed_ref[q + 1, rows, :]], axis=1)
            back = lax.dot_general(
                slopes[rows, :], shifted[...], (((1,), (1,)), ((), ())), preferred_element_type=F32
            )
            embed_grad[q, rows, :] += back[:, :SPAN]
            embed_grad[q + 1, rows, :] += back[:, SPAN:]
            for r in range(STEPS):
                cols = slice(r * width, (r + 1) * width)
                sums[:, cols] += lax.dot_general(
                    x, slopes[rows, cols], (((0,), (0,)), ((), ())), preferred_element_type=F32
                )

        middle = blocks // 2

        @pl.when(first < middle)
        def _():
            spread(0)

        @pl.when((first >= middle) & (first < blocks))
        def _():
            spread(middle * block)

        return outer

    lax.fori_loop(0, ROWS, row, 0)
    taps = filters_ref.shape[0]
    total = sums[:taps, :width]
    for r in range(1, STEPS):
        lower = CHAR_DIM * r
        total = total + sums[lower : lower + taps, r * width : (r + 1) * width]
    filter_out[...] = total


def cnn_backward(counts, embed, filters, bias, grad, embed_grad, block):
    words, width = grad.shape
    taps = filters.shape[0]
    vm = pl.BlockSpec(memory_space=pltpu.VMEM)
    operands = [counts, embed, filters, bias.reshape(1, -1), grad]
    kernel = functools.partial(backward_kernel, block)
    if embed_grad is None:
        inner = kernel

        def kernel(counts, embed, filters, bias, grad, *rest):
            inner(counts, embed, filters, bias, grad, None, *rest)
    else:
        operands.append(embed_grad)
    return pl.pallas_call(
        kernel,
        in_specs=[pl.BlockSpec(memory_space=pltpu.SMEM)] + [vm] * (len(operands) - 1),
        out_specs=[vm] * 3,
        out_shape=[
            jax.ShapeDtypeStruct((taps, width), F32),
            jax.ShapeDtypeStruct((1, width), F32),
            jax.ShapeDtypeStruct((ROWS + 1, words, SPAN), F32),
        ],
        scratch_shapes=[
            pltpu.VMEM((2 * SPAN, STEPS * width), BF16),
            pltpu.VMEM((words, STEPS * width), BF16),
            pltpu.VMEM((2 * SPAN, STEPS * width), F32),
        ],
        compiler_params=pltpu.CompilerParams(vmem_limit_bytes=VMEM_LIMIT),
        cost_estimate=FREE,
    )(*operands)


def table_kernel(ids_ref, embed_grad, table_out, hot):
    vocab, words = hot.shape[0], ids_ref.shape[1]
    high = embed_grad[:ROWS].reshape(ROWS * words, SPAN) * 2.0
    low = high.astype(BF16)
    pair = jnp.concatenate([low, (high - low.astype(F32)).astype(BF16)], axis=1)
    which = lax.broadcasted_iota(jnp.int32, (vocab, words), 0)
    lane = lax.broadcasted_iota(jnp.int32, (vocab, SPAN), 1) // CHAR_DIM
    table = jnp.zeros((vocab, SPAN), F32)
    for r in range(STEPS):
        for q in range(ROWS):
            j = q * STEPS + r
            cols = slice(q * words, (q + 1) * words)
            if j < CHARS:
                hot[:, cols] = jnp.where(ids_ref[j : j + 1, :] == which, 1.0, 0.0).astype(BF16)
            else:
                hot[:, cols] = jnp.zeros((vocab, words), BF16)
        both = jnp.dot(hot[...], pair, preferred_element_type=F32)
        table = jnp.where(lane == r, both[:, :SPAN] + both[:, SPAN:], table)
    step = table_out.shape[0]
    for shift in (64, 32, 16):
        table = table + pltpu.roll(table, shift, 1)
    table_out[...] = jnp.zeros_like(table_out)
    for g in range(-(-vocab // step)):
        rows = min(step, vocab - g * step)
        cols = slice(g * CHAR_DIM, (g + 1) * CHAR_DIM)
        table_out[:rows, cols] = table[g * step : g * step + rows, cols]


def table_gradient(ids_columns, embed_grad, vocab):
    words = ids_columns.shape[1]
    rows = -(-vocab // 16) * 16
    vm = pl.BlockSpec(memory_space=pltpu.VMEM)
    return pl.pallas_call(
        table_kernel,
        in_specs=[vm, vm],
        out_specs=vm,
        out_shape=jax.ShapeDtypeStruct((-(-vocab // 64) * 8, SPAN), F32),
        scratch_shapes=[pltpu.VMEM((rows, ROWS * words), BF16)],
        compiler_params=pltpu.CompilerParams(vmem_limit_bytes=VMEM_LIMIT),
        cost_estimate=FREE,
    )(ids_columns, embed_grad)


def level_call(kernel, places, level, picks, weights, arrays, shapes, hidden=False):
    width = weights.shape[3]
    rows = arrays[0].shape[0]
    tile = rows // TILES
    weights = pltpu.with_memory_space_constraint(weights, pltpu.HBM)

    def picked(pick):
        return pl.BlockSpec((1, 2, width, width), lambda i, spots: (level, 0, spots[pick], 0))

    def tiled(shape):
        if shape[0] == rows:
            return pl.BlockSpec((tile, shape[1]), lambda i, spots: (i, 0))
        return pl.BlockSpec(shape, lambda i, spots: (0, 0))

    cost = FREE
    if hidden:
        cost = pl.CostEstimate(
            flops=8 * rows * width * width, bytes_accessed=16 * rows * width, transcendentals=0
        )
    return pl.pallas_call(
        kernel,
        grid_spec=pltpu.PrefetchScalarGridSpec(
            num_scalar_prefetch=1,
            grid=(TILES,),
            in_specs=[picked(pick) for pick in picks] + [tiled(item.shape) for item in arrays],
            out_specs=[tiled(item.shape) for item in shapes],
        ),
        out_shape=shapes,
        compiler_params=pltpu.CompilerParams(vmem_limit_bytes=VMEM_LIMIT),
        cost_estimate=cost,
    )(places, *[weights] * len(picks), *arrays)


def level_kernel(
    places, own_w, near_w, mid_w, far_w, own, near, mid, far, carried, bias,
    transform_out, gate_out, carried_out, low_out, *peers_out,
):
    if peers_out:
        ours, theirs = peers_out
        size = own.shape[1] * 4 // (places.shape[0] - 4)
        count = own.shape[1] // size
        for r, piece in enumerate((own, near, mid, far)):
            for h in range(count):
                spot = places[4 + places[r] * count + h]
                half = (places.shape[0] - 4) // 2
                block = piece[:, h * size : (h + 1) * size]

                @pl.when(spot < half)
                def _():
                    ours[:, pl.ds(pl.multiple_of(spot * size, size), size)] = block

                @pl.when(spot >= half)
                def _():
                    theirs[:, pl.ds(pl.multiple_of((spot - half) * size, size), size)] = block

    parts = []
    for j in range(2):
        total = dot(own[...], own_w[0, j]) + dot(near[...], near_w[0, j])
        total = total + dot(mid[...], mid_w[0, j]) + dot(far[...], far_w[0, j])
        parts.append(total + bias[j : j + 1, :])
    transform, gate = parts
    transform_out[...] = transform
    gate_out[...] = gate
    opened = 1.0 / (1.0 + jnp.exp(-gate))
    swished = transform / (1.0 + jnp.exp(-transform))
    mixed = opened * swished + (1.0 - opened) * carried[...].astype(F32)
    carried_out[...] = mixed
    low_out[...] = mixed.astype(BF16)


def level_back_kernel(places, far_w, mid_w, transform, gate, carried, grad, both_out, carry_out, bias_out, far_out, mid_out):
    width = transform.shape[1]
    value = grad[...]
    opened = 1.0 / (1.0 + jnp.exp(-gate[...]))
    squashed = 1.0 / (1.0 + jnp.exp(-transform[...]))
    swished = transform[...] * squashed
    slope = value * opened
    first = slope * (squashed * (1.0 + transform[...] * (1.0 - squashed)))
    second = (slope * (1.0 - opened)) * (swished - carried[...].astype(F32))
    carry_out[...] = value - slope
    both_out[:, :width] = first.astype(BF16)
    both_out[:, width:] = second.astype(BF16)

    @pl.when(pl.program_id(0) == 0)
    def _():
        bias_out[...] = jnp.zeros_like(bias_out)

    bias_out[:, :width] += jnp.sum(first.astype(BF16).astype(F32), axis=0, keepdims=True)
    bias_out[:, width:] += jnp.sum(second.astype(BF16).astype(F32), axis=0, keepdims=True)
    far_out[...] = back_product(both_out, far_w).astype(BF16)
    mid_out[...] = back_product(both_out, mid_w)


def back_product(both, weights):
    width = weights.shape[3]
    dims = (((1,), (1,)), ((), ()))
    first = lax.dot_general(both[:, :width], weights[0, 0], dims, preferred_element_type=F32)
    return first + lax.dot_general(both[:, width:], weights[0, 1], dims, preferred_element_type=F32)


def level_rest_kernel(places, near_w, own_w, both, carry, near_out, own_out):
    near_out[...] = back_product(both, near_w).astype(BF16)
    own_out[...] = back_product(both, own_w) + carry[...]


NT = (((1,), (1,)), ((), ()))
TN = (((0,), (0,)), ((), ()))


def dot(left, right, dims=(((1,), (0,)), ((), ()))):
    return lax.dot_general(left, right, dims, preferred_element_type=F32)


def local_call(kernel, arrays, shapes, scalars=None, cost=FREE):
    vm = pl.BlockSpec(memory_space=pltpu.VMEM)
    specs = [vm] * len(arrays)
    if scalars is not None:
        arrays = (scalars, *arrays)
        specs = [pl.BlockSpec(memory_space=pltpu.SMEM)] + specs
    return pl.pallas_call(
        kernel,
        in_specs=specs,
        out_specs=[vm] * len(shapes),
        out_shape=[jax.ShapeDtypeStruct(shape, kind) for shape, kind in shapes],
        compiler_params=pltpu.CompilerParams(vmem_limit_bytes=VMEM_LIMIT),
        cost_estimate=cost,
    )(*arrays)


def center_scale(total):
    center = total - jnp.mean(total, axis=-1, keepdims=True)
    return center, lax.rsqrt(jnp.mean(center * center, axis=-1, keepdims=True) + EPSILON)


def norm_kernel(pair, got, bias, base, gain, shift, total_out, hidden_out, low_out):
    total = pair[...].astype(F32) + got[...].astype(F32) + bias[...] + base[...]
    center, spread = center_scale(total)
    hidden = center * spread * gain[...] + shift[...]
    total_out[...] = total
    hidden_out[...] = hidden
    low_out[...] = hidden.astype(BF16)


def norm_back(total, gain, grad, grad_out, low_out, sums_out):
    center, spread = center_scale(total)
    normed = center * spread
    inner = grad * gain
    mean_inner = jnp.mean(inner, axis=-1, keepdims=True)
    mean_both = jnp.mean(inner * normed, axis=-1, keepdims=True)
    result = spread * (inner - mean_inner - normed * mean_both)
    low = result.astype(BF16)
    grad_out[...] = result
    low_out[...] = low
    sums_out[0:1, :] = jnp.sum(grad * normed, axis=0, keepdims=True)
    sums_out[1:2, :] = jnp.sum(grad, axis=0, keepdims=True)
    sums_out[2:3, :] = jnp.sum(low.astype(F32), axis=0, keepdims=True)


def last_norm_kernel(
    pair, got, bias, base, gain, shift, out_grad, encoded_out, grad_out, low_out, sums_out
):
    total = pair[...].astype(F32) + got[...].astype(F32) + bias[...] + base[...]
    center, spread = center_scale(total)
    encoded_out[...] = center * spread * gain[...] + shift[...]
    norm_back(total, gain[...], out_grad[...], grad_out, low_out, sums_out)


def norm_back_kernel(pair, got, base, total, gain, grad_out, low_out, sums_out):
    grad = pair[...].astype(F32) + got[...].astype(F32) + base[...]
    norm_back(total[...], gain[...], grad, grad_out, low_out, sums_out)


def project_kernel(perm, inputs, weight, own_out, send_out):
    half = own_out.shape[0]
    state = dot(perm[...], inputs[...]).astype(BF16)
    own_out[...] = state[:half]
    send_out[...] = dot(state[half:], weight[...]).astype(BF16)


def project_back_kernel(own, other, perm, weight, words_out, grad_out):
    half = own.shape[0]
    words = dot(perm[:half], own[...], TN) + dot(perm[half:], other[...], TN)
    words = words.astype(BF16)
    words_out[...] = words
    grad_out[...] = dot(words, weight[...], NT)


def head_probs(qkv, head, width, same):
    query = qkv[:, head * HEAD : (head + 1) * HEAD]
    keys = qkv[:, width + head * HEAD : width + (head + 1) * HEAD]
    scores = jnp.where(same, dot(query, keys, NT) * HEAD ** (-0.5), NEGATIVE)
    exps = jnp.exp(scores - jnp.max(scores, axis=-1, keepdims=True))
    return query, keys, exps * (1.0 / jnp.sum(exps, axis=-1, keepdims=True))


def attend_kernel(own, other, weight, biases, column, row, out_w, qkv_out, mixed_out, send_out):
    half, width = own.shape[0], out_w.shape[0]
    for rows, part in ((slice(0, half), own), (slice(half, 2 * half), other)):
        product = dot(part[...], weight[...], NT)
        qkv_out[rows, :width] = (product[:, :width] + biases[0:1, :]).astype(BF16)
        qkv_out[rows, width : 2 * width] = product[:, width : 2 * width].astype(BF16)
        qkv_out[rows, 2 * width :] = (product[:, 2 * width :] + biases[1:2, :]).astype(BF16)
    qkv = qkv_out[...]
    same = column[...] == row[...]
    for head in range(width // HEAD):
        _, _, probs = head_probs(qkv, head, width, same)
        values = qkv[:, 2 * width + head * HEAD : 2 * width + (head + 1) * HEAD]
        mixed_out[:, head * HEAD : (head + 1) * HEAD] = dot(probs.astype(BF16), values).astype(BF16)
    send_out[...] = dot(mixed_out[half:, :], out_w[...]).astype(BF16)


def attend_back_kernel(own, other, out_w, qkv_ref, column, row, weight, grad_out, sums_out, send_out):
    half, width = own.shape[0], out_w.shape[0]
    qkv = qkv_ref[...]
    same = column[...] == row[...]
    mixed = jnp.concatenate(
        [dot(part[...], out_w[...], NT).astype(BF16) for part in (own, other)], axis=0
    )
    scale = HEAD ** (-0.5)
    for head in range(width // HEAD):
        query, keys, probs = head_probs(qkv, head, width, same)
        values = qkv[:, 2 * width + head * HEAD : 2 * width + (head + 1) * HEAD]
        grads = mixed[:, head * HEAD : (head + 1) * HEAD]
        inner = dot(grads, values, NT)
        slope = probs * (inner - jnp.sum(probs * inner, axis=-1, keepdims=True))
        slope = slope.astype(BF16)
        parts = (
            dot(slope, keys) * scale,
            dot(slope, query, TN) * scale,
            dot(probs.astype(BF16), grads, TN),
        )
        for j, part in enumerate(parts):
            first = j * width + head * HEAD
            grad_out[:, first : first + HEAD] = part.astype(BF16)
    sums_out[...] = jnp.sum(grad_out[...].astype(F32), axis=0, keepdims=True)
    send_out[...] = dot(grad_out[half:, :], weight[...]).astype(BF16)


def gelu_parts(value):
    scale = 0.7978845608028654
    square = value * value
    t = jnp.tanh(scale * value * (1.0 + 0.044715 * square))
    return t, scale * (1.0 + 3 * 0.044715 * square)


def feed_kernel(own, other, up_w, up_b, down_w, upward_out, active_out, send_out):
    half = own.shape[0]
    for rows, part in ((slice(0, half), own), (slice(half, 2 * half), other)):
        upward = dot(part[...], up_w[...]) + up_b[...]
        t, _ = gelu_parts(upward)
        upward_out[rows, :] = upward
        active_out[rows, :] = (0.5 * upward * (1.0 + t)).astype(BF16)
    send_out[...] = dot(active_out[half:, :], down_w[...]).astype(BF16)


def feed_back_kernel(own, other, down_w, upward_ref, up_w, grad_out, sums_out, send_out):
    half = own.shape[0]
    total = jnp.zeros(sums_out.shape, F32)
    for rows, part in ((slice(0, half), own), (slice(half, 2 * half), other)):
        grad = dot(part[...], down_w[...], NT)
        upward = upward_ref[rows, :]
        t, inner = gelu_parts(upward)
        slope = 0.5 * (1.0 + t) + 0.5 * upward * (1.0 - t * t) * inner
        low = (grad * slope).astype(BF16)
        grad_out[rows, :] = low
        total = total + jnp.sum(low.astype(F32), axis=0, keepdims=True)
    sums_out[...] = total
    send_out[...] = dot(grad_out[half:, :], up_w[...], NT).astype(BF16)


def products_kernel(counts, spots, *refs):
    pieces = 1 + (len(refs) - sum(counts) - len(counts) - 1)
    operands, keep, sends = refs[: -pieces], refs[-pieces], refs[1 - pieces :]
    half, rows, _ = keep.shape
    first, position = 0, 0
    for count in counts:
        lefts, right = operands[position : position + count], operands[position + count]
        position += count + 1
        width, step = right.shape[1], right.shape[0] // count
        product = sum(
            dot(left[...], right[i * step : (i + 1) * step, :], TN) for i, left in enumerate(lefts)
        )
        cols = slice(first, first + width)
        for d in range(2 * half):
            block = product[d * rows : (d + 1) * rows].astype(BF16)

            @pl.when(spots[d] < half)
            def _():
                keep[spots[d], :, cols] = block

            @pl.when(spots[d] >= half)
            def _():
                start = 0
                for send in sends:
                    low = max(first, start)
                    high = min(first + width, start + send.shape[2])
                    if low < high:
                        send[spots[d] - half, :, low - start : high - start] = block[
                            :, low - first : high - first
                        ]
                    start += send.shape[2]

        first += width


def products(groups, spots, split=0):
    peers = spots.shape[0]
    total = sum(right.shape[1] for _, right in groups)
    rows = groups[0][0][0].shape[1] // peers
    widths = [split, total - split] if split else [total]
    return local_call(
        functools.partial(products_kernel, [len(lefts) for lefts, _ in groups]),
        [item for lefts, right in groups for item in (*lefts, right)],
        [((peers // 2, rows, columns), BF16) for columns in (total, *widths)],
        spots,
        pl.CostEstimate(flops=4 * 10**9, bytes_accessed=10**7, transcendentals=0),
    )


def join_kernel(counts, *refs):
    outs = refs[sum(counts) :]
    position = 0
    for i, count in enumerate(counts):
        kept, *got = refs[position : position + count]
        position += count
        first, second = outs[2 * i], outs[2 * i + 1]
        half = first.shape[0]
        for j in range(half):
            start = 0
            for piece in got:
                cols = slice(start, start + piece.shape[2])
                start += piece.shape[2]
                first[j, :, cols] = (kept[j, :, cols].astype(F32) + piece[j].astype(F32)).astype(BF16)
                second[j, :, cols] = (
                    kept[half + j, :, cols].astype(F32) + piece[half + j].astype(F32)
                ).astype(BF16)


def join_blocks(*parts):
    shapes = []
    for kept, *_ in parts:
        shapes += [((kept.shape[0] // 2, *kept.shape[1:]), BF16)] * 2
    joined = local_call(
        functools.partial(join_kernel, [len(items) for items in parts]),
        [item for items in parts for item in items],
        shapes,
    )
    return [joined[2 * i : 2 * i + 2] for i in range(len(parts))]


def level_product_kernel(lower, ours, *refs):
    *theirs, half, peer, keep, send = refs
    middle, width = keep.shape
    cols = slice(lower, lower + width)
    product = dot(ours[...], half[:, cols], TN)
    first = 0
    for piece in theirs:
        product = product + dot(piece[...], peer[first : first + piece.shape[0], cols], TN)
        first += piece.shape[0]
    keep[...] = product[:middle].astype(BF16)
    send[...] = product[middle:].astype(BF16)


def level_product(ours, theirs, half, peer, lower, width):
    shape = ((ours.shape[1] // 2, width), BF16)
    return local_call(
        functools.partial(level_product_kernel, lower),
        (ours, *theirs, half, peer),
        [shape, shape],
        None,
        pl.CostEstimate(flops=4 * 10**9, bytes_accessed=10**7, transcendentals=0),
    )


def fence(*values):
    return lax.optimization_barrier(values)


def swap(values, axis, bit):
    count = lax.axis_size(axis)
    return lax.ppermute(values, axis, [(i, i ^ bit) for i in range(count)])


def peer_order(bits):
    count = 1 << len(bits)
    return [
        sum(bit for i, bit in enumerate(bits) if (p >> (len(bits) - 1 - i)) & 1) for p in range(count)
    ]


def blocks_by_peer(values, axis, order, count):
    size = values.shape[axis] // count
    me = lax.axis_index("dp")
    return [lax.dynamic_slice_in_dim(values, (me ^ r) * size, size, axis) for r in order]


def on_device(
    chars,
    char_mask,
    word_order,
    segment_ids,
    char_table,
    conv_weight,
    conv_bias,
    highway_weight,
    highway_bias,
    project_weight,
    project_bias,
    position_table,
    norm_gain,
    norm_bias,
    qkv_weight,
    qv_bias,
    out_weight,
    out_bias,
    up_weight,
    up_bias,
    down_weight,
    down_bias,
    out_grad,
):
    dp_count = lax.axis_size("dp")
    dp_index = lax.axis_index("dp")
    mp_index = lax.axis_index("mp")
    low = mp_index & 1
    word_count = chars.shape[0]
    per_peer = word_count // dp_count
    half_count = word_count // 2
    local_channels = conv_weight.shape[1]
    dp_bits = [1 << b for b in range(dp_count.bit_length() - 1)]
    order = peer_order(dp_bits)
    far_bits = dp_bits[1:] + dp_bits[:1]

    local_rows = (
        lax.dynamic_slice(
            word_order.reshape(dp_count, dp_count, per_peer),
            (0, dp_index, 0),
            (dp_count, 1, per_peer),
        ).reshape(word_count)
        - dp_index * word_count
    )
    places = local_rows ^ (low * half_count)
    perm = (jnp.arange(word_count, dtype=jnp.int32)[:, None] == places[None, :]).astype(BF16)

    def own_half(values):
        return lax.dynamic_slice_in_dim(values, low * half_count, half_count, 0)

    ids = jnp.where(char_mask > 0, chars, -1).reshape(dp_count, per_peer * CHARS)
    ids = lax.all_to_all(ids, "dp", split_axis=0, concat_axis=0, tiled=True)
    ids = ids.reshape(word_count, CHARS)

    used_taps = filter_mask(local_channels, mp_index * local_channels)
    filters = jnp.where(used_taps, conv_weight, jnp.zeros_like(conv_weight))
    counts = block_counts(ids, BLOCK)
    pooled, embedded = cnn_forward(
        ids, counts, spread_table(char_table), filters, conv_bias, BLOCK
    )

    weights = jnp.swapaxes(fence(highway_weight, pooled)[0], 1, 2)

    def spots_of(bits):
        peers = dp_index ^ jnp.array(peer_order(bits), jnp.int32)
        index = jnp.arange(dp_count, dtype=jnp.int32)
        return jnp.sum(jnp.where(peers[None, :] == index[:, None], index[None, :], 0), axis=1)

    spots, far_spots = spots_of(dp_bits), spots_of(far_bits)
    places = jnp.concatenate([mp_index ^ jnp.arange(4, dtype=jnp.int32), spots])
    square = (word_count, local_channels)
    wide_f32 = jax.ShapeDtypeStruct(square, F32)
    wide_bf16 = jax.ShapeDtypeStruct(square, BF16)

    carried = inputs = pooled
    kept = []
    theirs = None
    for depth in range(LAYERS):
        a = inputs
        b = swap(a, "mp", 1)
        c = swap(a, "mp", 2)
        if depth:
            c, kept[0][4][0] = fence(c, kept[0][4][0])
        else:
            c, weights = fence(c, weights)
        d = swap(c, "mp", 1)
        peer_shape = jax.ShapeDtypeStruct((word_count, CHANNELS // 2), BF16)
        far_peer = pltpu.HBM(peer_shape.shape, BF16)
        far_f32 = pltpu.HBM(square, F32)
        direct = (CHANNELS // dp_count) % 128 == 0
        transform, gate, mixed_state, inputs, *peer_blocks = level_call(
            level_kernel,
            places,
            depth,
            (0, 1, 2, 3),
            weights,
            (a, b, c, d, carried, highway_bias[depth]),
            [far_f32, far_f32, wide_f32, wide_bf16] + [far_peer, peer_shape] * direct,
        )
        if direct:
            ours, theirs = peer_blocks
        else:
            whole = jnp.zeros((word_count, CHANNELS), BF16)
            for r, piece in enumerate((a, b, c, d)):
                whole = lax.dynamic_update_slice(
                    whole, piece, (0, (mp_index ^ r) * local_channels)
                )
            blocks = blocks_by_peer(whole, 1, order, dp_count)
            ours = jnp.concatenate(blocks[: dp_count // 2], axis=1)
            theirs = jnp.concatenate(blocks[dp_count // 2 :], axis=1)
        step = -(-word_count // 48) * 16
        theirs = [
            swap(theirs[first : first + step], "dp", 1) for first in range(0, word_count, step)
        ]
        kept.append([carried, transform, gate, ours, theirs])
        carried = mixed_state

    width = project_weight.shape[1]
    half_f32, half_bf16 = ((half_count, width), F32), ((half_count, width), BF16)
    sums_shape = ((3, width), F32)

    def cross(own, matrix, sent, beside=None, dims=(((1,), (0,)), ((), ())), after=None):
        got = swap(sent, "mp", 1)
        pair, after = fence((dot(own, matrix, dims) + got.astype(F32)).astype(BF16), after)
        got, beside = fence(swap(pair, "mp", 2), beside)
        return (pair, got, beside) if after is None else (pair, got, beside, after)

    def row(vector):
        return vector.reshape(1, -1)

    def send(parts, bit):
        return parts[0], swap(parts[1], "dp", bit)

    def blocked(parts):
        shape = (dp_count // 4, CHANNELS // dp_count, local_channels)
        return [part.reshape(shape) for part in parts]

    def finish(parts, bits):
        for bit in bits:
            parts = send(join_blocks(parts)[0], bit)
        return parts[0][0].astype(F32) + parts[1][0].astype(F32)

    def blocked(parts):
        shape = (dp_count // 4, CHANNELS // dp_count, local_channels)
        return [part.reshape(shape) for part in parts]

    def finish(parts, bits):
        for bit in bits:
            parts = send(join_blocks(parts)[0], bit)
        return parts[0][0].astype(F32) + parts[1][0].astype(F32)

    spots = jnp.sum(
        jnp.where(
            (dp_index ^ jnp.array(order, jnp.int32))[None, :]
            == jnp.arange(dp_count, dtype=jnp.int32)[:, None],
            jnp.arange(dp_count, dtype=jnp.int32)[None, :],
            0,
        ),
        axis=1,
    )

    own_state, sent = local_call(
        project_kernel,
        (perm, inputs, project_weight),
        [((half_count, local_channels), BF16), half_bf16],
    )
    pair, got, kept[0][4][1] = cross(own_state, project_weight, sent, kept[0][4][1])
    embed_total, hidden_in, x_own = local_call(
        norm_kernel,
        (pair, got, row(project_bias), own_half(position_table), row(norm_gain[0]), row(norm_bias[0])),
        [half_f32, half_f32, half_bf16],
    )
    x_other = swap(x_own, "mp", 1)
    local_heads = qkv_weight.shape[2]
    qkv_flat = jnp.transpose(qkv_weight, (1, 2, 0)).reshape(3 * local_heads, width)
    segments = segment_ids[0]
    segments = jnp.where(low > 0, jnp.roll(segments, half_count), segments)
    column, line = segments.reshape(-1, 1), segments.reshape(1, -1)
    qkv_shape = ((word_count, 3 * local_heads), BF16)
    qkv, mixed, sent = local_call(
        attend_kernel,
        (x_own, x_other, qkv_flat, qv_bias, column, line, out_weight),
        [qkv_shape, ((word_count, local_heads), BF16), half_bf16],
    )
    pair, got, kept[0][4][2] = cross(mixed[:half_count], out_weight, sent, kept[0][4][2])
    resid_one, hidden_mid, mid_own = local_call(
        norm_kernel,
        (pair, got, row(out_bias), hidden_in, row(norm_gain[1]), row(norm_bias[1])),
        [half_f32, half_f32, half_bf16],
    )
    mid_other = swap(mid_own, "mp", 1)
    hidden_units = up_weight.shape[1]
    upward, activated, sent = local_call(
        feed_kernel,
        (mid_own, mid_other, up_weight, row(up_bias), down_weight),
        [((word_count, hidden_units), F32), ((word_count, hidden_units), BF16), half_bf16],
    )
    pair, got, kept[1][4][0] = cross(activated[:half_count], down_weight, sent, kept[1][4][0])
    encoded, resid_two_grad, down_own, sums_two = local_call(
        last_norm_kernel,
        (
            pair,
            got,
            row(down_bias),
            hidden_mid,
            row(norm_gain[2]),
            row(norm_bias[2]),
            own_half(out_grad),
        ),
        [half_f32, half_f32, half_bf16, sums_shape],
    )
    down_other = swap(down_own, "mp", 1)
    encoded_other = swap(encoded, "mp", 1)
    up_grad, up_bias_grad, sent = local_call(
        feed_back_kernel,
        (down_own, down_other, down_weight, upward, up_weight),
        [((word_count, hidden_units), BF16), ((1, hidden_units), F32), half_bf16],
    )
    pair, got, beside, up_later = cross(
        up_grad[:half_count], up_weight, sent, (kept[1][4][1], encoded_other), NT, up_grad
    )
    kept[1][4][1], encoded_other = beside
    resid_one_grad, attn_own, sums_one = local_call(
        norm_back_kernel,
        (pair, got, resid_two_grad, resid_one, row(norm_gain[1])),
        [half_f32, half_bf16, sums_shape],
    )
    first_blocks = products(
        [((mid_own, mid_other), up_later), ((down_own, down_other), activated)], far_spots, 512
    )
    attn_own, first_blocks = fence(attn_own, first_blocks)
    first_kept, *first_sent = first_blocks
    first_got = [swap(piece, "dp", far_bits[0]) for piece in first_sent]
    attn_other = swap(attn_own, "mp", 1)
    qkv_grad, qkv_sums, sent = local_call(
        attend_back_kernel,
        (attn_own, attn_other, out_weight, qkv, column, line, qkv_flat),
        [qkv_shape, ((1, 3 * local_heads), F32), half_bf16],
    )
    pair, got, beside = cross(
        qkv_grad[:half_count], qkv_flat, sent, (kept[1][4][2], first_got[0])
    )
    kept[1][4][2], first_got[0] = beside
    embed_grad, proj_own, sums_zero = local_call(
        norm_back_kernel,
        (pair, got, resid_one_grad, embed_total, row(norm_gain[0])),
        [half_f32, half_bf16, sums_shape],
    )
    proj_other = swap(proj_own, "mp", 1)
    proj_words, state_grad = local_call(
        project_back_kernel,
        (proj_own, proj_other, perm, project_weight),
        [((word_count, width), BF16), ((word_count, local_channels), F32)],
    )
    def level_back(depth, grad, before, beside, after):
        carried_now, transform_now, gate_now, _, _ = kept[depth]
        both_low, carry, bias_sum, far, mid = level_call(
            level_back_kernel,
            places,
            depth,
            (3, 2),
            weights,
            (transform_now, gate_now, carried_now, grad),
            [
                jax.ShapeDtypeStruct((word_count, 2 * local_channels), BF16),
                wide_f32,
                jax.ShapeDtypeStruct((1, 2 * local_channels), F32),
                wide_bf16,
                wide_f32,
            ],
        )
        got = swap(far, "mp", 1)
        pair = (mid + got.astype(F32)).astype(BF16)
        pair, later, before, after = fence(pair, both_low, before, after)
        near, own = level_call(
            level_rest_kernel, places, depth, (1, 0), weights, (later, carry), [wide_bf16, wide_f32]
        )
        halves = [both_low]
        if not depth:
            halves = [both_low[:, :local_channels], both_low[:, local_channels:]]
        peers = [swap(half, "dp", 1) for half in halves]
        crossing, peers[0], beside = fence(swap(pair, "mp", 2), peers[0], beside)
        below = own + swap(near, "mp", 1).astype(F32) + crossing.astype(F32)
        return below, bias_sum.reshape(2, local_channels), halves, peers, before, beside, after

    def level_part(depth, half, peer, column=0):
        return level_product(
            kept[depth][3], kept[depth][4], half, peer, column * local_channels, local_channels
        )

    def exchange(values, bit):
        sent = fence(values.astype(BF16))[0]
        return sent, swap(sent, "dp", bit)

    def combine(parts):
        return parts[0].astype(F32) + parts[1].astype(F32)

    def complete(parts, bits):
        for bit in bits:
            parts = exchange(combine(parts), bit)
        return combine(parts)

    def rows_of(values, rows):
        values = values.reshape(-1, values.shape[-1])
        return jnp.pad(values, ((0, rows - values.shape[0]), (0, width - values.shape[1])))

    row_pack = jnp.concatenate([sums_zero, sums_one, sums_two], axis=0)
    row_pack = row_pack + swap(row_pack, "mp", 1)
    quarter = half_count // 2
    high = (mp_index >> 1) & 1
    position_part = lax.dynamic_slice_in_dim(embed_grad, high * quarter, quarter, 0)
    small_rows = -(-(row_pack.shape[0] + 2) // 16) * 16
    small_pack = jnp.concatenate(
        [row_pack, rows_of(up_bias_grad, 1), rows_of(qkv_sums, small_rows - row_pack.shape[0] - 1)],
        axis=0,
    )

    state_grad, bias_one, halves_one, peers_one, _, first_parts, words_later = level_back(
        1, state_grad, None, first_got[1], proj_words
    )
    first_got[1] = first_parts
    first_parts = send(join_blocks((first_kept, *first_got))[0], far_bits[1])
    second_blocks = products(
        [((x_own, x_other), qkv_grad), ((attn_own, attn_other), mixed), ((words_later,), inputs)],
        spots,
    )
    early = jnp.concatenate([position_part, small_pack], axis=0).astype(BF16)
    state_grad, second_blocks, early = fence(state_grad, second_blocks, early)
    early = exchange(early, dp_bits[0])
    first_one = level_part(1, halves_one[0], peers_one[0], 0)
    state_grad, bias_zero, halves_zero, peers_zero, before, beside, later = level_back(
        0, state_grad, (first_one, early), first_parts, (halves_one[0], peers_one[0])
    )
    first_one, early = before
    first_parts = beside
    first_one = send(blocked(first_one), dp_bits[1])
    second_one = level_part(1, *later, 1)
    state_grad, second_one = fence(state_grad, second_one)
    first_zero = level_part(0, halves_zero[0], peers_zero[0])
    pooled_grad, first_zero, first_one, second_blocks = fence(
        state_grad.astype(BF16), first_zero, first_one, second_blocks
    )
    first_parts = join_blocks(first_parts)[0]
    first_one = send(join_blocks(first_one)[0], dp_bits[2])
    second_parts = send(second_blocks, dp_bits[0])
    second_one = send(blocked(second_one), dp_bits[1])
    first_zero = send(blocked(first_zero), dp_bits[1])

    middle = local_channels // 2
    lower, upper = slice(0, middle), slice(middle, local_channels)
    cnn_out = cnn_backward(
        counts, embedded, filters[:, lower], conv_bias[lower], pooled_grad[:, lower], None, BLOCK
    )
    (conv_low, bias_low, embed_part), first_one, second_one, first_zero, peers_zero[1] = fence(
        cnn_out, first_one, second_one, first_zero, peers_zero[1]
    )
    second_zero = level_part(0, halves_zero[1], peers_zero[1])
    second_one, first_zero = join_blocks(second_one, first_zero)
    second_parts = join_blocks(second_parts)[0]
    embed_part, second_one, first_zero, second_zero, second_parts, early = fence(
        embed_part, second_one, first_zero, second_zero, second_parts, combine(early)
    )
    second_zero = send(blocked(second_zero), dp_bits[1])
    second_one = send(second_one, dp_bits[2])
    first_zero = send(first_zero, dp_bits[2])
    second_parts = send(second_parts, dp_bits[1])
    early = exchange(early, dp_bits[1])
    cnn_out = cnn_backward(
        counts, embedded, filters[:, upper], conv_bias[upper], pooled_grad[:, upper], embed_part, BLOCK
    )
    (conv_high, bias_high, embed_part), second_one, first_zero, second_zero, early, first_parts = fence(
        cnn_out, second_one, first_zero, second_zero, early, first_parts
    )
    second_zero = send(join_blocks(second_zero)[0], dp_bits[2])
    early = exchange(combine(early), dp_bits[2])
    first_sum = finish(send(first_parts, far_bits[2]), far_bits[3:])
    conv_sum = jnp.concatenate([conv_low, conv_high], axis=1)
    conv_pack = jnp.concatenate(
        [
            jnp.where(used_taps, conv_sum, jnp.zeros_like(conv_sum)),
            jnp.concatenate([bias_low, bias_high], axis=1),
            bias_zero,
            bias_one,
        ],
        axis=0,
    )
    conv_rows = conv_sum.shape[0]
    conv_pack = jnp.pad(conv_pack, ((0, -conv_pack.shape[0] % 16), (0, 0)))
    conv_parts = exchange(conv_pack, dp_bits[0])
    table_sum = table_gradient(ids.T, embed_part, char_table.shape[0])
    table_sum, conv_parts, second_parts = fence(table_sum, conv_parts, second_parts)
    second_parts = send(join_blocks(second_parts)[0], dp_bits[2])
    conv_parts = exchange(combine(conv_parts), dp_bits[1])
    table_total = table_sum
    table_total = table_total + swap(table_total, "mp", 1)
    table_total = table_total + swap(table_total, "mp", 2)
    table_total, conv_parts = fence(table_total, conv_parts)
    conv_parts = exchange(combine(conv_parts), dp_bits[2])
    for bit in dp_bits:
        table_total = table_total + swap(table_total, "dp", bit)
    table_total = table_total.reshape(-1, STEPS, CHAR_DIM)
    table_total = jnp.swapaxes(table_total, 0, 1).reshape(-1, CHAR_DIM)[: char_table.shape[0]]
    conv_pack = complete(conv_parts, dp_bits[3:])
    conv_sums = (
        conv_pack[:conv_rows],
        conv_pack[conv_rows],
        conv_pack[conv_rows + 1 : conv_rows + 5].reshape(LAYERS, 2, local_channels),
    )
    second_sum = finish(second_parts, dp_bits[3:])
    level_sums = [
        jnp.stack([finish(parts, dp_bits[3:]) for parts in level], axis=1)
        for level in ((first_zero, second_zero), (first_one, second_one))
    ]
    highway_weight_grad = jnp.stack(level_sums, axis=0)
    early = complete(early, dp_bits[3:])
    position_part, small_pack = early[:quarter], early[quarter:]
    rows = row_pack.shape[0]
    sums_zero, sums_one, sums_two = (small_pack[3 * i : 3 * i + 3] for i in range(3))
    up_bias_grad = small_pack[rows : rows + 1]
    qkv_sums = small_pack[rows + 1 : rows + 2, : 3 * local_heads]
    qv_bias_grad = jnp.stack(
        [qkv_sums[0, :local_heads], qkv_sums[0, 2 * local_heads :]], axis=0
    )
    position_part = fence(position_part.astype(BF16))[0]
    position_other = swap(position_part, "mp", 2)
    position_half = jnp.concatenate(
        [
            jnp.where(high > 0, position_other, position_part),
            jnp.where(high > 0, position_part, position_other),
        ],
        axis=0,
    )

    def both_halves(values):
        return jnp.concatenate([values, swap(values, "mp", 1)], axis=0)

    position_grad = both_halves(position_half).astype(F32)

    def in_order(values):
        first, second = values[:half_count], values[half_count:]
        return jnp.concatenate(
            [jnp.where(low > 0, second, first), jnp.where(low > 0, first, second)], axis=0
        )

    def split(total, widths):
        parts, first = [], 0
        for width in widths:
            parts.append(total[:, first : first + width])
            first += width
        return parts

    up_sum, down_sum = split(first_sum, (up_weight.shape[1], down_weight.shape[0]))
    qkv_sum, out_sum, project_sum = split(
        second_sum, (3 * local_heads, local_heads, local_channels)
    )
    return (
        in_order(jnp.concatenate([encoded, encoded_other], axis=0)),
        table_total,
        conv_sums[0],
        conv_sums[1],
        highway_weight_grad,
        conv_sums[2],
        project_sum.T,
        sums_zero[2],
        in_order(position_grad),
        jnp.stack([sums_zero[0], sums_one[0], sums_two[0]], axis=0),
        jnp.stack([sums_zero[1], sums_one[1], sums_two[1]], axis=0),
        qkv_sum.reshape(-1, 3, local_heads),
        qv_bias_grad,
        out_sum.T,
        sums_one[2],
        up_sum,
        up_bias_grad[0],
        down_sum.T,
        sums_two[2],
    )


def solution(mesh):
    return jax.shard_map(
        on_device,
        mesh=mesh,
        in_specs=(
            P("dp", None),
            P("dp", None),
            P(),
            P("dp", None),
            P(),
            P(None, "mp"),
            P("mp"),
            P(None, None, None, "mp"),
            P(None, None, "mp"),
            P("mp", None),
            P(),
            P(),
            P(),
            P(),
            P(None, None, "mp"),
            P(None, "mp"),
            P("mp", None),
            P(),
            P(None, "mp"),
            P("mp"),
            P("mp", None),
            P(),
            P("dp", None),
        ),
        out_specs=(
            P("dp", None),
            P(),
            P(None, "mp"),
            P("mp"),
            P(None, "dp", None, "mp"),
            P(None, None, "mp"),
            P("mp", "dp"),
            P(),
            P(),
            P(),
            P(),
            P("dp", None, "mp"),
            P(None, "mp"),
            P("mp", "dp"),
            P(),
            P("dp", "mp"),
            P("mp"),
            P("mp", "dp"),
            P(),
        ),
        check_vma=False,
    )
```

```python
import functools

import jax
import jax.numpy as jnp
from jax import lax
from jax.experimental import pallas as pl
from jax.experimental.pallas import tpu as pltpu
from jax.sharding import PartitionSpec as P

HEAD = 64
CHANNELS = 2048
CHAR_DIM = 16
CHARS = 50
TAPS = 7
LAYERS = 2
BLOCK = 128
TILES = 1

EPSILON = 1e-05
NEGATIVE = -1e30
F32 = jnp.float32
BF16 = jnp.bfloat16


def filter_mask(local_count, first):
    channel = first + jnp.arange(local_count, dtype=jnp.int32)
    tap_count = 1 + sum(
        ((channel >= CHANNELS // divisor).astype(jnp.int32) for divisor in (64, 32, 16, 8, 4, 2))
    )
    tap_index = jnp.arange(TAPS * CHAR_DIM, dtype=jnp.int32) // CHAR_DIM
    return tap_index[:, None] < tap_count[None, :]


STEPS = 8
ROWS = 7
SPAN = STEPS * CHAR_DIM
VMEM_LIMIT = 24 << 20
FREE = pl.CostEstimate(flops=1, bytes_accessed=1, transcendentals=0)

def spread_table(char_table):
    low = char_table.astype(BF16)
    eye = jnp.eye(STEPS, dtype=BF16)
    first = low[:256]
    rest = jnp.pad(low[256:], ((0, CHAR_DIM - (low.shape[0] - 256)), (0, 0)))
    parts = [(eye[:, None, :, None] * part[None, :, None, :]).reshape(-1, SPAN) for part in (first, rest)]
    return jnp.concatenate(parts, axis=0)

def place_filters(filters_ref, shifted):
    shifted[...] = jnp.zeros_like(shifted)
    taps = filters_ref.shape[0]
    width = filters_ref.shape[1]
    halved = (filters_ref[...].astype(F32) * 0.5).astype(BF16)
    for r in range(STEPS):
        shifted[CHAR_DIM * r : CHAR_DIM * r + taps, r * width : (r + 1) * width] = halved

def forward_kernel(block, counts, ids_ref, table_ref, filters_ref, bias_ref, pooled_ref, embed_ref, shifted, hot, total):
    words, width = pooled_ref.shape
    place_filters(filters_ref, shifted)
    lanes = lax.broadcasted_iota(jnp.int32, (words, 256), 1)
    lane = lax.broadcasted_iota(jnp.int32, (words, 128), 1)
    embed_ref[ROWS] = jnp.zeros_like(embed_ref[ROWS])
    total[...] = jnp.zeros_like(total)

    def embed(q, carry):
        left = jnp.zeros((words, 128), F32)
        for r in range(STEPS):
            ids = ids_ref[q, :, r : r + 1]
            hot[:, r * 256 : (r + 1) * 256] = jnp.where(ids == lanes, 1.0, 0.0).astype(BF16)
            mark = jnp.where(lane // CHAR_DIM == r, lane % CHAR_DIM + 256, -7)
            left = jnp.where(ids == mark, 1.0, left)
        hot[:, STEPS * 256 :] = left.astype(BF16)
        embed_ref[q] = jnp.dot(hot[...], table_ref[...], preferred_element_type=F32).astype(BF16)
        return carry

    lax.fori_loop(0, ROWS, embed, 0)
    half = bias_ref[...] * 0.5
    blocks = words // block

    def row(q, carry):
        def one(i, inner):
            rows = pl.ds(pl.multiple_of(i * block, block), block)
            x = jnp.concatenate([embed_ref[q, rows, :], embed_ref[q + 1, rows, :]], axis=1)
            for r in range(STEPS):
                u = jnp.dot(x, shifted[:, r * width : (r + 1) * width], preferred_element_type=F32) + half
                total[rows, :] += u + u * jnp.tanh(u)
            return inner

        lax.fori_loop(counts[blocks + q], blocks, one, 0)
        return carry

    lax.fori_loop(0, ROWS, row, 0)
    rest = half + half * jnp.tanh(half)
    for i in range(blocks):
        rows = slice(i * block, (i + 1) * block)
        seen = STEPS * counts[i]
        pooled_ref[rows, :] = (
            (total[rows, :] + (CHARS - seen).astype(F32) * rest) * (1.0 / CHARS)
        ).astype(BF16)


def block_counts(ids, block):
    most = jnp.max(jnp.sum((ids >= 0).astype(jnp.int32), axis=1).reshape(-1, block), axis=1)
    need = (most + STEPS - 1) // STEPS
    first = jnp.sum((need[None, :] <= jnp.arange(ROWS, dtype=jnp.int32)[:, None]).astype(jnp.int32), axis=1)
    return jnp.concatenate([need, first])

def cnn_forward(ids, counts, table, filters, bias, block):
    words = ids.shape[0]
    width = filters.shape[1]
    ids = jnp.pad(ids, ((0, 0), (0, ROWS * STEPS - CHARS)), constant_values=-1)
    ids = jnp.swapaxes(ids.reshape(words, ROWS, STEPS), 0, 1)
    vm = pl.BlockSpec(memory_space=pltpu.VMEM)
    return pl.pallas_call(
        functools.partial(forward_kernel, block),
        in_specs=[pl.BlockSpec(memory_space=pltpu.SMEM), vm, vm, vm, vm],
        out_specs=[vm, vm],
        out_shape=[jax.ShapeDtypeStruct((words, width), BF16), jax.ShapeDtypeStruct((ROWS + 1, words, SPAN), BF16)],
        scratch_shapes=[pltpu.VMEM((2 * SPAN, STEPS * width), BF16), pltpu.VMEM((words, STEPS * 256 + 128), BF16), pltpu.VMEM((words, width), F32)],
        compiler_params=pltpu.CompilerParams(vmem_limit_bytes=VMEM_LIMIT),
        cost_estimate=FREE,
    )(counts, ids, table, filters, bias.reshape(1, -1))


def backward_kernel(
    block,
    counts,
    embed_ref,
    filters_ref,
    bias_ref,
    grad_ref,
    embed_in,
    filter_out,
    bias_out,
    embed_grad,
    shifted,
    slopes,
    sums,
):
    words, width = grad_ref.shape
    blocks = words // block
    place_filters(filters_ref, shifted)
    half = bias_ref[...] * 0.5
    still = jnp.tanh(half)
    rest = (1.0 + still) + half * (1.0 - still * still)
    bias_out[...] = jnp.zeros_like(bias_out)
    sums[...] = jnp.zeros_like(sums)
    if embed_in is None:
        embed_grad[...] = jnp.zeros_like(embed_grad)
    else:
        embed_grad[...] = embed_in[...]
    scale = 0.5 / CHARS
    for i in range(blocks):
        grads = grad_ref[i * block : (i + 1) * block, :].astype(F32) * scale
        left = (CHARS - STEPS * counts[i]).astype(F32)
        bias_out[...] += jnp.sum(grads, axis=0, keepdims=True) * (rest * left)
    def row(q, outer):
        first = counts[blocks + q]

        def clear(i, carry):
            rows = pl.ds(pl.multiple_of(i * block, block), block)
            slopes[rows, :] = jnp.zeros((block, STEPS * width), BF16)
            return carry

        lax.fori_loop(counts[blocks + jnp.maximum(q - 1, 0)], first, clear, 0)

        def one(i, carry):
            rows = pl.ds(pl.multiple_of(i * block, block), block)
            x = jnp.concatenate([embed_ref[q, rows, :], embed_ref[q + 1, rows, :]], axis=1)
            grads = grad_ref[rows, :].astype(F32) * scale
            column = jnp.zeros((1, width), F32)
            for r in range(STEPS):
                cols = slice(r * width, (r + 1) * width)
                u = jnp.dot(x, shifted[:, cols], preferred_element_type=F32) + half
                t = jnp.tanh(u)
                slope = grads * ((1.0 + t) + u * (1.0 - t * t))
                column += jnp.sum(slope, axis=0, keepdims=True)
                slopes[rows, cols] = slope.astype(BF16)
            bias_out[...] += column
            return carry

        lax.fori_loop(first, blocks, one, 0)

        def spread(start):
            rows = slice(start, words)
            x = jnp.concatenate([embed_ref[q, rows, :], embed_ref[q + 1, rows, :]], axis=1)
            back = lax.dot_general(
                slopes[rows, :], shifted[...], (((1,), (1,)), ((), ())), preferred_element_type=F32
            )
            embed_grad[q, rows, :] += back[:, :SPAN]
            embed_grad[q + 1, rows, :] += back[:, SPAN:]
            for r in range(STEPS):
                cols = slice(r * width, (r + 1) * width)
                sums[:, cols] += lax.dot_general(
                    x, slopes[rows, cols], (((0,), (0,)), ((), ())), preferred_element_type=F32
                )

        middle = blocks // 2

        @pl.when(first < middle)
        def _():
            spread(0)

        @pl.when((first >= middle) & (first < blocks))
        def _():
            spread(middle * block)

        return outer

    lax.fori_loop(0, ROWS, row, 0)
    taps = filters_ref.shape[0]
    total = sums[:taps, :width]
    for r in range(1, STEPS):
        lower = CHAR_DIM * r
        total = total + sums[lower : lower + taps, r * width : (r + 1) * width]
    filter_out[...] = total


def cnn_backward(counts, embed, filters, bias, grad, embed_grad, block):
    words, width = grad.shape
    taps = filters.shape[0]
    vm = pl.BlockSpec(memory_space=pltpu.VMEM)
    operands = [counts, embed, filters, bias.reshape(1, -1), grad]
    kernel = functools.partial(backward_kernel, block)
    if embed_grad is None:
        inner = kernel

        def kernel(counts, embed, filters, bias, grad, *rest):
            inner(counts, embed, filters, bias, grad, None, *rest)
    else:
        operands.append(embed_grad)
    return pl.pallas_call(
        kernel,
        in_specs=[pl.BlockSpec(memory_space=pltpu.SMEM)] + [vm] * (len(operands) - 1),
        out_specs=[vm] * 3,
        out_shape=[
            jax.ShapeDtypeStruct((taps, width), F32),
            jax.ShapeDtypeStruct((1, width), F32),
            jax.ShapeDtypeStruct((ROWS + 1, words, SPAN), F32),
        ],
        scratch_shapes=[
            pltpu.VMEM((2 * SPAN, STEPS * width), BF16),
            pltpu.VMEM((words, STEPS * width), BF16),
            pltpu.VMEM((2 * SPAN, STEPS * width), F32),
        ],
        compiler_params=pltpu.CompilerParams(vmem_limit_bytes=VMEM_LIMIT),
        cost_estimate=FREE,
    )(*operands)


def table_kernel(ids_ref, embed_grad, table_out, hot):
    vocab, words = hot.shape[0], ids_ref.shape[1]
    high = embed_grad[:ROWS].reshape(ROWS * words, SPAN) * 2.0
    low = high.astype(BF16)
    pair = jnp.concatenate([low, (high - low.astype(F32)).astype(BF16)], axis=1)
    which = lax.broadcasted_iota(jnp.int32, (vocab, words), 0)
    lane = lax.broadcasted_iota(jnp.int32, (vocab, SPAN), 1) // CHAR_DIM
    table = jnp.zeros((vocab, SPAN), F32)
    for r in range(STEPS):
        for q in range(ROWS):
            j = q * STEPS + r
            cols = slice(q * words, (q + 1) * words)
            if j < CHARS:
                hot[:, cols] = jnp.where(ids_ref[j : j + 1, :] == which, 1.0, 0.0).astype(BF16)
            else:
                hot[:, cols] = jnp.zeros((vocab, words), BF16)
        both = jnp.dot(hot[...], pair, preferred_element_type=F32)
        table = jnp.where(lane == r, both[:, :SPAN] + both[:, SPAN:], table)
    step = table_out.shape[0]
    for shift in (64, 32, 16):
        table = table + pltpu.roll(table, shift, 1)
    table_out[...] = jnp.zeros_like(table_out)
    for g in range(-(-vocab // step)):
        rows = min(step, vocab - g * step)
        cols = slice(g * CHAR_DIM, (g + 1) * CHAR_DIM)
        table_out[:rows, cols] = table[g * step : g * step + rows, cols]


def table_gradient(ids_columns, embed_grad, vocab):
    words = ids_columns.shape[1]
    rows = -(-vocab // 16) * 16
    vm = pl.BlockSpec(memory_space=pltpu.VMEM)
    return pl.pallas_call(
        table_kernel,
        in_specs=[vm, vm],
        out_specs=vm,
        out_shape=jax.ShapeDtypeStruct((-(-vocab // 64) * 8, SPAN), F32),
        scratch_shapes=[pltpu.VMEM((rows, ROWS * words), BF16)],
        compiler_params=pltpu.CompilerParams(vmem_limit_bytes=VMEM_LIMIT),
        cost_estimate=FREE,
    )(ids_columns, embed_grad)


def level_call(kernel, places, level, picks, weights, arrays, shapes, hidden=False):
    width = weights.shape[3]
    rows = arrays[0].shape[0]
    tile = rows // TILES
    weights = pltpu.with_memory_space_constraint(weights, pltpu.HBM)

    def picked(pick):
        return pl.BlockSpec((1, 2, width, width), lambda i, spots: (level, 0, spots[pick], 0))

    def tiled(shape):
        if shape[0] == rows:
            return pl.BlockSpec((tile, shape[1]), lambda i, spots: (i, 0))
        return pl.BlockSpec(shape, lambda i, spots: (0, 0))

    cost = FREE
    if hidden:
        cost = pl.CostEstimate(
            flops=8 * rows * width * width, bytes_accessed=16 * rows * width, transcendentals=0
        )
    return pl.pallas_call(
        kernel,
        grid_spec=pltpu.PrefetchScalarGridSpec(
            num_scalar_prefetch=1,
            grid=(TILES,),
            in_specs=[picked(pick) for pick in picks] + [tiled(item.shape) for item in arrays],
            out_specs=[tiled(item.shape) for item in shapes],
        ),
        out_shape=shapes,
        compiler_params=pltpu.CompilerParams(vmem_limit_bytes=VMEM_LIMIT),
        cost_estimate=cost,
    )(places, *[weights] * len(picks), *arrays)


def level_kernel(
    places, own_w, near_w, mid_w, far_w, own, near, mid, far, carried, bias,
    transform_out, gate_out, low_out, *rest_out,
):
    peers_out = rest_out[len(rest_out) % 2 :]
    if peers_out:
        ours, theirs = peers_out
        size = own.shape[1] * 4 // (places.shape[0] - 4)
        count = own.shape[1] // size
        for r, piece in enumerate((own, near, mid, far)):
            for h in range(count):
                spot = places[4 + places[r] * count + h]
                half = (places.shape[0] - 4) // 2
                block = piece[:, h * size : (h + 1) * size]

                @pl.when(spot < half)
                def _():
                    ours[:, pl.ds(pl.multiple_of(spot * size, size), size)] = block

                @pl.when(spot >= half)
                def _():
                    theirs[:, pl.ds(pl.multiple_of((spot - half) * size, size), size)] = block

    parts = []
    for j in range(2):
        total = dot(own[...], own_w[0, j]) + dot(near[...], near_w[0, j])
        total = total + dot(mid[...], mid_w[0, j]) + dot(far[...], far_w[0, j])
        parts.append(total + bias[j : j + 1, :])
    transform, gate = parts
    transform_out[...] = transform
    gate_out[...] = gate
    opened = 1.0 / (1.0 + jnp.exp(-gate))
    swished = transform / (1.0 + jnp.exp(-transform))
    mixed = opened * swished + (1.0 - opened) * carried[...].astype(F32)
    low_out[...] = mixed.astype(BF16)
    if len(rest_out) % 2:
        rest_out[0][...] = mixed


def level_back_kernel(places, far_w, mid_w, transform, gate, carried, grad, both_out, carry_out, bias_out, far_out, mid_out):
    width = transform.shape[1]
    value = grad[...]
    opened = 1.0 / (1.0 + jnp.exp(-gate[...]))
    squashed = 1.0 / (1.0 + jnp.exp(-transform[...]))
    swished = transform[...] * squashed
    slope = value * opened
    first = slope * (squashed * (1.0 + transform[...] * (1.0 - squashed)))
    second = (slope * (1.0 - opened)) * (swished - carried[...].astype(F32))
    carry_out[...] = value - slope
    both_out[:, :width] = first.astype(BF16)
    both_out[:, width:] = second.astype(BF16)

    @pl.when(pl.program_id(0) == 0)
    def _():
        bias_out[...] = jnp.zeros_like(bias_out)

    bias_out[:, :width] += jnp.sum(first.astype(BF16).astype(F32), axis=0, keepdims=True)
    bias_out[:, width:] += jnp.sum(second.astype(BF16).astype(F32), axis=0, keepdims=True)
    far_out[...] = back_product(both_out, far_w).astype(BF16)
    mid_out[...] = back_product(both_out, mid_w)


def back_product(both, weights):
    width = weights.shape[3]
    dims = (((1,), (1,)), ((), ()))
    first = lax.dot_general(both[:, :width], weights[0, 0], dims, preferred_element_type=F32)
    return first + lax.dot_general(both[:, width:], weights[0, 1], dims, preferred_element_type=F32)


def level_rest_kernel(places, near_w, own_w, both, carry, near_out, own_out):
    near_out[...] = back_product(both, near_w).astype(BF16)
    own_out[...] = back_product(both, own_w) + carry[...]


NT = (((1,), (1,)), ((), ()))
TN = (((0,), (0,)), ((), ()))


def dot(left, right, dims=(((1,), (0,)), ((), ()))):
    return lax.dot_general(left, right, dims, preferred_element_type=F32)


def local_call(kernel, arrays, shapes, scalars=None, cost=FREE):
    vm = pl.BlockSpec(memory_space=pltpu.VMEM)
    specs = [vm] * len(arrays)
    if scalars is not None:
        arrays = (scalars, *arrays)
        specs = [pl.BlockSpec(memory_space=pltpu.SMEM)] + specs
    return pl.pallas_call(
        kernel,
        in_specs=specs,
        out_specs=[vm] * len(shapes),
        out_shape=[jax.ShapeDtypeStruct(shape, kind) for shape, kind in shapes],
        compiler_params=pltpu.CompilerParams(vmem_limit_bytes=VMEM_LIMIT),
        cost_estimate=cost,
    )(*arrays)


def center_scale(total):
    center = total - jnp.mean(total, axis=-1, keepdims=True)
    return center, lax.rsqrt(jnp.mean(center * center, axis=-1, keepdims=True) + EPSILON)


def norm_kernel(pair, got, bias, base, gain, shift, total_out, hidden_out, low_out):
    total = pair[...].astype(F32) + got[...].astype(F32) + bias[...] + base[...]
    center, spread = center_scale(total)
    hidden = center * spread * gain[...] + shift[...]
    total_out[...] = total
    hidden_out[...] = hidden
    low_out[...] = hidden.astype(BF16)


def norm_back(total, gain, grad, grad_out, low_out, sums_out):
    center, spread = center_scale(total)
    normed = center * spread
    inner = grad * gain
    mean_inner = jnp.mean(inner, axis=-1, keepdims=True)
    mean_both = jnp.mean(inner * normed, axis=-1, keepdims=True)
    result = spread * (inner - mean_inner - normed * mean_both)
    low = result.astype(BF16)
    grad_out[...] = result
    low_out[...] = low
    sums_out[0:1, :] = jnp.sum(grad * normed, axis=0, keepdims=True)
    sums_out[1:2, :] = jnp.sum(grad, axis=0, keepdims=True)
    sums_out[2:3, :] = jnp.sum(low.astype(F32), axis=0, keepdims=True)


def last_norm_kernel(
    pair, got, bias, base, gain, shift, out_grad, encoded_out, grad_out, low_out, sums_out
):
    total = pair[...].astype(F32) + got[...].astype(F32) + bias[...] + base[...]
    center, spread = center_scale(total)
    encoded_out[...] = center * spread * gain[...] + shift[...]
    norm_back(total, gain[...], out_grad[...], grad_out, low_out, sums_out)


def norm_back_kernel(pair, got, base, total, gain, grad_out, low_out, sums_out):
    grad = pair[...].astype(F32) + got[...].astype(F32) + base[...]
    norm_back(total[...], gain[...], grad, grad_out, low_out, sums_out)


def project_kernel(perm, inputs, weight, own_out, send_out):
    half = own_out.shape[0]
    state = dot(perm[...], inputs[...]).astype(BF16)
    own_out[...] = state[:half]
    send_out[...] = dot(state[half:], weight[...]).astype(BF16)


def project_back_kernel(own, other, perm, weight, words_out, grad_out):
    half = own.shape[0]
    words = dot(perm[:half], own[...], TN) + dot(perm[half:], other[...], TN)
    words = words.astype(BF16)
    words_out[...] = words
    grad_out[...] = dot(words, weight[...], NT)


def head_probs(qkv, head, width, same):
    query = qkv[:, head * HEAD : (head + 1) * HEAD]
    keys = qkv[:, width + head * HEAD : width + (head + 1) * HEAD]
    scores = jnp.where(same, dot(query, keys, NT) * HEAD ** (-0.5), NEGATIVE)
    exps = jnp.exp(scores - jnp.max(scores, axis=-1, keepdims=True))
    return query, keys, exps * (1.0 / jnp.sum(exps, axis=-1, keepdims=True))


def attend_kernel(own, other, weight, biases, column, row, out_w, qkv_out, mixed_out, send_out):
    half, width = own.shape[0], out_w.shape[0]
    for rows, part in ((slice(0, half), own), (slice(half, 2 * half), other)):
        product = dot(part[...], weight[...], NT)
        qkv_out[rows, :width] = (product[:, :width] + biases[0:1, :]).astype(BF16)
        qkv_out[rows, width : 2 * width] = product[:, width : 2 * width].astype(BF16)
        qkv_out[rows, 2 * width :] = (product[:, 2 * width :] + biases[1:2, :]).astype(BF16)
    qkv = qkv_out[...]
    same = column[...] == row[...]
    for head in range(width // HEAD):
        _, _, probs = head_probs(qkv, head, width, same)
        values = qkv[:, 2 * width + head * HEAD : 2 * width + (head + 1) * HEAD]
        mixed_out[:, head * HEAD : (head + 1) * HEAD] = dot(probs.astype(BF16), values).astype(BF16)
    send_out[...] = dot(mixed_out[half:, :], out_w[...]).astype(BF16)


def attend_back_kernel(own, other, out_w, qkv_ref, column, row, weight, grad_out, sums_out, send_out):
    half, width = own.shape[0], out_w.shape[0]
    qkv = qkv_ref[...]
    same = column[...] == row[...]
    mixed = jnp.concatenate(
        [dot(part[...], out_w[...], NT).astype(BF16) for part in (own, other)], axis=0
    )
    scale = HEAD ** (-0.5)
    for head in range(width // HEAD):
        query, keys, probs = head_probs(qkv, head, width, same)
        values = qkv[:, 2 * width + head * HEAD : 2 * width + (head + 1) * HEAD]
        grads = mixed[:, head * HEAD : (head + 1) * HEAD]
        inner = dot(grads, values, NT)
        slope = probs * (inner - jnp.sum(probs * inner, axis=-1, keepdims=True))
        slope = slope.astype(BF16)
        parts = (
            dot(slope, keys) * scale,
            dot(slope, query, TN) * scale,
            dot(probs.astype(BF16), grads, TN),
        )
        for j, part in enumerate(parts):
            first = j * width + head * HEAD
            grad_out[:, first : first + HEAD] = part.astype(BF16)
    sums_out[...] = jnp.sum(grad_out[...].astype(F32), axis=0, keepdims=True)
    send_out[...] = dot(grad_out[half:, :], weight[...]).astype(BF16)


def gelu_parts(value):
    scale = 0.7978845608028654
    square = value * value
    t = jnp.tanh(scale * value * (1.0 + 0.044715 * square))
    return t, scale * (1.0 + 3 * 0.044715 * square)


def feed_kernel(own, other, up_w, up_b, down_w, upward_out, active_out, send_out):
    half = own.shape[0]
    for rows, part in ((slice(0, half), own), (slice(half, 2 * half), other)):
        upward = dot(part[...], up_w[...]) + up_b[...]
        t, _ = gelu_parts(upward)
        upward_out[rows, :] = upward
        active_out[rows, :] = (0.5 * upward * (1.0 + t)).astype(BF16)
    send_out[...] = dot(active_out[half:, :], down_w[...]).astype(BF16)


def feed_back_kernel(own, other, down_w, upward_ref, up_w, grad_out, sums_out, send_out):
    half = own.shape[0]
    total = jnp.zeros(sums_out.shape, F32)
    for rows, part in ((slice(0, half), own), (slice(half, 2 * half), other)):
        grad = dot(part[...], down_w[...], NT)
        upward = upward_ref[rows, :]
        t, inner = gelu_parts(upward)
        slope = 0.5 * (1.0 + t) + 0.5 * upward * (1.0 - t * t) * inner
        low = (grad * slope).astype(BF16)
        grad_out[rows, :] = low
        total = total + jnp.sum(low.astype(F32), axis=0, keepdims=True)
    sums_out[...] = total
    send_out[...] = dot(grad_out[half:, :], up_w[...], NT).astype(BF16)


def products_kernel(counts, spots, *refs):
    pieces = 1 + (len(refs) - sum(counts) - len(counts) - 1)
    operands, keep, sends = refs[: -pieces], refs[-pieces], refs[1 - pieces :]
    half, rows, _ = keep.shape
    first, position = 0, 0
    for count in counts:
        lefts, right = operands[position : position + count], operands[position + count]
        position += count + 1
        width, step = right.shape[1], right.shape[0] // count
        product = sum(
            dot(left[...], right[i * step : (i + 1) * step, :], TN) for i, left in enumerate(lefts)
        )
        cols = slice(first, first + width)
        for d in range(2 * half):
            block = product[d * rows : (d + 1) * rows].astype(BF16)

            @pl.when(spots[d] < half)
            def _():
                keep[spots[d], :, cols] = block

            @pl.when(spots[d] >= half)
            def _():
                start = 0
                for send in sends:
                    low = max(first, start)
                    high = min(first + width, start + send.shape[2])
                    if low < high:
                        send[spots[d] - half, :, low - start : high - start] = block[
                            :, low - first : high - first
                        ]
                    start += send.shape[2]

        first += width


def products(groups, spots, split=0):
    peers = spots.shape[0]
    total = sum(right.shape[1] for _, right in groups)
    rows = groups[0][0][0].shape[1] // peers
    widths = [split, total - split] if split else [total]
    return local_call(
        functools.partial(products_kernel, [len(lefts) for lefts, _ in groups]),
        [item for lefts, right in groups for item in (*lefts, right)],
        [((peers // 2, rows, columns), BF16) for columns in (total, *widths)],
        spots,
        pl.CostEstimate(flops=4 * 10**9, bytes_accessed=10**7, transcendentals=0),
    )


def join_kernel(counts, *refs):
    outs = refs[sum(counts) :]
    position = 0
    for i, count in enumerate(counts):
        kept, *got = refs[position : position + count]
        position += count
        first, second = outs[2 * i], outs[2 * i + 1]
        half = first.shape[0]
        for j in range(half):
            start = 0
            for piece in got:
                cols = slice(start, start + piece.shape[2])
                start += piece.shape[2]
                first[j, :, cols] = (kept[j, :, cols].astype(F32) + piece[j].astype(F32)).astype(BF16)
                second[j, :, cols] = (
                    kept[half + j, :, cols].astype(F32) + piece[half + j].astype(F32)
                ).astype(BF16)


def join_blocks(*parts):
    shapes = []
    for kept, *_ in parts:
        shapes += [((kept.shape[0] // 2, *kept.shape[1:]), BF16)] * 2
    joined = local_call(
        functools.partial(join_kernel, [len(items) for items in parts]),
        [item for items in parts for item in items],
        shapes,
    )
    return [joined[2 * i : 2 * i + 2] for i in range(len(parts))]


def level_product_kernel(lower, ours, *refs):
    *theirs, half, peer, keep, send = refs
    middle, width = keep.shape
    cols = slice(lower, lower + width)
    product = dot(ours[...], half[:, cols], TN)
    first = 0
    for piece in theirs:
        product = product + dot(piece[...], peer[first : first + piece.shape[0], cols], TN)
        first += piece.shape[0]
    keep[...] = product[:middle].astype(BF16)
    send[...] = product[middle:].astype(BF16)


def level_product(ours, theirs, half, peer, lower, width):
    shape = ((ours.shape[1] // 2, width), BF16)
    return local_call(
        functools.partial(level_product_kernel, lower),
        (ours, *theirs, half, peer),
        [shape, shape],
        None,
        pl.CostEstimate(flops=4 * 10**9, bytes_accessed=10**7, transcendentals=0),
    )


def fence(*values):
    return lax.optimization_barrier(values)


def swap(values, axis, bit):
    count = lax.axis_size(axis)
    return lax.ppermute(values, axis, [(i, i ^ bit) for i in range(count)])


def peer_order(bits):
    count = 1 << len(bits)
    return [
        sum(bit for i, bit in enumerate(bits) if (p >> (len(bits) - 1 - i)) & 1) for p in range(count)
    ]


def blocks_by_peer(values, axis, order, count):
    size = values.shape[axis] // count
    me = lax.axis_index("dp")
    return [lax.dynamic_slice_in_dim(values, (me ^ r) * size, size, axis) for r in order]


def on_device(
    chars,
    char_mask,
    word_order,
    segment_ids,
    char_table,
    conv_weight,
    conv_bias,
    highway_weight,
    highway_bias,
    project_weight,
    project_bias,
    position_table,
    norm_gain,
    norm_bias,
    qkv_weight,
    qv_bias,
    out_weight,
    out_bias,
    up_weight,
    up_bias,
    down_weight,
    down_bias,
    out_grad,
):
    dp_count = lax.axis_size("dp")
    dp_index = lax.axis_index("dp")
    mp_index = lax.axis_index("mp")
    low = mp_index & 1
    word_count = chars.shape[0]
    per_peer = word_count // dp_count
    half_count = word_count // 2
    local_channels = conv_weight.shape[1]
    dp_bits = [1 << b for b in range(dp_count.bit_length() - 1)]
    order = peer_order(dp_bits)
    far_bits = dp_bits[1:] + dp_bits[:1]

    local_rows = (
        lax.dynamic_slice(
            word_order.reshape(dp_count, dp_count, per_peer),
            (0, dp_index, 0),
            (dp_count, 1, per_peer),
        ).reshape(word_count)
        - dp_index * word_count
    )
    places = local_rows ^ (low * half_count)
    perm = (jnp.arange(word_count, dtype=jnp.int32)[:, None] == places[None, :]).astype(BF16)

    def own_half(values):
        return lax.dynamic_slice_in_dim(values, low * half_count, half_count, 0)

    ids = jnp.where(char_mask > 0, chars, -1).reshape(dp_count, per_peer * CHARS)
    ids = lax.all_to_all(ids, "dp", split_axis=0, concat_axis=0, tiled=True)
    ids = ids.reshape(word_count, CHARS)

    used_taps = filter_mask(local_channels, mp_index * local_channels)
    filters = jnp.where(used_taps, conv_weight, jnp.zeros_like(conv_weight))
    counts = block_counts(ids, BLOCK)
    pooled, embedded = cnn_forward(
        ids, counts, spread_table(char_table), filters, conv_bias, BLOCK
    )

    weights = jnp.swapaxes(fence(highway_weight, pooled)[0], 1, 2)

    def spots_of(bits):
        peers = dp_index ^ jnp.array(peer_order(bits), jnp.int32)
        index = jnp.arange(dp_count, dtype=jnp.int32)
        return jnp.sum(jnp.where(peers[None, :] == index[:, None], index[None, :], 0), axis=1)

    spots, far_spots = spots_of(dp_bits), spots_of(far_bits)
    places = jnp.concatenate([mp_index ^ jnp.arange(4, dtype=jnp.int32), spots])
    square = (word_count, local_channels)
    wide_f32 = jax.ShapeDtypeStruct(square, F32)
    wide_bf16 = jax.ShapeDtypeStruct(square, BF16)

    carried = inputs = pooled
    kept = []
    theirs = None
    for depth in range(LAYERS):
        a = inputs
        b = swap(a, "mp", 1)
        c = swap(a, "mp", 2)
        if depth:
            c, kept[0][4][0] = fence(c, kept[0][4][0])
        else:
            c, weights = fence(c, weights)
        d = swap(c, "mp", 1)
        peer_shape = jax.ShapeDtypeStruct((word_count, CHANNELS // 2), BF16)
        far_peer = pltpu.HBM(peer_shape.shape, BF16)
        far_f32 = pltpu.HBM(square, F32)
        direct = (CHANNELS // dp_count) % 128 == 0
        more = depth + 1 < LAYERS
        transform, gate, inputs, *peer_blocks = level_call(
            level_kernel,
            places,
            depth,
            (0, 1, 2, 3),
            weights,
            (a, b, c, d, carried, highway_bias[depth]),
            [far_f32, far_f32, wide_bf16] + [wide_f32] * more + [far_peer, peer_shape] * direct,
        )
        mixed_state = peer_blocks.pop(0) if more else None
        if direct:
            ours, theirs = peer_blocks
        else:
            whole = jnp.zeros((word_count, CHANNELS), BF16)
            for r, piece in enumerate((a, b, c, d)):
                whole = lax.dynamic_update_slice(
                    whole, piece, (0, (mp_index ^ r) * local_channels)
                )
            blocks = blocks_by_peer(whole, 1, order, dp_count)
            ours = jnp.concatenate(blocks[: dp_count // 2], axis=1)
            theirs = jnp.concatenate(blocks[dp_count // 2 :], axis=1)
        step = -(-word_count // 48) * 16
        theirs = [
            swap(theirs[first : first + step], "dp", 1) for first in range(0, word_count, step)
        ]
        kept.append([carried, transform, gate, ours, theirs])
        carried = mixed_state

    width = project_weight.shape[1]
    half_f32, half_bf16 = ((half_count, width), F32), ((half_count, width), BF16)
    sums_shape = ((3, width), F32)

    def cross(own, matrix, sent, beside=None, dims=(((1,), (0,)), ((), ())), after=None):
        got = swap(sent, "mp", 1)
        pair, after = fence((dot(own, matrix, dims) + got.astype(F32)).astype(BF16), after)
        got, beside = fence(swap(pair, "mp", 2), beside)
        return (pair, got, beside) if after is None else (pair, got, beside, after)

    def row(vector):
        return vector.reshape(1, -1)

    def send(parts, bit):
        return parts[0], swap(parts[1], "dp", bit)

    def blocked(parts):
        shape = (dp_count // 4, CHANNELS // dp_count, local_channels)
        return [part.reshape(shape) for part in parts]

    def finish(parts, bits):
        for bit in bits:
            parts = send(join_blocks(parts)[0], bit)
        return parts[0][0].astype(F32) + parts[1][0].astype(F32)

    def blocked(parts):
        shape = (dp_count // 4, CHANNELS // dp_count, local_channels)
        return [part.reshape(shape) for part in parts]

    def finish(parts, bits):
        for bit in bits:
            parts = send(join_blocks(parts)[0], bit)
        return parts[0][0].astype(F32) + parts[1][0].astype(F32)

    spots = jnp.sum(
        jnp.where(
            (dp_index ^ jnp.array(order, jnp.int32))[None, :]
            == jnp.arange(dp_count, dtype=jnp.int32)[:, None],
            jnp.arange(dp_count, dtype=jnp.int32)[None, :],
            0,
        ),
        axis=1,
    )

    own_state, sent = local_call(
        project_kernel,
        (perm, inputs, project_weight),
        [((half_count, local_channels), BF16), half_bf16],
    )
    pair, got, kept[0][4][1] = cross(own_state, project_weight, sent, kept[0][4][1])
    embed_total, hidden_in, x_own = local_call(
        norm_kernel,
        (pair, got, row(project_bias), own_half(position_table), row(norm_gain[0]), row(norm_bias[0])),
        [half_f32, half_f32, half_bf16],
    )
    x_other = swap(x_own, "mp", 1)
    local_heads = qkv_weight.shape[2]
    qkv_flat = jnp.transpose(qkv_weight, (1, 2, 0)).reshape(3 * local_heads, width)
    segments = segment_ids[0]
    segments = jnp.where(low > 0, jnp.roll(segments, half_count), segments)
    column, line = segments.reshape(-1, 1), segments.reshape(1, -1)
    qkv_shape = ((word_count, 3 * local_heads), BF16)
    qkv, mixed, sent = local_call(
        attend_kernel,
        (x_own, x_other, qkv_flat, qv_bias, column, line, out_weight),
        [qkv_shape, ((word_count, local_heads), BF16), half_bf16],
    )
    pair, got, kept[0][4][2] = cross(mixed[:half_count], out_weight, sent, kept[0][4][2])
    resid_one, hidden_mid, mid_own = local_call(
        norm_kernel,
        (pair, got, row(out_bias), hidden_in, row(norm_gain[1]), row(norm_bias[1])),
        [half_f32, half_f32, half_bf16],
    )
    mid_other = swap(mid_own, "mp", 1)
    hidden_units = up_weight.shape[1]
    upward, activated, sent = local_call(
        feed_kernel,
        (mid_own, mid_other, up_weight, row(up_bias), down_weight),
        [((word_count, hidden_units), F32), ((word_count, hidden_units), BF16), half_bf16],
    )
    pair, got, kept[1][4][0] = cross(activated[:half_count], down_weight, sent, kept[1][4][0])
    encoded, resid_two_grad, down_own, sums_two = local_call(
        last_norm_kernel,
        (
            pair,
            got,
            row(down_bias),
            hidden_mid,
            row(norm_gain[2]),
            row(norm_bias[2]),
            own_half(out_grad),
        ),
        [half_f32, half_f32, half_bf16, sums_shape],
    )
    down_other = swap(down_own, "mp", 1)
    encoded_other = swap(encoded, "mp", 1)
    up_grad, up_bias_grad, sent = local_call(
        feed_back_kernel,
        (down_own, down_other, down_weight, upward, up_weight),
        [((word_count, hidden_units), BF16), ((1, hidden_units), F32), half_bf16],
    )
    pair, got, beside, up_later = cross(
        up_grad[:half_count], up_weight, sent, (kept[1][4][1], encoded_other), NT, up_grad
    )
    kept[1][4][1], encoded_other = beside
    resid_one_grad, attn_own, sums_one = local_call(
        norm_back_kernel,
        (pair, got, resid_two_grad, resid_one, row(norm_gain[1])),
        [half_f32, half_bf16, sums_shape],
    )
    first_blocks = products(
        [((mid_own, mid_other), up_later), ((down_own, down_other), activated)], far_spots, 512
    )
    attn_own, first_blocks = fence(attn_own, first_blocks)
    first_kept, *first_sent = first_blocks
    first_got = [swap(piece, "dp", far_bits[0]) for piece in first_sent]
    attn_other = swap(attn_own, "mp", 1)
    qkv_grad, qkv_sums, sent = local_call(
        attend_back_kernel,
        (attn_own, attn_other, out_weight, qkv, column, line, qkv_flat),
        [qkv_shape, ((1, 3 * local_heads), F32), half_bf16],
    )
    pair, got, beside = cross(
        qkv_grad[:half_count], qkv_flat, sent, (kept[1][4][2], first_got[0])
    )
    kept[1][4][2], first_got[0] = beside
    embed_grad, proj_own, sums_zero = local_call(
        norm_back_kernel,
        (pair, got, resid_one_grad, embed_total, row(norm_gain[0])),
        [half_f32, half_bf16, sums_shape],
    )
    proj_other = swap(proj_own, "mp", 1)
    proj_words, state_grad = local_call(
        project_back_kernel,
        (proj_own, proj_other, perm, project_weight),
        [((word_count, width), BF16), ((word_count, local_channels), F32)],
    )
    def level_back(depth, grad, before, beside, after):
        carried_now, transform_now, gate_now, _, _ = kept[depth]
        both_low, carry, bias_sum, far, mid = level_call(
            level_back_kernel,
            places,
            depth,
            (3, 2),
            weights,
            (transform_now, gate_now, carried_now, grad),
            [
                jax.ShapeDtypeStruct((word_count, 2 * local_channels), BF16),
                wide_f32,
                jax.ShapeDtypeStruct((1, 2 * local_channels), F32),
                wide_bf16,
                wide_f32,
            ],
        )
        got = swap(far, "mp", 1)
        pair = (mid + got.astype(F32)).astype(BF16)
        pair, later, before, after = fence(pair, both_low, before, after)
        near, own = level_call(
            level_rest_kernel, places, depth, (1, 0), weights, (later, carry), [wide_bf16, wide_f32]
        )
        halves = [both_low]
        if not depth:
            halves = [both_low[:, :local_channels], both_low[:, local_channels:]]
        peers = [swap(half, "dp", 1) for half in halves]
        crossing, peers[0], beside = fence(swap(pair, "mp", 2), peers[0], beside)
        below = own + swap(near, "mp", 1).astype(F32) + crossing.astype(F32)
        return below, bias_sum.reshape(2, local_channels), halves, peers, before, beside, after

    def level_part(depth, half, peer, column=0):
        return level_product(
            kept[depth][3], kept[depth][4], half, peer, column * local_channels, local_channels
        )

    def exchange(values, bit):
        sent = fence(values.astype(BF16))[0]
        return sent, swap(sent, "dp", bit)

    def combine(parts):
        return parts[0].astype(F32) + parts[1].astype(F32)

    def complete(parts, bits):
        for bit in bits:
            parts = exchange(combine(parts), bit)
        return combine(parts)

    def rows_of(values, rows):
        values = values.reshape(-1, values.shape[-1])
        return jnp.pad(values, ((0, rows - values.shape[0]), (0, width - values.shape[1])))

    row_pack = jnp.concatenate([sums_zero, sums_one, sums_two], axis=0)
    row_pack = row_pack + swap(row_pack, "mp", 1)
    quarter = half_count // 2
    high = (mp_index >> 1) & 1
    position_part = lax.dynamic_slice_in_dim(embed_grad, high * quarter, quarter, 0)
    small_rows = -(-(row_pack.shape[0] + 2) // 16) * 16
    small_pack = jnp.concatenate(
        [row_pack, rows_of(up_bias_grad, 1), rows_of(qkv_sums, small_rows - row_pack.shape[0] - 1)],
        axis=0,
    )

    state_grad, bias_one, halves_one, peers_one, _, first_parts, words_later = level_back(
        1, state_grad, None, first_got[1], proj_words
    )
    first_got[1] = first_parts
    first_parts = send(join_blocks((first_kept, *first_got))[0], far_bits[1])
    second_blocks = products(
        [((x_own, x_other), qkv_grad), ((attn_own, attn_other), mixed), ((words_later,), inputs)],
        spots,
    )
    early = jnp.concatenate([position_part, small_pack], axis=0).astype(BF16)
    state_grad, second_blocks, early = fence(state_grad, second_blocks, early)
    early = exchange(early, dp_bits[0])
    first_one = level_part(1, halves_one[0], peers_one[0], 0)
    state_grad, bias_zero, halves_zero, peers_zero, before, beside, later = level_back(
        0, state_grad, (first_one, early), first_parts, (halves_one[0], peers_one[0])
    )
    first_one, early = before
    first_parts = beside
    first_one = send(blocked(first_one), dp_bits[1])
    second_one = level_part(1, *later, 1)
    state_grad, second_one = fence(state_grad, second_one)
    first_zero = level_part(0, halves_zero[0], peers_zero[0])
    pooled_grad, first_zero, first_one, second_blocks = fence(
        state_grad.astype(BF16), first_zero, first_one, second_blocks
    )
    first_parts = join_blocks(first_parts)[0]
    first_one = send(join_blocks(first_one)[0], dp_bits[2])
    second_parts = send(second_blocks, dp_bits[0])
    second_one = send(blocked(second_one), dp_bits[1])
    first_zero = send(blocked(first_zero), dp_bits[1])

    middle = local_channels // 2
    lower, upper = slice(0, middle), slice(middle, local_channels)
    cnn_out = cnn_backward(
        counts, embedded, filters[:, lower], conv_bias[lower], pooled_grad[:, lower], None, BLOCK
    )
    (conv_low, bias_low, embed_part), first_one, second_one, first_zero, peers_zero[1] = fence(
        cnn_out, first_one, second_one, first_zero, peers_zero[1]
    )
    second_zero = level_part(0, halves_zero[1], peers_zero[1])
    second_one, first_zero = join_blocks(second_one, first_zero)
    second_parts = join_blocks(second_parts)[0]
    embed_part, second_one, first_zero, second_zero, second_parts, early = fence(
        embed_part, second_one, first_zero, second_zero, second_parts, combine(early)
    )
    second_zero = send(blocked(second_zero), dp_bits[1])
    second_one = send(second_one, dp_bits[2])
    first_zero = send(first_zero, dp_bits[2])
    second_parts = send(second_parts, dp_bits[1])
    early = exchange(early, dp_bits[1])
    cnn_out = cnn_backward(
        counts, embedded, filters[:, upper], conv_bias[upper], pooled_grad[:, upper], embed_part, BLOCK
    )
    (conv_high, bias_high, embed_part), second_one, first_zero, second_zero, early, first_parts = fence(
        cnn_out, second_one, first_zero, second_zero, early, first_parts
    )
    second_zero = send(join_blocks(second_zero)[0], dp_bits[2])
    early = exchange(combine(early), dp_bits[2])
    first_sum = finish(send(first_parts, far_bits[2]), far_bits[3:])
    conv_sum = jnp.concatenate([conv_low, conv_high], axis=1)
    conv_pack = jnp.concatenate(
        [
            jnp.where(used_taps, conv_sum, jnp.zeros_like(conv_sum)),
            jnp.concatenate([bias_low, bias_high], axis=1),
            bias_zero,
            bias_one,
        ],
        axis=0,
    )
    conv_rows = conv_sum.shape[0]
    conv_pack = jnp.pad(conv_pack, ((0, -conv_pack.shape[0] % 16), (0, 0)))
    conv_parts = exchange(conv_pack, dp_bits[0])
    table_sum = table_gradient(ids.T, embed_part, char_table.shape[0])
    table_sum, conv_parts, second_parts = fence(table_sum, conv_parts, second_parts)
    second_parts = send(join_blocks(second_parts)[0], dp_bits[2])
    conv_parts = exchange(combine(conv_parts), dp_bits[1])
    table_total = table_sum
    table_total = table_total + swap(table_total, "mp", 1)
    table_total = table_total + swap(table_total, "mp", 2)
    table_total, conv_parts = fence(table_total, conv_parts)
    conv_parts = exchange(combine(conv_parts), dp_bits[2])
    for bit in dp_bits:
        table_total = table_total + swap(table_total, "dp", bit)
    table_total = table_total.reshape(-1, STEPS, CHAR_DIM)
    table_total = jnp.swapaxes(table_total, 0, 1).reshape(-1, CHAR_DIM)[: char_table.shape[0]]
    conv_pack = complete(conv_parts, dp_bits[3:])
    conv_sums = (
        conv_pack[:conv_rows],
        conv_pack[conv_rows],
        conv_pack[conv_rows + 1 : conv_rows + 5].reshape(LAYERS, 2, local_channels),
    )
    second_sum = finish(second_parts, dp_bits[3:])
    level_sums = [
        jnp.stack([finish(parts, dp_bits[3:]) for parts in level], axis=1)
        for level in ((first_zero, second_zero), (first_one, second_one))
    ]
    highway_weight_grad = jnp.stack(level_sums, axis=0)
    early = complete(early, dp_bits[3:])
    position_part, small_pack = early[:quarter], early[quarter:]
    rows = row_pack.shape[0]
    sums_zero, sums_one, sums_two = (small_pack[3 * i : 3 * i + 3] for i in range(3))
    up_bias_grad = small_pack[rows : rows + 1]
    qkv_sums = small_pack[rows + 1 : rows + 2, : 3 * local_heads]
    qv_bias_grad = jnp.stack(
        [qkv_sums[0, :local_heads], qkv_sums[0, 2 * local_heads :]], axis=0
    )
    position_part = fence(position_part.astype(BF16))[0]
    position_other = swap(position_part, "mp", 2)
    position_half = jnp.concatenate(
        [
            jnp.where(high > 0, position_other, position_part),
            jnp.where(high > 0, position_part, position_other),
        ],
        axis=0,
    )

    def both_halves(values):
        return jnp.concatenate([values, swap(values, "mp", 1)], axis=0)

    position_grad = both_halves(position_half).astype(F32)

    def in_order(values):
        first, second = values[:half_count], values[half_count:]
        return jnp.concatenate(
            [jnp.where(low > 0, second, first), jnp.where(low > 0, first, second)], axis=0
        )

    def split(total, widths):
        parts, first = [], 0
        for width in widths:
            parts.append(total[:, first : first + width])
            first += width
        return parts

    up_sum, down_sum = split(first_sum, (up_weight.shape[1], down_weight.shape[0]))
    qkv_sum, out_sum, project_sum = split(
        second_sum, (3 * local_heads, local_heads, local_channels)
    )
    return (
        in_order(jnp.concatenate([encoded, encoded_other], axis=0)),
        table_total,
        conv_sums[0],
        conv_sums[1],
        highway_weight_grad,
        conv_sums[2],
        project_sum.T,
        sums_zero[2],
        in_order(position_grad),
        jnp.stack([sums_zero[0], sums_one[0], sums_two[0]], axis=0),
        jnp.stack([sums_zero[1], sums_one[1], sums_two[1]], axis=0),
        qkv_sum.reshape(-1, 3, local_heads),
        qv_bias_grad,
        out_sum.T,
        sums_one[2],
        up_sum,
        up_bias_grad[0],
        down_sum.T,
        sums_two[2],
    )


def solution(mesh):
    return jax.shard_map(
        on_device,
        mesh=mesh,
        in_specs=(
            P("dp", None),
            P("dp", None),
            P(),
            P("dp", None),
            P(),
            P(None, "mp"),
            P("mp"),
            P(None, None, None, "mp"),
            P(None, None, "mp"),
            P("mp", None),
            P(),
            P(),
            P(),
            P(),
            P(None, None, "mp"),
            P(None, "mp"),
            P("mp", None),
            P(),
            P(None, "mp"),
            P("mp"),
            P("mp", None),
            P(),
            P("dp", None),
        ),
        out_specs=(
            P("dp", None),
            P(),
            P(None, "mp"),
            P("mp"),
            P(None, "dp", None, "mp"),
            P(None, None, "mp"),
            P("mp", "dp"),
            P(),
            P(),
            P(),
            P(),
            P("dp", None, "mp"),
            P(None, "mp"),
            P("mp", "dp"),
            P(),
            P("dp", "mp"),
            P("mp"),
            P("mp", "dp"),
            P(),
        ),
        check_vma=False,
    )
```
